32 devices in a mesh: dp: 2 (over x), seq: 4 (over z), tp: 4 (over y, core).
Axes of the slice: x: 2, y: 2, z: 4, core: 2. Of those that a mesh axis runs over, the one named last changes fastest.
Arguments:
- tokens: float32 [4, 1024, 768], P('dp', ('seq', 'tp')), may hold values from -6 to 6
- ln1_gain: bfloat16 [768], P('dp'), may hold values from 0.5 to 1.5
- ln1_bias: bfloat16 [768], P('dp'), may hold values from -1.5 to 1.5
- qkv_weight: bfloat16 [768, 2304], P('dp'), may hold values from -0.21875 to 0.21875
- rel_h: bfloat16 [63, 64], P(None, 'dp'), may hold values from -0.75 to 0.75
- rel_w: bfloat16 [63, 64], P(None, 'dp'), may hold values from -0.75 to 0.75
- proj_weight: bfloat16 [768, 768], P('dp'), may hold values from -3 to 3
- ln2_gain: bfloat16 [768], P('dp'), may hold values from 0.5 to 1.5
- ln2_bias: bfloat16 [768], P('dp'), may hold values from -1.5 to 1.5
- fc1_weight: bfloat16 [768, 3072], P('dp', 'tp'), may hold values from -0.21875 to 0.21875
- fc2_weight: bfloat16 [3072, 768], P('tp', 'dp'), may hold values from -0.109375 to 0.109375
- cotangent: bfloat16 [4, 1024, 768], P('dp', ('seq', 'tp')), may hold values from -6 to 6
Outputs:
- output: float32 [4, 1024, 768], P('dp', ('seq', 'tp'))
- tokens_grad: float32 [4, 1024, 768], P('dp', ('seq', 'tp'))
- ln1_gain_grad: float32 [768], P('dp')
- ln1_bias_grad: float32 [768], P('dp')
- qkv_grad: float32 [768, 2304], P('dp')
- rel_h_grad: float32 [63, 64], P(None, 'dp')
- rel_w_grad: float32 [63, 64], P(None, 'dp')
- proj_grad: float32 [768, 768], P('dp')
- ln2_gain_grad: float32 [768], P('dp')
- ln2_bias_grad: float32 [768], P('dp')
- fc1_grad: float32 [768, 3072], P('dp', 'tp')
- fc2_grad: float32 [3072, 768], P('tp', 'dp')
The draws below stay inside these ranges and needn't reach their ends.
All inputs are finite; a program needn't handle non-finite values.
Results may differ from the reference program's by a relative error of at most 0.02.
Values may be sent and summed in bfloat16 or wider, within the bound.
No kernel may reach another device: no remote copies, remote signals or barrier semaphores. Data moves between devices by JAX's collectives and lax.ppermute only.
A program may use at most 128 MiB of HBM per device.

```python
from functools import partial
import jax
import jax.numpy as jnp
from jax import lax

D = 768
FF = 3072
HD = 64
REL = 63
NTOK = 1024
IMAGES = 4


def shard_levels(rng, extent, split, low, top_value):
    def one(dim, shards_of):
        steps = jax.random.uniform(jax.random.fold_in(jax.random.fold_in(rng, 6), dim), (shards_of,), jnp.float32, low / len(split), top_value / len(split))
        return jnp.repeat(jnp.exp(steps), extent[dim] // shards_of).reshape((-1,) + (1,) * (len(extent) - dim - 1))

    loudness = one(*split[0])
    for cut in split[1:]:
        loudness = loudness * one(*cut)
    return loudness


def bell_draw(key, extent, scale, most, cuts=(), kind=jnp.bfloat16):
    result = scale * jax.random.normal(key, extent, jnp.float32)
    if cuts:
        result = result * shard_levels(key, extent, cuts, -0.22, 0.18)
    return jnp.clip(result, -most, most).astype(kind)


def setup_inputs(seed: int = 0) -> dict:
    streams_of = jax.random.split(jax.random.key(seed), 13)
    return {
        "tokens": bell_draw(streams_of[0], (IMAGES, NTOK, D), 1.0, 6.0, ((0, 2), (1, 16)), jnp.float32),
        "ln1_gain": jnp.clip(1.0 + 0.1 * jax.random.normal(streams_of[1], (D,), jnp.float32), 0.5, 1.5).astype(jnp.bfloat16),
        "ln1_bias": bell_draw(streams_of[2], (D,), 0.3, 1.5, ((0, 2),)),
        "qkv_weight": bell_draw(streams_of[3], (D, 3 * D), D ** -0.5, 0.21875, ((0, 2),)),
        "rel_h": bell_draw(streams_of[4], (REL, HD), 0.125, 0.75, ((1, 2),)),
        "rel_w": bell_draw(streams_of[5], (REL, HD), 0.125, 0.75, ((1, 2),)),
        "proj_weight": bell_draw(streams_of[6], (D, D), 4 ** -0.5, 3.0, ((0, 2),)),
        "ln2_gain": jnp.clip(1.0 + 0.1 * jax.random.normal(streams_of[7], (D,), jnp.float32), 0.5, 1.5).astype(jnp.bfloat16),
        "ln2_bias": bell_draw(streams_of[8], (D,), 0.3, 1.5, ((0, 2),)),
        "fc1_weight": bell_draw(streams_of[9], (D, FF), D ** -0.5, 0.21875, ((0, 2), (1, 4))),
        "fc2_weight": bell_draw(streams_of[10], (FF, D), FF ** -0.5, 0.109375, ((0, 4), (1, 2))),
        "cotangent": bell_draw(streams_of[11], (IMAGES, NTOK, D), 1.0, 6.0, ((0, 2), (1, 16))),
    }


EPS = 1e-06
HIGH = lax.Precision.HIGHEST

@jax.custom_vjp
def low(v):
    return lax.optimization_barrier(v.astype(jnp.bfloat16)).astype(jnp.float32)

@jax.custom_vjp
def low_back(v):
    return v

def low_keep(v):
    return (low(v), None)

def low_pass(kept, grad):
    return (grad,)

def back_keep(v):
    return (v, None)

def back_low(kept, grad):
    return (low(grad),)
low.defvjp(low_keep, low_pass)
low_back.defvjp(back_keep, back_low)

def dot_high(left_mat, right_mat):
    return jnp.dot(left_mat, right_mat, precision=HIGH, preferred_element_type=jnp.float32)

def layer_norm(values, gain_vec, shift_vec):
    center = values - lax.optimization_barrier(jnp.mean(values, axis=-1, keepdims=True))
    spread = lax.optimization_barrier(jnp.mean(center * center, axis=-1, keepdims=True))
    return center * lax.rsqrt(spread + EPS) * gain_vec + shift_vec

def rel_terms(queries, table_h, table_w, grid_row, grid_col):
    grid_side = (table_h.shape[0] + 1) // 2
    reach_idx = jnp.arange(grid_side, dtype=jnp.int32)
    along_h = dot_high(queries, table_h.T)
    along_w = dot_high(queries, table_w.T)
    pick_h = grid_row[:, None] - reach_idx[None, :] + (grid_side - 1)
    pick_w = grid_col[:, None] - reach_idx[None, :] + (grid_side - 1)
    return (jnp.take_along_axis(along_h, pick_h, axis=1), jnp.take_along_axis(along_w, pick_w, axis=1))

def attend_head(pieces, table_h, table_w):
    queries, key_head, value_head = pieces
    tok_total = queries.shape[0]
    grid_side = (table_h.shape[0] + 1) // 2
    places = jnp.arange(tok_total, dtype=jnp.int32)
    term_h, term_w = rel_terms(queries, table_h, table_w, places // grid_side, places % grid_side)
    bias_full = (term_h[:, :, None] + term_w[:, None, :]).reshape(tok_total, tok_total)
    scores = low_back(dot_high(queries, key_head.T) * queries.shape[1] ** (-0.5) + bias_full)
    probs_soft = jax.nn.softmax(scores, axis=-1)
    return dot_high(low(probs_soft), value_head)

def image_forward(tokens, params):
    gain_one, shift_one, mix_weight, table_h, table_w, out_weight, gain_two, shift_two, up_weight, down_weight = params
    tok_total, model_width = tokens.shape
    head_width = table_h.shape[1]
    head_total = model_width // head_width
    normed_one = low(layer_norm(tokens, gain_one, shift_one))
    mixed_rows = dot_high(normed_one, mix_weight)

    def split_heads(part_rows):
        return low_back(low(part_rows)).reshape(tok_total, head_total, head_width).transpose(1, 0, 2)
    queries = split_heads(mixed_rows[:, :model_width])
    keys_all = split_heads(mixed_rows[:, model_width:2 * model_width])
    values_all = split_heads(mixed_rows[:, 2 * model_width:])
    head_fn = jax.checkpoint(partial(attend_head, table_h=table_h, table_w=table_w))
    attended = lax.map(head_fn, (queries, keys_all, values_all))
    attended = attended.transpose(1, 0, 2).reshape(tok_total, model_width)
    attended = low_back(low(attended))
    branch = low_back(dot_high(attended, out_weight))
    middle = tokens + branch
    normed_two = low(layer_norm(middle, gain_two, shift_two))
    hidden = low_back(dot_high(normed_two, up_weight))
    active = low(jax.nn.gelu(hidden, approximate=False))
    return middle + dot_high(active, down_weight)

def forward_all(tokens, params):
    image_fn = jax.checkpoint(image_forward)

    def scan_step(carry_zero, one_image):
        return (carry_zero, image_fn(one_image, params))
    carry_zero, outputs = lax.scan(scan_step, jnp.float32(0), tokens)
    return outputs

def reference(tokens, ln1_gain, ln1_bias, qkv_weight, rel_h, rel_w, proj_weight, ln2_gain, ln2_bias, fc1_weight, fc2_weight, cotangent):
    params = (ln1_gain.astype(jnp.float32), ln1_bias.astype(jnp.float32), qkv_weight.astype(jnp.float32), rel_h.astype(jnp.float32), rel_w.astype(jnp.float32), proj_weight.astype(jnp.float32), ln2_gain.astype(jnp.float32), ln2_bias.astype(jnp.float32), fc1_weight.astype(jnp.float32), fc2_weight.astype(jnp.float32))
    output, pull_back = jax.vjp(forward_all, tokens.astype(jnp.float32), params)
    tokens_grad, grads = pull_back(cotangent.astype(jnp.float32))
    return (output, tokens_grad, grads[0], grads[1], grads[2], grads[3], grads[4], grads[5], grads[6], grads[7], grads[8], grads[9])
```

```python
import jax
import jax.numpy as jnp
from jax import lax
from jax.experimental import pallas as pl
from jax.experimental.pallas import tpu as pltpu
from jax.sharding import PartitionSpec as P

EPS = 1e-06
LOW = jnp.bfloat16
FULL = jnp.float32
LANES = 128
CORE, ROW, NEAR, FAR = 1, 2, 4, 8


def hop(value, bits):
    count = lax.axis_size("seq") * lax.axis_size("tp")
    return lax.ppermute(value, ("seq", "tp"), [(i, i ^ bits) for i in range(count)])


def gather_dp(value, axis):
    if lax.axis_size("dp") != 2:
        return lax.all_gather(value, "dp", axis=axis, tiled=True)
    other = lax.ppermute(value, "dp", [(0, 1), (1, 0)])
    first = lax.axis_index("dp") == 0
    return jnp.concatenate(
        [jnp.where(first, value, other), jnp.where(first, other, value)], axis=axis
    )


def piece(value, index, size, axis):
    return lax.dynamic_slice_in_dim(value, index * size, size, axis)


def scatter_dp(value, axis):
    if lax.axis_size("dp") != 2:
        return lax.psum_scatter(
            value.astype(LOW), "dp", scatter_dimension=axis, tiled=True
        ).astype(FULL)
    half = value.shape[axis] // 2
    me = lax.axis_index("dp")
    sent = piece(value, 1 - me, half, axis).astype(LOW)
    got = lax.ppermute(sent, "dp", [(0, 1), (1, 0)])
    return piece(value, me, half, axis).astype(FULL) + got.astype(FULL)


def sum_dp(value):
    if lax.axis_size("dp") != 2:
        return lax.psum(value, "dp")
    return value + lax.ppermute(value, "dp", [(0, 1), (1, 0)])


def canon(blocks, index, axis):
    odd = (index & 1) == 1
    upper = (index & 2) == 2
    b = [
        jnp.where(odd, blocks[k ^ 1], blocks[k])
        for k in range(4)
    ]
    return jnp.concatenate([jnp.where(upper, b[k ^ 2], b[k]) for k in range(4)], axis=axis)


def dot_nn(a, b):
    return lax.dot_general(a, b, (((1,), (0,)), ((), ())), preferred_element_type=FULL)


def dot_nt(a, b):
    return lax.dot_general(a, b, (((1,), (1,)), ((), ())), preferred_element_type=FULL)


def dot_tn(a, b):
    return lax.dot_general(a, b, (((0,), (0,)), ((), ())), preferred_element_type=FULL)


def call(kernel, outs, flops, scratch=(), smem=0, vmem=32):
    def run(*args):
        size = sum(a.size * a.dtype.itemsize for a in args)
        size += sum(a.size * a.dtype.itemsize for a in outs)
        return pl.pallas_call(
            kernel,
            out_shape=outs,
            in_specs=[pl.BlockSpec(memory_space=pltpu.SMEM)] * smem
            + [pl.BlockSpec(memory_space=pltpu.VMEM)] * (len(args) - smem),
            out_specs=[pl.BlockSpec(memory_space=pltpu.VMEM)] * len(outs),
            scratch_shapes=scratch,
            compiler_params=pltpu.CompilerParams(vmem_limit_bytes=vmem * 2**20),
            cost_estimate=pl.CostEstimate(flops=flops, bytes_accessed=size, transcendentals=0),
        )(*args)

    return run


def shape(dims, kind):
    return jax.ShapeDtypeStruct(dims, kind)


def normal(values):
    center = values - jnp.mean(values, axis=-1, keepdims=True)
    scale = lax.rsqrt(jnp.mean(center * center, axis=-1, keepdims=True) + EPS)
    return center * scale, scale


def norm_kernel(mine, other, gain, shift, out):
    half = mine.shape[0]
    for start, part in ((0, mine), (half, other)):
        hat, _ = normal(part[...])
        out[start : start + half, :] = (hat * gain[...] + shift[...]).astype(LOW)


def lane_of(rows):
    return lax.broadcasted_iota(jnp.int32, (rows, LANES), 1)


def pieces_at(lane, first, value, rest):
    high = value.astype(LOW).astype(FULL)
    left = value - high
    mid = left.astype(LOW).astype(FULL)
    tail = left - mid
    out = jnp.where(lane == first, high, rest)
    out = jnp.where(lane == first + 1, mid, out)
    return jnp.where(lane == first + 2, tail, out)


def key_tiles(h, kva, kvb, spot_one, spot_two, keys):
    half = kva.shape[0]
    lane = lane_of(half)
    for start, part in ((0, kva), (half, kvb)):
        tile = part[:, h * LANES : (h + 1) * LANES].astype(FULL)
        spots = spot_one[start : start + half, :].astype(FULL)
        keys[start : start + half, :LANES] = jnp.where(lane < 64, tile, spots).astype(LOW)
        keys[start : start + half, LANES:] = spot_two[start : start + half, :]


def attend_kernel(
    group_rows, query, kva, kvb, spot_one, spot_two, table, out, out_low, left, keys, along
):
    rows = query.shape[0]
    heads = left.shape[0]
    lane32 = lane_of(32)
    block = 128
    lane = lane_of(block)
    for h in range(heads):
        key_tiles(h, kva, kvb, spot_one, spot_two, keys)
        tile = query[:, (h // 2) * LANES : (h // 2 + 1) * LANES].astype(FULL)
        if h % 2:
            tile = pltpu.roll(tile, 64, 1)
        along[...] = dot_nn(tile.astype(LOW), table[...])
        for g in range(rows // 32):
            here = slice(g * 32, (g + 1) * 32)
            term_h = pltpu.roll(along[here, :LANES], 33 + group_rows[g], 1)
            term_w = pltpu.roll(along[here, LANES:], 65, 1, stride=1, stride_axis=0)
            one = jnp.where(
                lane32 < 64, tile[here, :] * 0.125, jnp.where(lane32 < 96, term_h, term_w)
            )
            high = one.astype(LOW)
            rest = pltpu.roll(one - high.astype(FULL), 64, 1)
            left[h, here, :LANES] = high
            left[h, here, LANES:] = rest.astype(LOW)
        for q in range(rows // block):
            here = slice(q * block, (q + 1) * block)
            scores = dot_nt(left[h, here, :], keys[...])
            top = jnp.max(scores, axis=1, keepdims=True)
            expo = jnp.exp(scores - top)
            total = jnp.sum(expo, axis=1, keepdims=True)
            low = expo.astype(LOW)
            half = kva.shape[0]
            cols = slice(h * LANES, (h + 1) * LANES)
            result = dot_nn(low[:, :half], kva[:, cols]) + dot_nn(low[:, half:], kvb[:, cols])
            result = result / total
            if h % 2 == 0:
                result = pltpu.roll(result, 64, 1)
            spot = slice((h // 2) * LANES, (h // 2 + 1) * LANES)
            if h % 2:
                result = jnp.where(lane < 64, out[here, spot], result)
            else:
                result = jnp.where(lane < 64, result, 0.0)
            out[here, spot] = result
            out_low[here, spot] = result.astype(LOW)
            rest = left[h, here, LANES:].astype(FULL)
            left[h, here, LANES:] = pieces_at(lane, 64, -(top + jnp.log(total)), rest).astype(LOW)


def back_kernel(
    group_rows,
    left,
    kva,
    kvb,
    spot_one,
    spot_two,
    table,
    grad,
    value,
    dquery,
    dkv_mine,
    dkv_other,
    dtable,
    keys,
    vals,
    gright,
    qright,
    along,
):
    heads, rows, _ = left.shape
    half = kva.shape[0]
    lane = lane_of(rows)
    lane32 = lane_of(32)
    row = lax.broadcasted_iota(jnp.int32, (rows, LANES), 0)
    chunk = 256
    dtable[...] = jnp.zeros_like(dtable)
    for h in range(heads):
        key_tiles(h, kva, kvb, spot_one, spot_two, keys)
        cols = slice(h * LANES, (h + 1) * LANES)
        spot = slice((h // 2) * LANES, (h // 2 + 1) * LANES)
        vals[:half, :LANES] = kva[:, cols]
        vals[half:, :LANES] = kvb[:, cols]
        vals[:, LANES:] = spot_two[...]
        gtile = grad[:, spot].astype(FULL)
        otile = value[:, spot]
        if h % 2 == 0:
            gtile = pltpu.roll(gtile, 64, 1)
            otile = pltpu.roll(otile, 64, 1)
        gtile = jnp.where(lane >= 64, gtile, 0.0)
        inner = jnp.sum(gtile * otile, axis=1, keepdims=True)
        gright[:, :LANES] = gtile.astype(LOW)
        gright[:, LANES:] = pieces_at(lane, 64, -inner, jnp.zeros_like(gtile)).astype(LOW)
        qright[...] = jnp.where(lane < 64, left[h, :, :LANES].astype(FULL), 0.0).astype(LOW)
        dq_t = jnp.zeros((LANES, rows), FULL)
        for k in range(2 * half // chunk):
            here = slice(k * chunk, (k + 1) * chunk)
            probs = jnp.exp(dot_nt(keys[here, :], left[h]))
            dscores = (probs * dot_nt(vals[here, :], gright[...])).astype(LOW)
            dkv = dot_nn(probs.astype(LOW), gright[:, :LANES]) + dot_nn(dscores, qright[...])
            if k * chunk < half:
                dkv_mine[here, cols] = dkv
            else:
                dkv_other[k * chunk - half : (k + 1) * chunk - half, cols] = dkv.astype(LOW)
            dq_t = dq_t + dot_tn(keys[here, :LANES], dscores)
        dq = dq_t.T
        for g in range(rows // 32):
            here = slice(g * 32, (g + 1) * 32)
            part_h = jnp.where((lane32 >= 64) & (lane32 < 96), dq[here, :], 0.0)
            along[here, :LANES] = pltpu.roll(part_h, 95 - group_rows[g], 1).astype(LOW)
        part_w = pltpu.roll(jnp.where(lane >= 96, dq, 0.0), 63, 1)
        for bit in range(5):
            moved = pltpu.roll(part_w, LANES - 2**bit, 1)
            part_w = jnp.where((row >> bit) & 1 == 1, moved, part_w)
        along[:, LANES:] = part_w.astype(LOW)
        dq = jnp.where(lane < 64, dq * 0.125 + dot_nt(along[...], table[...]), 0.0)
        if h % 2:
            dquery[:, spot] = dquery[:, spot] + pltpu.roll(dq, 64, 1).astype(LOW)
        else:
            dquery[:, spot] = dq.astype(LOW)
        dtable[...] += dot_tn(along[...], qright[...])


def mid_kernel(j0, j1, j2, j3, weight, rows, gain, shift, middle, low):
    width = j0.shape[1]
    total = rows[...]
    for k, part in enumerate((j0, j1, j2, j3)):
        total = total + dot_nn(part[...], weight[k * width : (k + 1) * width, :])
    middle[...] = total
    hat, _ = normal(total)
    low[...] = (hat * gain[...] + shift[...]).astype(LOW)


def feed_kernel(rows, grad, up, down, active, dhidden, dnorm):
    hidden = dot_nn(rows[...], up[...])
    phi = 0.5 + 0.5 * lax.erf(hidden * 0.7071067811865476)
    active[...] = (hidden * phi).astype(LOW)
    slope = phi + hidden * (jnp.exp(hidden * hidden * -0.5) * 0.3989422804014327)
    low = (dot_nt(grad[...], down[...]) * slope).astype(LOW)
    dhidden[...] = low
    dnorm[...] = dot_nt(low, up[...]).astype(LOW)


def feed(rows, grad, up, down):
    total, width = rows.shape
    hid = up.shape[1]
    block = 128
    row_spec = pl.BlockSpec((block, width), lambda i: (i, 0))
    hid_spec = pl.BlockSpec((block, hid), lambda i: (i, 0))
    up_spec = pl.BlockSpec((width, hid), lambda i: (0, 0))
    down_spec = pl.BlockSpec((hid, width), lambda i: (0, 0))
    return pl.pallas_call(
        feed_kernel,
        grid=(total // block,),
        in_specs=[row_spec, row_spec, up_spec, down_spec],
        out_specs=[hid_spec, hid_spec, row_spec],
        out_shape=[shape((total, hid), LOW), shape((total, hid), LOW), shape((total, width), LOW)],
        compiler_params=pltpu.CompilerParams(vmem_limit_bytes=32 * 2**20),
        cost_estimate=pl.CostEstimate(
            flops=6 * total * width * hid, bytes_accessed=12 * width * hid, transcendentals=0
        ),
    )(rows, grad, up, down)


def norm_back(grad, values, gain):
    hat, scale = normal(values)
    scaled = grad * gain
    back = scale * (
        scaled
        - jnp.mean(scaled, axis=-1, keepdims=True)
        - hat * jnp.mean(scaled * hat, axis=-1, keepdims=True)
    )
    return back, jnp.sum(grad * hat, axis=0, keepdims=True), jnp.sum(grad, axis=0, keepdims=True)


def mid_back_kernel(
    a0, a1, a2, middle, gain, cot, weight, gmiddle, gbranch, b0, b1, b2, b3, dgain, dshift
):
    grad = a0[...].astype(FULL) + a1[...].astype(FULL) + a2[...].astype(FULL)
    back, dgain[...], dshift[...] = norm_back(grad, middle[...], gain[...])
    total = cot[...].astype(FULL) + back
    gmiddle[...] = total
    low = total.astype(LOW)
    gbranch[...] = low
    width = b0.shape[1]
    for k, out in enumerate((b0, b1, b2, b3)):
        out[...] = dot_nt(low, weight[k * width : (k + 1) * width, :]).astype(LOW)


def first_back_kernel(a0, a1, a2, a3, rows, gain, gmiddle, out, dgain, dshift):
    grad = (a0[...].astype(FULL) + a1[...].astype(FULL)) + (
        a2[...].astype(FULL) + a3[...].astype(FULL)
    )
    back, dgain[...], dshift[...] = norm_back(grad, rows[...], gain[...])
    out[...] = gmiddle[...] + back


def on_device(
    tokens,
    ln1_gain,
    ln1_bias,
    qkv_weight,
    rel_h,
    rel_w,
    proj_weight,
    ln2_gain,
    ln2_bias,
    fc1_weight,
    fc2_weight,
    cotangent,
):
    images, tok, width = tokens.shape
    hid = fc1_weight.shape[1]
    dp_count = lax.axis_size("dp")
    head = rel_h.shape[1] * dp_count
    reach = rel_h.shape[0]
    side = (reach + 1) // 2
    s, t = lax.axis_index("seq"), lax.axis_index("tp")
    d = lax.axis_index("dp")
    y, c = t // 2, t % 2
    image = s // 2
    group = (s % 2) * 2 + y
    groups = 4
    share = width // groups
    heads = share // head
    rows_n = 2 * tok

    def of_image(array):
        mine = lax.dynamic_index_in_dim(array, image, 0, keepdims=False)
        other = lax.dynamic_index_in_dim(array, 1 - image, 0, keepdims=False)
        return mine, other

    own, away = of_image(tokens)
    own_got = hop(away, FAR)

    small = jnp.concatenate(
        [v.reshape(1, -1) for v in (ln1_gain, ln1_bias, ln2_gain, ln2_bias)], axis=0
    )
    small = gather_dp(small, 1).astype(FULL)
    gain_one, shift_one, gain_two, shift_two = (small[k : k + 1] for k in range(4))
    tables = gather_dp(jnp.stack([rel_h, rel_w]), 2)
    tables = jnp.pad(tables[:, ::-1, :], ((0, 0), (0, LANES - reach), (0, LANES - head)))
    table_t = tables.reshape(2 * LANES, LANES)
    table = table_t.T

    cols = [
        piece(qkv_weight, p * groups + group, share, 1) for p in range(3)
    ]
    order = []
    for h in range(heads):
        order += [cols[1][:, h * head : (h + 1) * head], cols[2][:, h * head : (h + 1) * head]]
    mix = gather_dp(jnp.concatenate(order + [cols[0]], axis=1), 0)
    mix = jnp.pad(mix, ((0, 0), (0, 2 * LANES - share)))
    proj = gather_dp(proj_weight, 0)
    proj = jnp.concatenate([piece(proj, group ^ k, share, 0) for k in range(4)], axis=0)
    up = gather_dp(fc1_weight, 0)
    down = gather_dp(fc2_weight, 1)

    places = []
    for k in range(4):
        for u in range(2):
            chunk = ((s ^ (k >> 1)) ^ (2 * u)) * 4 + ((y ^ (k & 1)) * 2) + c
            places += [chunk * 2, chunk * 2 + 1]
    group_rows = jnp.stack(places).astype(jnp.int32)
    key_rows = jnp.concatenate([group_rows, group_rows ^ 2])
    key_row = jnp.repeat(key_rows, side)[:, None]
    key_col = (jnp.arange(2 * groups * rows_n, dtype=jnp.int32) % side)[:, None]
    reach_idx = jnp.arange(side, dtype=jnp.int32)[None, :]
    spots = jnp.concatenate([key_row == reach_idx, key_col == reach_idx], axis=1).astype(LOW)
    blank = jnp.zeros_like(spots)
    spot_one = jnp.concatenate([blank, spots], axis=1)
    ones = jnp.concatenate([jnp.ones_like(spots[:, :3]), blank[:, 3:]], axis=1)
    spot_two = jnp.concatenate([spots, ones], axis=1)

    normed = call(norm_kernel, [shape((rows_n, width), LOW)], 0)(
        own, own_got, gain_one, shift_one
    )[0]
    normed_all = jnp.concatenate(
        [normed, hop(normed, ROW), hop(normed, NEAR), hop(normed, ROW | NEAR)], axis=0
    )
    kv_cols = 2 * share
    kv = dot_nn(normed_all, mix[:, :kv_cols]).astype(LOW)
    kv_other = hop(kv, CORE)
    query = dot_nn(normed_all, mix[:, kv_cols:]).astype(LOW)

    n = 4 * rows_n
    pad_share = 2 * LANES
    key_n = 2 * n
    attended, attended_low, left = call(
        attend_kernel,
        [
            shape((n, pad_share), FULL),
            shape((n, pad_share), LOW),
            shape((heads, n, 2 * LANES), LOW),
        ],
        heads * 4 * n * key_n * 256,
        [pltpu.VMEM((key_n, 2 * LANES), LOW), pltpu.VMEM((n, 2 * LANES), FULL)],
        smem=1,
    )(group_rows, query, kv, kv_other, spot_one, spot_two, table)

    def block(array, k):
        return array[k * rows_n : (k + 1) * rows_n]

    way = (0, ROW, NEAR, ROW | NEAR)
    attended_low = attended_low[:, :share]
    joined = [block(attended_low, 0)] + [hop(block(attended_low, k), way[k]) for k in (1, 2, 3)]
    rows = jnp.concatenate([own, own_got], axis=0)
    middle, normed_two = call(
        mid_kernel,
        [shape((rows_n, width), FULL), shape((rows_n, width), LOW)],
        2 * rows_n * width * width,
    )(*joined, proj, rows, gain_two, shift_two)

    def gather_tp(array):
        pair = jnp.concatenate([array, hop(array, ROW)], axis=0)
        return jnp.concatenate([pair, hop(pair, CORE)], axis=0)

    cot_mine, cot_away = of_image(cotangent)
    cot = jnp.concatenate([cot_mine, hop(cot_away, FAR)], axis=0)
    cot_all = gather_tp(cot)
    feed_rows = gather_tp(normed_two)
    active, dhidden, dnorm = feed(feed_rows, cot_all, up, down)

    def scatter_tp(array):
        got = hop(array[2 * rows_n :], CORE)
        sent = (block(array, 1).astype(FULL) + block(got, 1).astype(FULL)).astype(LOW)
        return block(array, 0), block(got, 0), hop(sent, ROW)

    dnorm_parts = scatter_tp(dnorm)
    (gmiddle, gbranch, b0, b1, b2, b3, dgain_two, dshift_two) = call(
        mid_back_kernel,
        [shape((rows_n, width), FULL), shape((rows_n, width), LOW)]
        + [shape((rows_n, share), LOW)] * 4
        + [shape((1, width), FULL)] * 2,
        2 * rows_n * width * width,
    )(*dnorm_parts, middle, gain_two, cot, proj)

    grad_heads = jnp.concatenate(
        [b0] + [hop(b, bits) for b, bits in ((b1, ROW), (b2, NEAR), (b3, ROW | NEAR))], axis=0
    )
    grad_heads = jnp.pad(grad_heads, ((0, 0), (0, pad_share - share)))
    dquery, dkv_mine, dkv_other, dtable = call(
        back_kernel,
        [
            shape((n, pad_share), LOW),
            shape((n, kv_cols), FULL),
            shape((n, kv_cols), LOW),
            shape((2 * LANES, LANES), FULL),
        ],
        heads * 10 * n * key_n * 256,
        [
            pltpu.VMEM((key_n, 2 * LANES), LOW),
            pltpu.VMEM((key_n, 2 * LANES), LOW),
            pltpu.VMEM((n, 2 * LANES), LOW),
            pltpu.VMEM((n, LANES), LOW),
            pltpu.VMEM((n, 2 * LANES), LOW),
        ],
        smem=1,
    )(group_rows, left, kv, kv_other, spot_one, spot_two, table, grad_heads, attended)

    dkv = (dkv_mine + hop(dkv_other, CORE).astype(FULL)).astype(LOW)
    dmixed = jnp.concatenate([dkv, dquery], axis=1)
    dnormed = dot_nt(dmixed, mix).astype(LOW)
    dnormed_parts = [block(dnormed, 0)] + [hop(block(dnormed, k), way[k]) for k in (1, 2, 3)]
    token_rows, dgain_one, dshift_one = call(
        first_back_kernel,
        [shape((rows_n, width), FULL)] + [shape((1, width), FULL)] * 2,
        0,
    )(*dnormed_parts, rows, gain_one, gmiddle)

    def to_owner(mine, other_low):
        got = hop(other_low, FAR).astype(FULL)
        return jnp.where(image == 0, jnp.stack([mine, got]), jnp.stack([got, mine]))

    tokens_grad = to_owner(token_rows[:tok], token_rows[tok:].astype(LOW))

    fed = dot_nn(active, down).astype(LOW)
    f0, f1, f2 = scatter_tp(fed)
    change = middle - rows + (f0.astype(FULL) + f1.astype(FULL) + f2.astype(FULL))
    got = hop(change[tok:].astype(LOW), FAR).astype(FULL)
    mine_out, got_out = own + change[:tok], away + got
    output = jnp.where(
        image == 0, jnp.stack([mine_out, got_out]), jnp.stack([got_out, mine_out])
    )

    def sum_seq(value, axis):
        size = value.shape[axis] // 4
        total = piece(value, s, size, axis).astype(FULL)
        for k in (1, 2, 3):
            sent = piece(value, s ^ k, size, axis).astype(LOW)
            total = total + hop(sent, k * NEAR).astype(FULL)
        low = total.astype(LOW)
        parts = [low] + [hop(low, k * NEAR) for k in (1, 2, 3)]
        return canon(parts, s, axis).astype(FULL)

    fc2_grad = sum_seq(scatter_dp(dot_tn(active, cot_all).astype(LOW), 1), 0)
    fc1_grad = sum_seq(scatter_dp(dot_tn(feed_rows, dhidden).astype(LOW), 0), 0)

    def halve(value, bits, bit, axis):
        size = value.shape[axis] // 2
        sent = piece(value, 1 - bit, size, axis).astype(LOW)
        return piece(value, bit, size, axis).astype(FULL) + hop(sent, bits).astype(FULL)

    def double(value, bits, bit, axis):
        got = hop(value, bits)
        return jnp.concatenate(
            [jnp.where(bit == 0, value, got), jnp.where(bit == 0, got, value)], axis=axis
        )

    def exchange(value, bits):
        low = value.astype(LOW)
        return low.astype(FULL) + hop(low, bits).astype(FULL)

    joined_all = canon(joined, group, 1)
    proj_grad = dot_tn(joined_all, gbranch)
    proj_grad = halve(halve(proj_grad, CORE, c, 1), ROW, y, 1)
    proj_grad = exchange(exchange(scatter_dp(proj_grad, 0), NEAR), FAR).astype(LOW)
    proj_grad = double(double(proj_grad, ROW, y, 1), CORE, c, 1).astype(FULL)

    qkv_cols = 3 * share
    qkv_part = dot_tn(normed_all, dmixed[:, :qkv_cols])
    qkv_part = exchange(scatter_dp(halve(qkv_part, CORE, c, 1), 0), FAR).astype(LOW)
    qkv_parts = [qkv_part] + [hop(qkv_part, bits) for bits in way[1:]]
    qkv_all = jnp.stack(qkv_parts)
    qkv_all = double(qkv_all, CORE, c, 2)
    qkv_all = canon([qkv_all[k : k + 1] for k in range(4)], group, 0)
    keys_values = qkv_all[:, :, :kv_cols].reshape(groups, -1, heads, 2, head)
    depth = qkv_all.shape[1]
    qkv_grad = jnp.concatenate(
        [
            qkv_all[:, :, kv_cols:].transpose(1, 0, 2).reshape(depth, width),
            keys_values[:, :, :, 0].transpose(1, 0, 2, 3).reshape(depth, width),
            keys_values[:, :, :, 1].transpose(1, 0, 2, 3).reshape(depth, width),
        ],
        axis=1,
    ).astype(FULL)

    dtable = (dtable[:, :head] * 8.0).reshape(-1)
    vector = jnp.concatenate(
        [v.reshape(-1) for v in (dgain_one, dshift_one, dgain_two, dshift_two)] + [dtable]
    ).reshape(-1, LANES)
    for bits in (CORE, ROW, NEAR, FAR):
        vector = vector + hop(vector, bits)
    vector = sum_dp(vector).reshape(-1)
    norms = vector[: 4 * width].reshape(4, width)
    norms = piece(norms, d, width // dp_count, 1)
    dtables = vector[4 * width :].reshape(2, LANES, head)[:, :reach][:, ::-1]
    dtables = piece(dtables, d, head // dp_count, 2)
    return (
        output,
        tokens_grad,
        norms[0],
        norms[1],
        qkv_grad,
        dtables[0],
        dtables[1],
        proj_grad,
        norms[2],
        norms[3],
        fc1_grad,
        fc2_grad,
    )


def solution(mesh):
    split = P("dp", ("seq", "tp"), None)
    params = (
        P("dp"),
        P("dp"),
        P("dp", None),
        P(None, "dp"),
        P(None, "dp"),
        P("dp", None),
        P("dp"),
        P("dp"),
        P("dp", "tp"),
        P("tp", "dp"),
    )
    return jax.shard_map(
        on_device,
        mesh=mesh,
        in_specs=(split, *params, split),
        out_specs=(split, split, *params),
        check_vma=False,
    )
```

```python
import math

import jax
import jax.numpy as jnp
from jax import lax
from jax.experimental import pallas as pl
from jax.experimental.pallas import tpu as pltpu
from jax.sharding import PartitionSpec as P

EPS = 1e-06
LOW = jnp.bfloat16
FULL = jnp.float32
LANES = 128
CORE, ROW, NEAR, FAR = 1, 2, 4, 8


def hop(value, bits):
    count = lax.axis_size("seq") * lax.axis_size("tp")
    return lax.ppermute(value, ("seq", "tp"), [(i, i ^ bits) for i in range(count)])


def swap_dp(value):
    return lax.ppermute(value, "dp", [(0, 1), (1, 0)])


def pair_dp(value, axis):
    if lax.axis_size("dp") == 2:
        return value, swap_dp(value), lax.axis_index("dp")
    whole = lax.all_gather(value, "dp", axis=axis, tiled=True)
    low, high = jnp.split(whole, 2, axis=axis)
    return low, high, jnp.int32(0)


def after(value, *events):
    return lax.optimization_barrier((value, *events))[0]


def piece(value, index, size, axis):
    return lax.dynamic_slice_in_dim(value, index * size, size, axis)


def scatter_dp(sent, kept, axis):
    if lax.axis_size("dp") == 2:
        return kept, swap_dp(sent)
    whole = jnp.concatenate([kept, sent], axis=axis)
    return lax.psum_scatter(whole, "dp", scatter_dimension=axis, tiled=True), None


def canon(blocks, index, axis):
    odd = (index & 1) == 1
    upper = (index & 2) == 2
    b = [
        jnp.where(odd, blocks[k ^ 1], blocks[k])
        for k in range(4)
    ]
    return jnp.concatenate([jnp.where(upper, b[k ^ 2], b[k]) for k in range(4)], axis=axis)


def dot_nn(a, b):
    return lax.dot_general(a, b, (((1,), (0,)), ((), ())), preferred_element_type=FULL)


def dot_nt(a, b):
    return lax.dot_general(a, b, (((1,), (1,)), ((), ())), preferred_element_type=FULL)


def dot_tn(a, b):
    return lax.dot_general(a, b, (((0,), (0,)), ((), ())), preferred_element_type=FULL)


def in_order():
    before = []

    def call(kernel, outs, scratch=(), smem=0, extra=2, wait=()):
        def run(*args):
            held = sum(a.size * jnp.dtype(a.dtype).itemsize for a in (*args, *outs))
            held += sum(math.prod(a.shape) * jnp.dtype(a.dtype).itemsize for a in scratch)
            used = len(args)
            events = (*before, *wait)

            def body(*refs):
                kernel(*refs[:used], *refs[used + len(events) :])

            results = pl.pallas_call(
                body,
                name=kernel.__qualname__.split(".")[0],
                out_shape=outs,
                in_specs=[pl.BlockSpec(memory_space=pltpu.SMEM)] * smem
                + [pl.BlockSpec(memory_space=pltpu.VMEM)] * (used - smem)
                + [pl.BlockSpec(memory_space=pl.ANY)] * len(events),
                out_specs=[pl.BlockSpec(memory_space=pltpu.VMEM)] * len(outs),
                scratch_shapes=scratch,
                compiler_params=pltpu.CompilerParams(vmem_limit_bytes=held + extra * 2**20),
                cost_estimate=pl.CostEstimate(flops=0, bytes_accessed=0, transcendentals=0),
            )(*args, *events)
            before[:] = [min(results, key=lambda r: r.size)]
            return results

        return run

    return call


def shape(dims, kind):
    return jax.ShapeDtypeStruct(dims, kind)


def normal(values):
    center = values - jnp.mean(values, axis=-1, keepdims=True)
    scale = lax.rsqrt(jnp.mean(center * center, axis=-1, keepdims=True) + EPS)
    return center * scale, scale


def pick_kernel(ids, array, mine, other):
    mine[...] = array[ids[3]]
    other[...] = array[1 - ids[3]]


def stack_kernel(*refs):
    out, start = refs[-1], 0
    for ref in refs[:-1]:
        out[start : start + ref.shape[0], :] = ref[...]
        start += ref.shape[0]


def pack_kernel(share, heads):
    def kernel(ids, weight, top, bottom):
        width = weight.shape[1] // 3
        head = share // heads
        rows = top.shape[0]
        for g in range(width // share):

            @pl.when(ids[1] == g)
            def _():
                for out, start in ((top, 0), (bottom, rows)):
                    here = slice(start, start + rows)

                    def move(at_col, first):
                        out[:, at_col : at_col + head] = weight[here, first : first + head]

                    for h in range(heads):
                        first = g * share + h * head
                        move(2 * h * head, width + first)
                        move((2 * h + 1) * head, 2 * width + first)
                        move(2 * share + h * head, first)

    return kernel


def rows_kernel(ids, array, out):
    out[...] = array[at(ids[2], out.shape[0]), :]


def fill_rows(ids, out, mine, other, other_two):
    half = mine.shape[0]
    out[at(ids[0], half), :] = mine[...]
    if other.shape[0] == half:
        out[at(1 - ids[0], half), :] = other[...]
        return
    size = half // 2
    out[at((1 - ids[0]) * 2 + ids[2], size), :] = other[...]
    out[at((1 - ids[0]) * 2 + 1 - ids[2], size), :] = other_two[...]


def norm_kernel(ids, mine, other, small, small_other, out, params):
    width = small.shape[1]
    params[:, lanes(ids[0], width)] = small[...].astype(FULL)
    params[:, lanes(1 - ids[0], width)] = small_other[...].astype(FULL)
    half = mine.shape[0]
    for start, part in ((0, mine), (half, other)):
        hat, _ = normal(part[...])
        out[start : start + half, :] = (hat * params[0:1, :] + params[1:2, :]).astype(LOW)


def grid_row(ids, n):
    k, u, i = n // 4, (n // 2) % 2, n % 2
    chunk = ((ids[6] ^ (k >> 1)) ^ (2 * u)) * 4 + ((ids[5] ^ (k & 1)) * 2) + ids[2]
    return chunk * 2 + i


def table_kernel(ids, mine, other, table, spot_one, spot_two):
    part, reach = mine.shape[1:]
    rows = lax.broadcasted_iota(jnp.int32, (reach, LANES), 0)
    cols = lax.broadcasted_iota(jnp.int32, (reach, LANES), 1)
    turn = jnp.where(rows == reach - 1 - cols, 1.0, 0.0).astype(LOW)
    table[...] = jnp.zeros_like(table)
    for k in range(2):
        spot = slice(k * LANES, (k + 1) * LANES)
        table[at(ids[0], part), spot] = dot_nn(mine[k], turn).astype(LOW)
        table[at(1 - ids[0], part), spot] = dot_nn(other[k], turn).astype(LOW)
    side = (reach + 1) // 2
    lane = lane_of(side)
    col = lax.broadcasted_iota(jnp.int32, (side, LANES), 0)
    total = spot_one.shape[0] // side
    for n in range(total):
        row = grid_row(ids, n % (total // 2))
        if n >= total // 2:
            row = row ^ 2
        here = slice(n * side, (n + 1) * side)
        target = jnp.where(lane < 96, row + 64, col + 96)
        one = jnp.where(lane == target, 1.0, 0.0)
        spot_one[here, :] = one.astype(LOW)
        ones = jnp.where((lane >= 64) & (lane < 67), 1.0, 0.0)
        spot_two[here, :] = (pltpu.roll(one, 64, 1) + ones).astype(LOW)


def lane_of(rows):
    return lax.broadcasted_iota(jnp.int32, (rows, LANES), 1)


def pieces_at(lane, first, value, rest):
    high = value.astype(LOW).astype(FULL)
    left = value - high
    mid = left.astype(LOW).astype(FULL)
    tail = left - mid
    out = jnp.where(lane == first, high, rest)
    out = jnp.where(lane == first + 1, mid, out)
    return jnp.where(lane == first + 2, tail, out)


def key_tiles(h, kva, kvb, spot_one, spot_two, keys):
    half = kva.shape[0]
    lane = lane_of(half)
    for start, part in ((0, kva), (half, kvb)):
        tile = part[:, h * LANES : (h + 1) * LANES].astype(FULL)
        spots = spot_one[start : start + half, :].astype(FULL)
        keys[start : start + half, :LANES] = jnp.where(lane < 64, tile, spots).astype(LOW)
        keys[start : start + half, LANES:] = spot_two[start : start + half, :]


def attend_kernel(
    ids, query, kva, kvb, spot_one, spot_two, table, out, a0, a1, a2, a3, left, keys, along
):
    rows = query.shape[0]
    heads = left.shape[0]
    lane32 = lane_of(32)
    block = 128
    lane = lane_of(block)
    for h in range(heads):
        key_tiles(h, kva, kvb, spot_one, spot_two, keys)
        tile = query[:, (h // 2) * LANES : (h // 2 + 1) * LANES].astype(FULL)
        if h % 2:
            tile = pltpu.roll(tile, 64, 1)
        along[...] = dot_nn(tile.astype(LOW), table[...])
        for g in range(rows // 32):
            here = slice(g * 32, (g + 1) * 32)
            term_h = pltpu.roll(along[here, :LANES], 33 + grid_row(ids, g), 1)
            term_w = pltpu.roll(along[here, LANES:], 65, 1, stride=1, stride_axis=0)
            one = jnp.where(
                lane32 < 64, tile[here, :] * 0.125, jnp.where(lane32 < 96, term_h, term_w)
            )
            high = one.astype(LOW)
            rest = pltpu.roll(one - high.astype(FULL), 64, 1)
            left[h, here, :LANES] = high
            left[h, here, LANES:] = rest.astype(LOW)
        for q in range(rows // block):
            here = slice(q * block, (q + 1) * block)
            scores = dot_nt(left[h, here, :], keys[...])
            top = jnp.max(scores, axis=1, keepdims=True)
            expo = jnp.exp(scores - top)
            total = jnp.sum(expo, axis=1, keepdims=True)
            low = expo.astype(LOW)
            half = kva.shape[0]
            cols = slice(h * LANES, (h + 1) * LANES)
            result = dot_nn(low[:, :half], kva[:, cols]) + dot_nn(low[:, half:], kvb[:, cols])
            result = result / total
            if h % 2 == 0:
                result = pltpu.roll(result, 64, 1)
            spot = slice((h // 2) * LANES, (h // 2 + 1) * LANES)
            if h % 2:
                result = jnp.where(lane < 64, out[here, spot], result)
            else:
                result = jnp.where(lane < 64, result, 0.0)
            out[here, spot] = result
            low_out = (a0, a1, a2, a3)[q]
            if h % 2:
                low_out[:, spot] = result.astype(LOW)
            elif h == heads - 1:
                low_out[:, h * 64 :] = result[:, :64].astype(LOW)
            rest = left[h, here, LANES:].astype(FULL)
            left[h, here, LANES:] = pieces_at(lane, 64, -(top + jnp.log(total)), rest).astype(LOW)


def back_kernel(h):
    def kernel(
        ids, left, kva, kvb, spot_one, spot_two, table, g0, g1, g2, g3, value,
        dquery, dkv_mine, dkv_other, dtable,
        keys, vals, gright, qright, along, grad,
    ):
        rows = left.shape[1]
        half = kva.shape[0]
        lane = lane_of(rows)
        lane32 = lane_of(32)
        row = lax.broadcasted_iota(jnp.int32, (rows, LANES), 0)
        chunk = 256
        key_tiles(h, kva, kvb, spot_one, spot_two, keys)
        cols = slice(h * LANES, (h + 1) * LANES)
        spot = slice((h // 2) * LANES, (h // 2 + 1) * LANES)
        for k, part in enumerate((g0, g1, g2, g3)):
            size, width = part.shape
            last = min(width, spot.stop)
            grad[k * size : (k + 1) * size, : last - spot.start] = part[:, spot.start : last].astype(FULL)
        vals[:half, :LANES] = kva[:, cols]
        vals[half:, :LANES] = kvb[:, cols]
        vals[:, LANES:] = spot_two[...]
        gtile = grad[...]
        otile = value[:, spot]
        if h % 2 == 0:
            gtile = pltpu.roll(gtile, 64, 1)
            otile = pltpu.roll(otile, 64, 1)
        gtile = jnp.where(lane >= 64, gtile, 0.0)
        inner = jnp.sum(gtile * otile, axis=1, keepdims=True)
        gright[:, :LANES] = gtile.astype(LOW)
        gright[:, LANES:] = pieces_at(lane, 64, -inner, jnp.zeros_like(gtile)).astype(LOW)
        qright[...] = jnp.where(lane < 64, left[h, :, :LANES].astype(FULL), 0.0).astype(LOW)
        dq_t = jnp.zeros((LANES, rows), FULL)
        for k in range(2 * half // chunk):
            here = slice(k * chunk, (k + 1) * chunk)
            probs = jnp.exp(dot_nt(keys[here, :], left[h]))
            dscores = (probs * dot_nt(vals[here, :], gright[...])).astype(LOW)
            dkv = dot_nn(probs.astype(LOW), gright[:, :LANES]) + dot_nn(dscores, qright[...])
            if k * chunk < half:
                dkv_mine[here, :] = dkv
            else:
                dkv_other[k * chunk - half : (k + 1) * chunk - half, :] = dkv.astype(LOW)
            dq_t = dq_t + dot_tn(keys[here, :LANES], dscores)
        dq = dq_t.T
        for g in range(rows // 32):
            here = slice(g * 32, (g + 1) * 32)
            part_h = jnp.where((lane32 >= 64) & (lane32 < 96), dq[here, :], 0.0)
            along[here, :LANES] = pltpu.roll(part_h, 95 - grid_row(ids, g), 1).astype(LOW)
        part_w = pltpu.roll(jnp.where(lane >= 96, dq, 0.0), 63, 1)
        for bit in range(5):
            moved = pltpu.roll(part_w, LANES - 2**bit, 1)
            part_w = jnp.where((row >> bit) & 1 == 1, moved, part_w)
        along[:, LANES:] = part_w.astype(LOW)
        dq = jnp.where(lane < 64, dq * 0.125 + dot_nt(along[...], table[...]), 0.0)
        if h % 2:
            dq = pltpu.roll(dq, 64, 1)
        dquery[...] = dq.astype(LOW)
        dtable[...] = dot_tn(along[...], qright[...])

    return kernel


def at(index, size):
    return pl.ds(pl.multiple_of(index * size, 16), size)


def lanes(index, size):
    return pl.ds(pl.multiple_of(index * size, LANES), size)


def mix_kernel(ids, n0, n1, n2, n3, w0, w1, o0, o1, kv, query, rows, mix):
    part, last = w0.shape
    kv_cols = kv.shape[1]
    for place, top, bottom in ((ids[0], w0, w1), (1 - ids[0], o0, o1)):
        mix[at(place * 2, part), :last] = top[...]
        mix[at(place * 2 + 1, part), :last] = bottom[...]
    mix[:, last:] = jnp.zeros((mix.shape[0], mix.shape[1] - last), LOW)
    size = n0.shape[0]
    for k, part in enumerate((n0, n1, n2, n3)):
        here = slice(k * size, (k + 1) * size)
        rows[here, :] = part[...]
        both = dot_nn(part[...], mix[...]).astype(LOW)
        kv[here, :] = both[:, :kv_cols]
        query[here, :] = both[:, kv_cols:]


def mid_kernel(
    ids, j0, j1, j2, j3, w_mine, w_other, w_two, own, own_got, params, middle, low, weight, whole
):
    fill_rows(ids, whole, w_mine, w_other, w_two)
    tok = own.shape[0]
    middle[:tok, :] = own[...]
    middle[tok:, :] = own_got[...]
    total = middle[...]
    width = j0.shape[1]
    for k, part in enumerate((j0, j1, j2, j3)):
        block = whole[at(ids[1] ^ k, width), :]
        weight[k * width : (k + 1) * width, :] = block
        total = total + dot_nn(part[...], block)
    middle[...] = total
    hat, _ = normal(total)
    low[...] = (hat * params[2:3, :] + params[3:4, :]).astype(LOW)


def feed_kernel(
    ids, r0, r1, r2, r3, c0, c1, c2, c3, up_mine, up_other, down_mine, down_other,
    d0, d1, d2, d3, active, dhidden, rows, cots, down, up,
):
    half = up_mine.shape[0]
    up[at(ids[0], half), :] = up_mine[...]
    up[at(1 - ids[0], half), :] = up_other[...]
    down[:, lanes(ids[0], half)] = down_mine[...]
    down[:, lanes(1 - ids[0], half)] = down_other[...]
    size = r0.shape[0]
    blocks = ((r0, c0, d0), (r1, c1, d1), (r2, c2, d2), (r3, c3, d3))
    for k, (row, cot, out) in enumerate(blocks):
        here = slice(k * size, (k + 1) * size)
        part, grad = row[...], cot[:size, :]
        rows[here, :] = part
        cots[here, :] = grad
        hidden = dot_nn(part, up[...])
        phi = 0.5 + 0.5 * lax.erf(hidden * 0.7071067811865476)
        active[here, :] = (hidden * phi).astype(LOW)
        slope = phi + hidden * (jnp.exp(hidden * hidden * -0.5) * 0.3989422804014327)
        back = (dot_nt(grad, down[...]) * slope).astype(LOW)
        dhidden[here, :] = back
        out[...] = dot_nt(back, up[...]).astype(LOW)


def fed_kernel(active, down, f0, f1, f2):
    size = f0.shape[0]
    for k, (out, start) in enumerate(((f0, 0), (f1, 0), (f2, 0), (f2, size))):
        part = dot_nn(active[k * size : (k + 1) * size, :], down[...])
        out[start : start + size, :] = part.astype(LOW)


def outer_kernel(which, axis):
    def kernel(ids, a, b, sent, kept):
        half = sent.shape[axis]
        for index, out in ((1 - ids[which], sent), (ids[which], kept)):
            if axis == 0:
                out[...] = dot_tn(a[:, lanes(index, half)], b[...]).astype(LOW)
            else:
                out[...] = dot_tn(a[...], b[:, lanes(index, half)]).astype(LOW)

    return kernel


def proj_grad_kernel(ids, j0, j1, j2, j3, grad, sent, kept, whole):
    width = j0.shape[1]
    for k, part in enumerate((j0, j1, j2, j3)):
        whole[at(ids[1] ^ k, width), :] = dot_tn(part[...], grad[...])
    size = sent.shape[0] // 2
    for k, owner in enumerate((ids[0], 1 - ids[0])):
        here = slice(k * size, (k + 1) * size)
        sent[here, :] = whole[at(owner * 2 + 1 - ids[2], size), :].astype(LOW)
        kept[here, :] = whole[at(owner * 2 + ids[2], size), :].astype(LOW)


def split_kernel(which):
    def kernel(ids, a, b, sent, kept):
        size = sent.shape[0] // 2
        for k in range(2):
            here = slice(k * size, (k + 1) * size)
            for bit, out in ((1 - ids[which], sent), (ids[which], kept)):
                rows = pl.ds(pl.multiple_of(k * 2 * size + bit * size, 16), size)
                out[here, :] = (a[rows, :].astype(FULL) + b[rows, :].astype(FULL)).astype(LOW)

    return kernel


def owner_kernel(a, b, sent, kept):
    size = sent.shape[0]
    kept[...] = (a[:size, :].astype(FULL) + b[:size, :].astype(FULL)).astype(kept.dtype)
    sent[...] = (a[size:, :].astype(FULL) + b[size:, :].astype(FULL)).astype(LOW)


def tail_add_kernel(a, b, out):
    size = a.shape[0]
    out[...] = (a[...].astype(FULL) + b[b.shape[0] - size :, :].astype(FULL)).astype(out.dtype)


def vector_block(out, n0, n1, n2, n3, t0, t1, t2):
    out[...] = jnp.zeros_like(out)
    tables = (t0[...] + t1[...] + t2[...]) * 8.0
    side = 16
    for k in range(8):
        start = k // 4 * LANES + k % 4 * side
        out[:side, k * 64 : (k + 1) * 64] = tables[start : start + side, :64]
    tile = 0
    for row in (n0, n1, n2, n3):
        for k in range(row.shape[1] // LANES):
            spot = slice(tile % 4 * LANES, (tile % 4 + 1) * LANES)
            out[side + tile // 4 : side + tile // 4 + 1, spot] = row[:, k * LANES : (k + 1) * LANES]
            tile += 1


def row_sums(product):
    total = product[:, :LANES]
    for k in range(1, product.shape[1] // LANES):
        total = total + product[:, k * LANES : (k + 1) * LANES]
    return jnp.sum(total.T, axis=0, keepdims=True)


def vector_out_kernel(reach, split):
    def kernel(ids, *refs):
        *parts, params, n0, n1, n2, n3, t0, t1, total, norms = refs
        first = parts[0].shape[0] - total.shape[0]
        total[...] = sum(part[first:, :].astype(FULL) for part in parts)
        side = 16
        for tile in range(norms.shape[0] * norms.shape[1] // LANES):
            each = norms.shape[1] // LANES
            spot = slice(tile % 4 * LANES, (tile % 4 + 1) * LANES)
            norms[tile // each : tile // each + 1, tile % each * LANES : (tile % each + 1) * LANES] = (
                total[side + tile // 4 : side + tile // 4 + 1, spot]
            )
        gain, shift = params[0:1, :], params[1:2, :]
        norms[0:1, :] = (norms[0:1, :] - shift * norms[1:2, :]) / gain
        for k, out in enumerate((n0, n1, n2, n3)):
            width = norms.shape[1] // 2
            if split:
                out[...] = norms[k : k + 1, lanes(ids[7], width)]
            else:
                out[...] = norms[k : k + 1, :]
        rows = lax.broadcasted_iota(jnp.int32, (side, reach), 0)
        cols = lax.broadcasted_iota(jnp.int32, (side, reach), 1)
        for k, out in enumerate((t0, t1)):
            both = jnp.zeros((64, reach), FULL)
            for part in range(4):
                turn = jnp.where(rows + part * side == reach - 1 - cols, 1.0, 0.0)
                start = (k * 4 + part) * 64
                both = both + lax.dot_general(
                    total[:side, start : start + 64],
                    turn,
                    (((0,), (0,)), ((), ())),
                    precision=lax.Precision.HIGHEST,
                    preferred_element_type=FULL,
                )
            if split:
                size = out.shape[0]
                out[...] = jnp.where(ids[7] == 0, both[:size, :], both[size:, :])
            else:
                out[...] = both

    return kernel


def dmix_kernel(dkv, dquery, mix, mine, near, sent):
    size = mine.shape[0]
    cols = dkv.shape[1]
    for k, (out, start) in enumerate(((mine, 0), (sent, 0), (near, 0), (sent, size))):
        here = slice(k * size, (k + 1) * size)
        part = dot_nt(dkv[here, :], mix[:, :cols]) + dot_nt(dquery[here, :], mix[:, cols:])
        out[start : start + size, :] = part.astype(LOW)


def dkv_kernel(m0, m1, m2, o0, o1, o2, q0, q1, q2, dkv, dquery):
    for h, (mine, got) in enumerate(((m0, o0), (m1, o1), (m2, o2))):
        cols = slice(h * LANES, (h + 1) * LANES)
        dkv[:, cols] = (mine[...] + got[...].astype(FULL)).astype(LOW)
    dquery[:, :LANES] = (q0[...].astype(FULL) + q1[...].astype(FULL)).astype(LOW)
    dquery[:, LANES:] = q2[...]


def qkv_grad_kernel(
    ids, rows, m0, m1, m2, o0, o1, o2, q0, q1, q2, mix, v2, v3, t0, t1, t2,
    dkv, dquery, sent, sent_two, kept, whole, vector,
):
    dkv_kernel(m0, m1, m2, o0, o1, o2, q0, q1, q2, dkv, dquery)
    cols = dkv.shape[1]
    whole[:, :cols] = dot_tn(rows[...], dkv[...])
    whole[:, cols:] = dot_tn(rows[...], dquery[...])
    width = kept.shape[1]
    size = (kept.shape[0] - vector.shape[0]) // 2
    extra = vector.shape[0] // 2
    sums_block(whole, dkv, dquery, mix, v2, v3, t0, t1, t2, vector)
    kept[2 * size :, :] = vector[...].astype(LOW)
    for k, (owner, out) in enumerate(((ids[0], sent), (1 - ids[0], sent_two))):
        here = slice(k * size, (k + 1) * size)
        kept[here, :] = whole[at(owner * 2 + ids[2], size), :width].astype(LOW)
        out[:size, :] = whole[at(owner * 2 + 1 - ids[2], size), :width].astype(LOW)
        out[size:, :] = vector[k * extra : (k + 1) * extra, :].astype(LOW)


def sums_block(whole, dkv, dquery, mix, v2, v3, t0, t1, t2, vector):
    weights = mix[...].astype(FULL)
    sums = jnp.concatenate(
        [jnp.sum(part[...].astype(FULL), axis=0, keepdims=True) for part in (dkv, dquery)], axis=1
    )
    both = row_sums(whole[...] * weights)
    shift = row_sums(weights * sums)
    vector_block(vector, both, shift, v2, v3, t0, t1, t2)


def sums_kernel(rows, dkv, dquery, mix, v2, v3, t0, t1, t2, vector, whole):
    cols = dkv.shape[1]
    whole[:, :cols] = dot_tn(rows[...], dkv[...])
    whole[:, cols:] = dot_tn(rows[...], dquery[...])
    sums_block(whole, dkv, dquery, mix, v2, v3, t0, t1, t2, vector)


def qkv_owner_kernel(a, b0, b1, s0, s1, kept):
    size = a.shape[0] - kept.shape[0]
    extra = kept.shape[0] - size
    kept[:size, :] = a[:size, :].astype(FULL) + b0[:size, :].astype(FULL)
    for k, (b, sent) in enumerate(((b0, s0), (b1, s1))):
        step, part = size // 2, extra // 2
        here = slice(size + k * step, size + (k + 1) * step)
        total = a[here, :].astype(FULL) + b1[k * step : (k + 1) * step, :].astype(FULL)
        sent[:step, :] = total.astype(LOW)
        start = 2 * size + k * part
        total = a[start : start + part, :].astype(FULL) + b[size:, :].astype(FULL)
        kept[size + k * part : size + (k + 1) * part, :] = total
        sent[step:, :] = total.astype(LOW)


def qkv_total_kernel(kept, g0, g1, out):
    part = g0.shape[0]
    step = part // 16 * 16 - 16
    size = 2 * step
    for k, got in enumerate((g0, g1)):
        here = slice(k * step, (k + 1) * step)
        out[here, :] = (kept[here, :] + got[:step, :].astype(FULL)).astype(LOW)
        here = slice(size + k * (part - step), size + (k + 1) * (part - step))
        out[here, :] = (kept[here, :] + got[step:, :].astype(FULL)).astype(LOW)


def fc_pack_kernel(ids, k1, g1, k2, g2, out):
    size, width = g1.shape[0], g2.shape[1]
    out[:size, :] = (k1[...] + g1[...].astype(FULL)).astype(LOW)
    for p in range(2):
        here = slice(p * size, (p + 1) * size)
        out[size:, p * width : (p + 1) * width] = (k2[here, :] + g2[here, :].astype(FULL)).astype(LOW)


def fc_join_kernel(ids, mine, got, out):
    size = mine.shape[0] // 2
    width = mine.shape[1] // 2
    for bit, ref in ((ids[3], mine), (1 - ids[3], got)):
        out[at(bit, size), :] = ref[:size, :]
        for p in range(2):
            start = (2 + p) * size
            out[start : start + size, lanes(bit, width)] = ref[size:, p * width : (p + 1) * width]


def fc_out_kernel(ids, mine, got, fc1, fc2):
    size = mine.shape[0] // 4
    width = mine.shape[1] // 2
    for bit, ref in ((ids[4], mine), (1 - ids[4], got)):
        fc1[at(bit, 2 * size), :] = ref[: 2 * size, :].astype(FULL)
        for b in range(2):
            for p in range(2):
                here = pl.ds(pl.multiple_of((bit * 4 + b * 2 + p) * size, 16), size)
                start = (2 + p) * size
                part = ref[start : start + size, b * width : (b + 1) * width]
                fc2[here, :] = part.astype(FULL)


def add_kernel(*refs):
    total = refs[0][...].astype(FULL)
    for ref in refs[1:-1]:
        total = total + ref[...].astype(FULL)
    refs[-1][...] = total.astype(refs[-1].dtype)


def halve_kernel(which):
    def kernel(ids, a, b, sent, kept):
        size = sent.shape[0]
        bit = ids[which]
        for index, out in ((1 - bit, sent), (bit, kept)):
            here = at(index, size)
            out[...] = (a[here, :].astype(FULL) + b[here, :].astype(FULL)).astype(out.dtype)

    return kernel


def join_kernel(which):
    def kernel(ids, mine, other, out):
        size = mine.shape[0]
        out[at(ids[which], size), :] = mine[...].astype(out.dtype)
        out[at(1 - ids[which], size), :] = other[...].astype(out.dtype)

    return kernel


def join_lanes_kernel(which):
    def kernel(ids, mine, other, out):
        size = mine.shape[1]
        out[:, lanes(ids[which], size)] = mine[...].astype(out.dtype)
        out[:, lanes(1 - ids[which], size)] = other[...].astype(out.dtype)

    return kernel


def qkv_out_kernel(heads):
    def kernel(ids, q0, q1, q2, q3, o0, o1, o2, o3, out):
        size = out.shape[0] // 2
        lane = lane_of(size)
        groups = 4
        odd, upper = (ids[1] & 1) == 1, (ids[1] & 2) == 2

        def tile(part, column, g):
            refs = (q0, q1, q2, q3) if part == 0 else (o0, o1, o2, o3)
            cols = slice(column, min(column + LANES, q0.shape[1]))
            v = [r[:size, cols].astype(FULL) for r in refs]
            v = [jnp.where(odd, v[k ^ 1], v[k]) for k in (g, g ^ 2)]
            one = jnp.where(upper, v[1], v[0])
            if one.shape[1] < LANES:
                one = jnp.concatenate([one, jnp.zeros_like(one)], axis=1)
            return one

        share = heads * 64
        for part in range(2):
            place = ids[2] if part == 0 else 1 - ids[2]
            here = pl.ds(pl.multiple_of(place * size, 16), size)
            total = groups * heads
            for pair in range(total // 2):
                ends = []
                for n in (2 * pair, 2 * pair + 1):
                    g, h = n // heads, n % heads
                    kv = tile(part, h * LANES, g)
                    q = tile(part, 2 * share + (h // 2) * LANES, g)
                    if h % 2:
                        q = pltpu.roll(q, 64, 1)
                    ends.append((q, kv))
                (qa, kva), (qb, kvb) = ends
                first = lane < 64
                at_col = pair * LANES
                width = groups * share
                out[here, at_col : at_col + LANES] = jnp.where(first, qa, pltpu.roll(qb, 64, 1))
                out[here, width + at_col : width + at_col + LANES] = jnp.where(
                    first, kva, pltpu.roll(kvb, 64, 1)
                )
                out[here, 2 * width + at_col : 2 * width + at_col + LANES] = jnp.where(
                    first, pltpu.roll(kva, 64, 1), kvb
                )

    return kernel


def change_kernel(middle, own, own_got, f0, f1, f2, mine, sent):
    tok = own.shape[0]
    for part, base, out in ((0, own, mine), (tok, own_got, sent)):
        here = slice(part, part + tok)
        fed = f0[here, :].astype(FULL) + f1[here, :].astype(FULL) + f2[here, :].astype(FULL)
        total = middle[here, :] + fed
        if part:
            total = total - base[...]
        out[...] = total.astype(out.dtype)


def place_kernel(ids, mine, got, base, out):
    out[ids[3]] = mine[...]
    out[1 - ids[3]] = got[...].astype(FULL) + base[...]


def place_two_kernel(ids, mine, got, out):
    out[ids[3]] = mine[...]
    out[1 - ids[3]] = got[...].astype(FULL)


def norm_back(grad, values, gain):
    hat, scale = normal(values)
    scaled = grad * gain
    back = scale * (
        scaled
        - jnp.mean(scaled, axis=-1, keepdims=True)
        - hat * jnp.mean(scaled * hat, axis=-1, keepdims=True)
    )
    return back, jnp.sum(grad * hat, axis=0, keepdims=True), jnp.sum(grad, axis=0, keepdims=True)


def mid_back_kernel(
    a0, a1, a2, middle, params, cot, weight, gmiddle, gbranch, b0, b1, b2, b3, dgain, dshift
):
    size = a0.shape[0]
    grad = a0[...].astype(FULL) + a1[...].astype(FULL) + a2[...].astype(FULL)
    back, dgain[...], dshift[...] = norm_back(grad, middle[...], params[2:3, :])
    total = cot[:size, :].astype(FULL) + back
    gmiddle[...] = total
    low = total.astype(LOW)
    gbranch[...] = low
    width = b0.shape[1]
    for k, out in enumerate((b0, b1, b2, b3)):
        out[...] = dot_nt(low, weight[k * width : (k + 1) * width, :]).astype(LOW)


def first_back_kernel(a0, a1, a2, own, own_got, params, gmiddle, mine, sent, rows):
    tok = own.shape[0]
    rows[:tok, :] = own[...]
    rows[tok:, :] = own_got[...]
    grad = a0[...].astype(FULL) + a1[: 2 * tok, :].astype(FULL) + a2[...].astype(FULL)
    back, _, _ = norm_back(grad, rows[...], params[0:1, :])
    total = gmiddle[...] + back
    mine[...] = total[:tok, :]
    sent[...] = total[tok:, :].astype(LOW)


def on_device(
    tokens,
    ln1_gain,
    ln1_bias,
    qkv_weight,
    rel_h,
    rel_w,
    proj_weight,
    ln2_gain,
    ln2_bias,
    fc1_weight,
    fc2_weight,
    cotangent,
):
    images, tok, width = tokens.shape
    hid = fc1_weight.shape[1]
    dp_count = lax.axis_size("dp")
    head = rel_h.shape[1] * dp_count
    reach = rel_h.shape[0]
    s, t = lax.axis_index("seq"), lax.axis_index("tp")
    d = lax.axis_index("dp")
    y, c = t // 2, t % 2
    image = s // 2
    group = (s % 2) * 2 + y
    groups = 4
    share = width // groups
    heads = share // head
    rows_n = 2 * tok
    half = width // 2
    me = d if dp_count == 2 else jnp.int32(0)
    ids = jnp.stack([me, group, c, image, s % 2, y, s, d]).astype(jnp.int32)
    n = 4 * rows_n
    kv_cols = 2 * share
    pad_share = 2 * LANES
    key_n = 2 * n
    qkv_cols = 3 * share
    low_tok, full_tok = shape((tok, width), LOW), shape((tok, width), FULL)
    low_rows, full_rows = shape((rows_n, width), LOW), shape((rows_n, width), FULL)
    two_rows = shape((2 * rows_n, width), LOW)
    heads_rows = shape((rows_n, share), LOW)
    way = (0, ROW, NEAR, ROW | NEAR)

    def add(kind, *args, wait=()):
        return call(add_kernel, [shape(args[0].shape, kind)], wait=wait)(*args)[0]

    call = in_order()
    quarter, eighth = half // 2, half // 4
    norm_sums = [shape((1, width), FULL)] * 2

    def total_of(kind, *args):
        return call(add_kernel, [shape(args[0].shape, kind)])(*args)[0]

    def halve(which, a, b, kind=FULL):
        dims = (a.shape[0] // 2, a.shape[1])
        return call(halve_kernel(which), [shape(dims, LOW), shape(dims, kind)], smem=1)(ids, a, b)

    def split(which, a, b):
        dims = (a.shape[0] // 2, a.shape[1])
        return call(split_kernel(which), [shape(dims, LOW)] * 2, smem=1)(ids, a, b)

    def join(which, mine, other, kind):
        dims = (2 * mine.shape[0], mine.shape[1])
        return call(join_kernel(which), [shape(dims, kind)], smem=1)(ids, mine, other)[0]

    own, away = call(pick_kernel, [full_tok] * 2, smem=1)(ids, tokens)
    with jax.named_scope("tokens_swap"):
        own_got = hop(away, FAR)
    small = jnp.concatenate([ln1_gain, ln1_bias, ln2_gain, ln2_bias]).reshape(4, -1)
    with jax.named_scope("small_params"):
        small, small_other, _ = pair_dp(after(small, away), 1)
    tables = jnp.stack([rel_h.T, rel_w.T])
    with jax.named_scope("tables_hop"):
        tables, tables_other, _ = pair_dp(after(tables, away), 1)
    cot_mine, cot_away = call(pick_kernel, [low_tok] * 2, smem=1)(ids, cotangent)
    with jax.named_scope("cot_swap"):
        cot_got = hop(cot_away, FAR)
    depth = qkv_weight.shape[0] // 2
    mix_mine = call(pack_kernel(share, heads), [shape((depth, qkv_cols), LOW)] * 2, smem=1)(
        ids, qkv_weight
    )
    with jax.named_scope("qkv_weight_hop"):
        if dp_count == 2:
            mix_other = [swap_dp(after(v, small_other, tables_other)) for v in mix_mine]
        else:
            whole = lax.all_gather(
                jnp.concatenate(mix_mine, axis=0), "dp", axis=0, tiled=True
            )
            *mix_mine, low, high = jnp.split(whole, 4, axis=0)
            mix_other = [low, high]

    normed, params = call(norm_kernel, [low_rows, shape((4, width), FULL)], smem=1)(
        ids, own, own_got, small, small_other
    )
    with jax.named_scope("normed_gather"):
        normed_parts = [normed] + [hop(normed, b) for b in way[1:]]
    cot = call(stack_kernel, [low_rows])(cot_mine, cot_got)[0]
    table, spot_one, spot_two = call(
        table_kernel,
        [shape((LANES, 2 * LANES), LOW)] + [shape((key_n, LANES), LOW)] * 2,
        smem=1,
    )(ids, tables, tables_other)
    if dp_count == 2:
        proj_part = call(rows_kernel, [shape((half // 2, width), LOW)], smem=1)(ids, proj_weight)[0]

    kv, query, normed_all, mix = call(
        mix_kernel,
        [
            shape((n, kv_cols), LOW),
            shape((n, pad_share), LOW),
            shape((n, width), LOW),
            shape((width, kv_cols + pad_share), LOW),
        ],
        smem=1,
        extra=3,
    )(ids, *normed_parts, *mix_mine, *mix_other)
    with jax.named_scope("kv_hop"):
        kv_other = hop(kv, CORE)
    with jax.named_scope("cot_row"):
        cot_row = hop(after(cot, kv), ROW)
    with jax.named_scope("proj_weight_hop"):
        if dp_count == 2:
            proj_mine, proj_other = proj_weight, swap_dp(after(proj_part, kv))
        else:
            proj_mine, proj_other, _ = pair_dp(proj_weight, 0)
    with jax.named_scope("fc1_weight_hop"):
        up_mine, up_other, _ = pair_dp(after(fc1_weight, kv), 0)

    attended, *attended_low, left = call(
        attend_kernel,
        [shape((n, pad_share), FULL)]
        + [heads_rows] * 4
        + [shape((heads, n, 2 * LANES), LOW)],
        [pltpu.VMEM((key_n, 2 * LANES), LOW), pltpu.VMEM((n, 2 * LANES), FULL)],
        smem=1,
        extra=8,
    )(ids, query, kv, kv_other, spot_one, spot_two, table)
    attended_low = lax.optimization_barrier((*attended_low, cot_row))[:4]
    with jax.named_scope("proj_weight_core"):
        proj_two = hop(after(proj_other, attended), CORE)
    with jax.named_scope("attended_hop"):
        joined = [attended_low[0]] + [hop(attended_low[k], way[k]) for k in (1, 2, 3)]
    with jax.named_scope("fc2_weight_hop"):
        down_mine, down_other, _ = pair_dp(after(fc2_weight, *joined), 1)
    middle, normed_two, proj = call(
        mid_kernel,
        [full_rows, low_rows, shape((width, width), LOW)],
        [pltpu.VMEM((width, width), LOW)],
        smem=1,
        wait=(up_other,),
    )(ids, *joined, proj_mine, proj_other, proj_two, own, own_got, params)

    with jax.named_scope("normed_two_row"):
        two_row = hop(normed_two, ROW)
    with jax.named_scope("normed_two_core"):
        two_core = hop(normed_two, CORE)
        two_diag = hop(two_row, CORE)
    with jax.named_scope("cot_core"):
        cot_core = hop(after(cot, two_row), CORE)
        cot_diag = hop(after(cot_row, two_row), CORE)
    d0, d1, d2, d3, active, dhidden, rows_all, cot_all, down = call(
        feed_kernel,
        [low_rows] * 4
        + [shape((n, hid), LOW)] * 2
        + [shape((n, width), LOW)] * 2
        + [shape((hid, width), LOW)],
        [pltpu.VMEM((width, hid), LOW)],
        smem=1,
        extra=6,
    )(
        ids, normed_two, two_row, two_core, two_diag, cot, cot_row, cot_core, cot_diag,
        up_mine, up_other, down_mine, down_other,
    )
    with jax.named_scope("dnorm_core"):
        dnorm_next = hop(d3, CORE)
        dnorm_mine = hop(d2, CORE)
    dnorm_sent = total_of(LOW, d1, dnorm_next)
    with jax.named_scope("dnorm_row"):
        dnorm_row = hop(dnorm_sent, ROW)

    fc1_sent, fc1_kept = call(outer_kernel(0, 0), [shape((half, hid), LOW)] * 2, smem=1, extra=4)(
        ids, rows_all, dhidden
    )
    with jax.named_scope("fc1_dp"):
        fc1_kept, fc1_got = scatter_dp(fc1_sent, fc1_kept, 0)
    fc2_sent, fc2_kept = call(outer_kernel(0, 1), [shape((hid, half), LOW)] * 2, smem=1, extra=4)(
        ids, active, cot_all
    )
    with jax.named_scope("fc2_dp"):
        fc2_kept, fc2_got = scatter_dp(fc2_sent, fc2_kept, 1)
    (gmiddle, gbranch, b0, b1, b2, b3, dgain_two, dshift_two) = call(
        mid_back_kernel, [full_rows, low_rows] + [heads_rows] * 4 + norm_sums
    )(d0, dnorm_mine, dnorm_row, middle, params, cot, proj)
    with jax.named_scope("grad_heads_hop"):
        grad_parts = [b0] + [hop(b, bits) for b, bits in zip((b1, b2, b3), way[1:])]
    proj_sent, proj_kept = call(
        proj_grad_kernel,
        [shape((half, width), LOW)] * 2,
        [pltpu.VMEM((width, width), FULL)],
        smem=1,
    )(ids, *joined, gbranch)
    f0, f1, f2 = call(fed_kernel, [low_rows, low_rows, two_rows])(active, down)
    with jax.named_scope("proj_core"):
        proj_got = hop(after(proj_sent, *grad_parts), CORE)
    with jax.named_scope("fed_core"):
        fed_got = hop(after(f2, *grad_parts), CORE)

    def back(h, wait=()):
        dquery, mine, other, dtable = call(
            back_kernel(h),
            [
                shape((n, LANES), LOW),
                shape((n, LANES), FULL),
                shape((n, LANES), LOW),
                shape((2 * LANES, LANES), FULL),
            ],
            [
                pltpu.VMEM((key_n, 2 * LANES), LOW),
                pltpu.VMEM((key_n, 2 * LANES), LOW),
                pltpu.VMEM((n, 2 * LANES), LOW),
                pltpu.VMEM((n, LANES), LOW),
                pltpu.VMEM((n, 2 * LANES), LOW),
                pltpu.VMEM((n, LANES), FULL),
            ],
            smem=1,
            extra=8,
            wait=wait,
        )(ids, left, kv, kv_other, spot_one, spot_two, table, *grad_parts, attended)
        with jax.named_scope("dkv_hop"):
            return mine, hop(other, CORE), dquery, dtable

    first = back(0)
    fed_sent = call(tail_add_kernel, [low_rows])(f1, fed_got)[0]
    with jax.named_scope("fed_row"):
        fed_row = hop(fed_sent, ROW)
    if dp_count == 2:
        fc1_sent, fc1_kept = halve(4, fc1_kept, fc1_got)
        with jax.named_scope("fc1_near_sum"):
            fc1_got = hop(fc1_sent, NEAR)
    second = back(1, (first[1],))
    if dp_count == 2:
        proj_sent, proj_kept = split(5, proj_kept, proj_got)
        with jax.named_scope("proj_row"):
            proj_got = hop(proj_sent, ROW)
    third = back(2, (second[1],))

    def change():
        return call(change_kernel, [full_tok, low_tok])(
            middle, own, own_got, f0, fed_got, fed_row
        )

    def place_output():
        return call(place_kernel, [shape(tokens.shape, FULL)], smem=1)(
            ids, change_mine, change_got, away
        )[0]

    dkv_mine, dkv_got, dqueries, dtables = zip(first, second, third)
    mixed_shapes = [shape((n, kv_cols), LOW), shape((n, pad_share), LOW)]
    vector_rows = 32
    whole_shape = pltpu.VMEM((width, kv_cols + pad_share), FULL)
    if dp_count == 2:
        fc2_sent, fc2_kept = halve(4, fc2_kept, fc2_got)
        with jax.named_scope("fc2_near_sum"):
            fc2_got = hop(fc2_sent, NEAR)
        fc1_sent, fc1_kept = halve(3, fc1_kept, fc1_got)
        with jax.named_scope("fc1_far_sum"):
            fc1_got = hop(fc1_sent, FAR)
        sent_rows = quarter + vector_rows // 2
        dkv, dquery, *qkv_sent, qkv_kept = call(
            qkv_grad_kernel,
            mixed_shapes
            + [shape((sent_rows, qkv_cols), LOW)] * 2
            + [shape((half + vector_rows, qkv_cols), LOW)],
            [whole_shape, pltpu.VMEM((vector_rows, qkv_cols), FULL)],
            smem=1,
            extra=6,
        )(
            ids, normed_all, *dkv_mine, *dkv_got, *dqueries, mix, dgain_two, dshift_two, *dtables
        )
        with jax.named_scope("qkv_core"):
            qkv_got = [hop(v, CORE) for v in qkv_sent]
    else:
        dkv, dquery = call(dkv_kernel, mixed_shapes)(*dkv_mine, *dkv_got, *dqueries)
    e_mine, e_near, e_row = call(dmix_kernel, [low_rows, low_rows, two_rows])(dkv, dquery, mix)
    with jax.named_scope("dnormed_row"):
        e_got = hop(e_row, ROW)

    def dnormed_near():
        sent = call(tail_add_kernel, [low_rows])(e_near, e_got)[0]
        with jax.named_scope("dnormed_near"):
            return hop(sent, NEAR)

    def first_back():
        return call(
            first_back_kernel, [full_tok, low_tok], [pltpu.VMEM((rows_n, width), FULL)]
        )(e_mine, e_got, dnormed_got, own, own_got, params, gmiddle)

    def place_tokens():
        return call(place_two_kernel, [shape(tokens.shape, FULL)], smem=1)(
            ids, token_mine, token_got
        )[0]

    def vector_out(parts, size, features):
        return call(
            vector_out_kernel(reach, dp_count == 2),
            [shape((1, size), FULL)] * 4 + [shape((features, reach), FULL)] * 2,
            [pltpu.VMEM((vector_rows, qkv_cols), FULL), pltpu.VMEM((4, width), FULL)],
            smem=1,
        )(ids, *parts, params)

    if dp_count == 2:
        qkv_rows = (quarter + vector_rows, qkv_cols)
        part_rows = ((quarter + vector_rows) // 2, qkv_cols)
        *qkv_sent, qkv_kept = call(
            qkv_owner_kernel, [shape(part_rows, LOW)] * 2 + [shape(qkv_rows, FULL)]
        )(qkv_kept, *qkv_got)
        with jax.named_scope("qkv_dp"):
            qkv_got = [swap_dp(v) for v in qkv_sent]
        qkv_part = call(qkv_total_kernel, [shape(qkv_rows, LOW)])(qkv_kept, *qkv_got)[0]
        with jax.named_scope("qkv_far"):
            qkv_got = hop(qkv_part, FAR)
        fc2_sent, fc2_kept = call(
            halve_kernel(3), [shape((quarter, half), LOW), shape((quarter, half), FULL)], smem=1,
            wait=(fc1_got,),
        )(ids, fc2_kept, fc2_got)
        with jax.named_scope("fc2_far_sum"):
            fc2_got = hop(fc2_sent, FAR)
        dnormed_got = dnormed_near()
        proj_low = shape((eighth, width), LOW)
        proj_sent, proj_kept = call(owner_kernel, [proj_low] * 2)(proj_kept, proj_got)
        with jax.named_scope("proj_dp"):
            proj_got = swap_dp(proj_sent)
        qkv_part = total_of(LOW, qkv_part, qkv_got)
        with jax.named_scope("qkv_all"):
            qkv_parts = [qkv_part] + [hop(qkv_part, bits) for bits in way[1:]]
        fc_part = call(fc_pack_kernel, [shape((quarter, width), LOW)], smem=1)(
            ids, fc1_kept, fc1_got, fc2_kept, fc2_got
        )[0]
        with jax.named_scope("fc_far_all"):
            fc_got = hop(fc_part, FAR)
        token_mine, token_sent = first_back()
        with jax.named_scope("tokens_grad_swap"):
            token_got = hop(token_sent, FAR)
        proj_part = total_of(LOW, proj_kept, proj_got)
        with jax.named_scope("proj_near"):
            proj_got = hop(proj_part, NEAR)
        *norms, table_h, table_w = vector_out(qkv_parts, half, head // 2)
        norms = [v.reshape(half) for v in norms]
        dtables = (table_h.T, table_w.T)
        with jax.named_scope("qkv_core_all"):
            qkv_others = [hop(part, CORE) for part in qkv_parts]
        tokens_grad = place_tokens()
        proj_part = total_of(LOW, proj_part, proj_got)
        with jax.named_scope("proj_far"):
            proj_got = hop(proj_part, FAR)
        fc_part = call(fc_join_kernel, [shape((half, width), LOW)], smem=1)(ids, fc_part, fc_got)[0]
        with jax.named_scope("fc_near_all"):
            fc_got = hop(fc_part, NEAR)
        change_mine, change_sent = change()
        with jax.named_scope("output_swap"):
            change_got = hop(change_sent, FAR)
        proj_part = total_of(LOW, proj_part, proj_got)
        with jax.named_scope("proj_all_row"):
            proj_got = hop(proj_part, ROW)
        qkv_grad = call(
            qkv_out_kernel(heads), [shape((half, 3 * width), FULL)], smem=1, extra=4
        )(ids, *qkv_parts, *qkv_others)[0]
        proj_part = join(5, proj_part, proj_got, LOW)
        with jax.named_scope("proj_all_core"):
            proj_got = hop(proj_part, CORE)
        output = place_output()
        proj_grad = join(2, proj_part, proj_got, FULL)
        fc1_grad, fc2_grad = call(
            fc_out_kernel, [shape((half, hid), FULL), shape((hid, half), FULL)], smem=1
        )(ids, fc_part, fc_got)
    else:
        every = ("seq", "tp")
        dnormed_got = dnormed_near()
        token_mine, token_sent = first_back()
        token_got = hop(token_sent, FAR)
        change_mine, change_sent = change()
        change_got = hop(change_sent, FAR)
        output, tokens_grad = place_output(), place_tokens()

        def weight_sum(a, b, axes, axis=0):
            part = lax.psum_scatter(
                dot_tn(a, b).astype(LOW), "dp", scatter_dimension=axis, tiled=True
            )
            return lax.psum(part, axes).astype(FULL)

        fc1_grad = weight_sum(rows_all, dhidden, "seq")
        fc2_grad = weight_sum(active, cot_all, "seq", 1)
        proj_grad = weight_sum(canon(joined, group, 1), gbranch, every)
        dmixed = jnp.concatenate([dkv, dquery], axis=1)[:, :qkv_cols]
        part = dot_tn(normed_all, dmixed).astype(LOW)
        part = lax.psum_scatter(part, "dp", scatter_dimension=0, tiled=True)
        part = part.astype(FULL) + hop(part, FAR).astype(FULL)
        part = part.astype(LOW)
        part = (part.astype(FULL) + hop(part, CORE).astype(FULL)).astype(LOW)
        whole = canon([part[None]] + [hop(part, bits)[None] for bits in way[1:]], group, 0)
        depth = whole.shape[1]
        pairs = whole[:, :, :kv_cols].reshape(groups, depth, heads, 2, head)
        qkv_grad = jnp.concatenate(
            [
                whole[:, :, kv_cols:].transpose(1, 0, 2).reshape(depth, width),
                pairs[:, :, :, 0].transpose(1, 0, 2, 3).reshape(depth, width),
                pairs[:, :, :, 1].transpose(1, 0, 2, 3).reshape(depth, width),
            ],
            axis=1,
        ).astype(FULL)
        vector = call(sums_kernel, [shape((vector_rows, qkv_cols), FULL)], [whole_shape], extra=6)(
            normed_all, dkv, dquery, mix, dgain_two, dshift_two, *dtables
        )[0]
        vector = lax.psum(vector, ("dp", *every))
        *norms, table_h, table_w = vector_out((vector,), width, head)
        norms = [piece(v.reshape(-1), d, width // dp_count, 0) for v in norms]
        dtables = [piece(v.T, d, head // dp_count, 1) for v in (table_h, table_w)]
    return (
        output,
        tokens_grad,
        norms[0],
        norms[1],
        qkv_grad,
        dtables[0],
        dtables[1],
        proj_grad,
        norms[2],
        norms[3],
        fc1_grad,
        fc2_grad,
    )


def solution(mesh):
    split = P("dp", ("seq", "tp"), None)
    params = (
        P("dp"),
        P("dp"),
        P("dp", None),
        P(None, "dp"),
        P(None, "dp"),
        P("dp", None),
        P("dp"),
        P("dp"),
        P("dp", "tp"),
        P("tp", "dp"),
    )
    return jax.shard_map(
        on_device,
        mesh=mesh,
        in_specs=(split, *params, split),
        out_specs=(split, split, *params),
        check_vma=False,
    )
```

```python
import math
import types

import jax
import jax.numpy as jnp
from jax import lax
from jax.experimental import pallas as pl
from jax.experimental.pallas import tpu as pltpu
from jax.sharding import PartitionSpec as P

EPS = 1e-06
LOW = jnp.bfloat16
FULL = jnp.float32
LANES = 128
CORE, ROW, NEAR, FAR = 1, 2, 4, 8


def hop(value, bits):
    count = lax.axis_size("seq") * lax.axis_size("tp")
    return lax.ppermute(value, ("seq", "tp"), [(i, i ^ bits) for i in range(count)])


def swap_dp(value):
    return lax.ppermute(value, "dp", [(0, 1), (1, 0)])


def pair_dp(value, axis):
    if lax.axis_size("dp") == 2:
        return value, swap_dp(value), lax.axis_index("dp")
    whole = lax.all_gather(value, "dp", axis=axis, tiled=True)
    low, high = jnp.split(whole, 2, axis=axis)
    return low, high, jnp.int32(0)


def after(value, *events):
    return lax.optimization_barrier((value, *events))[0]


def piece(value, index, size, axis):
    return lax.dynamic_slice_in_dim(value, index * size, size, axis)


def canon(blocks, index, axis):
    odd = (index & 1) == 1
    upper = (index & 2) == 2
    b = [
        jnp.where(odd, blocks[k ^ 1], blocks[k])
        for k in range(4)
    ]
    return jnp.concatenate([jnp.where(upper, b[k ^ 2], b[k]) for k in range(4)], axis=axis)


def dot_nn(a, b):
    return lax.dot_general(a, b, (((1,), (0,)), ((), ())), preferred_element_type=FULL)


def dot_nt(a, b):
    return lax.dot_general(a, b, (((1,), (1,)), ((), ())), preferred_element_type=FULL)


def dot_tn(a, b):
    return lax.dot_general(a, b, (((0,), (0,)), ((), ())), preferred_element_type=FULL)


def in_order():
    before = []

    def call(kernel, outs, scratch=(), smem=0, extra=2, wait=(), written=False):
        def run(*args):
            held = sum(a.size * jnp.dtype(a.dtype).itemsize for a in (*args, *outs))
            held += sum(
                math.prod(a.shape) * jnp.dtype(a.dtype).itemsize
                for a in scratch
                if a.memory_space == pltpu.VMEM
            )
            used = len(args)
            events = (*before, *wait)

            def body(*refs):
                rest = refs[used + len(events) :]
                if written:
                    rest[0][...] = jnp.zeros_like(rest[0])
                    rest = rest[1:]
                kernel(*refs[:used], *rest)

            vmem = pl.BlockSpec(memory_space=pltpu.VMEM)
            out_specs = [vmem] * len(outs)
            out_shape = list(outs)
            if written:
                out_specs = [vmem, pl.BlockSpec(memory_space=pltpu.HBM)]
                out_shape = [shape((8, LANES), FULL), *outs]
            results = pl.pallas_call(
                body,
                name=kernel.__qualname__.split(".")[0],
                out_shape=out_shape,
                in_specs=[pl.BlockSpec(memory_space=pltpu.SMEM)] * smem
                + [vmem] * (used - smem)
                + [pl.BlockSpec(memory_space=pl.ANY)] * len(events),
                out_specs=out_specs,
                scratch_shapes=scratch,
                compiler_params=pltpu.CompilerParams(vmem_limit_bytes=held + extra * 2**20),
                cost_estimate=pl.CostEstimate(flops=0, bytes_accessed=0, transcendentals=0),
            )(*args, *events)
            before[:] = [min(results, key=lambda r: r.size)]
            return results[-1] if written else results

        return run

    return call


def shape(dims, kind):
    return jax.ShapeDtypeStruct(dims, kind)


def normal(values):
    center = values - jnp.mean(values, axis=-1, keepdims=True)
    scale = lax.rsqrt(jnp.mean(center * center, axis=-1, keepdims=True) + EPS)
    return center * scale, scale


def pick_kernel(ids, array, mine, other):
    mine[...] = array[ids[3]]
    other[...] = array[1 - ids[3]]


def stack_kernel(*refs):
    out, start = refs[-1], 0
    for ref in refs[:-1]:
        out[start : start + ref.shape[0], :] = ref[...]
        start += ref.shape[0]


def pack_kernel(share, heads):
    def kernel(ids, weight, out):
        width = weight.shape[1] // 3
        head = share // heads
        for g in range(width // share):

            @pl.when(ids[1] == g)
            def _():
                def move(at_col, first):
                    out[:, at_col : at_col + head] = weight[:, first : first + head]

                for h in range(heads):
                    first = g * share + h * head
                    move(2 * h * head, width + first)
                    move((2 * h + 1) * head, 2 * width + first)
                    move(2 * share + h * head, first)

    return kernel


def rows_kernel(ids, array, out):
    out[...] = array[at(ids[2], out.shape[0]), :]


def fill_rows(ids, out, mine, other, other_two):
    half = mine.shape[0]
    out[at(ids[0], half), :] = mine[...]
    if other.shape[0] == half:
        out[at(1 - ids[0], half), :] = other[...]
        return
    size = half // 2
    out[at((1 - ids[0]) * 2 + ids[2], size), :] = other[...]
    out[at((1 - ids[0]) * 2 + 1 - ids[2], size), :] = other_two[...]


def norm_kernel(ids, mine, other, small, small_other, out, params):
    width = small.shape[1]
    params[:, lanes(ids[0], width)] = small[...].astype(FULL)
    params[:, lanes(1 - ids[0], width)] = small_other[...].astype(FULL)
    half = mine.shape[0]
    for start, part in ((0, mine), (half, other)):
        hat, _ = normal(part[...])
        out[start : start + half, :] = (hat * params[0:1, :] + params[1:2, :]).astype(LOW)


def grid_row(ids, n):
    k, u, i = n // 4, (n // 2) % 2, n % 2
    chunk = ((ids[6] ^ (k >> 1)) ^ (2 * u)) * 4 + ((ids[5] ^ (k & 1)) * 2) + ids[2]
    return chunk * 2 + i


def table_kernel(ids, mine, other, table, spot_one, spot_two):
    part, reach = mine.shape[1:]
    rows = lax.broadcasted_iota(jnp.int32, (reach, LANES), 0)
    cols = lax.broadcasted_iota(jnp.int32, (reach, LANES), 1)
    turn = jnp.where(rows == reach - 1 - cols, 1.0, 0.0).astype(LOW)
    table[...] = jnp.zeros_like(table)
    for k in range(2):
        spot = slice(k * LANES, (k + 1) * LANES)
        table[at(ids[0], part), spot] = dot_nn(mine[k], turn).astype(LOW)
        table[at(1 - ids[0], part), spot] = dot_nn(other[k], turn).astype(LOW)
    side = (reach + 1) // 2
    lane = lane_of(side)
    col = lax.broadcasted_iota(jnp.int32, (side, LANES), 0)
    total = spot_one.shape[0] // side
    for n in range(total):
        row = grid_row(ids, n % (total // 2))
        if n >= total // 2:
            row = row ^ 2
        here = slice(n * side, (n + 1) * side)
        target = jnp.where(lane < 96, row + 64, col + 96)
        one = jnp.where(lane == target, 1.0, 0.0)
        spot_one[here, :] = one.astype(LOW)
        ones = jnp.where((lane >= 64) & (lane < 67), 1.0, 0.0)
        spot_two[here, :] = (pltpu.roll(one, 64, 1) + ones).astype(LOW)


def lane_of(rows):
    return lax.broadcasted_iota(jnp.int32, (rows, LANES), 1)


def pieces_at(lane, first, value, rest):
    high = value.astype(LOW).astype(FULL)
    left = value - high
    mid = left.astype(LOW).astype(FULL)
    tail = left - mid
    out = jnp.where(lane == first, high, rest)
    out = jnp.where(lane == first + 1, mid, out)
    return jnp.where(lane == first + 2, tail, out)


def key_tiles(h, kva, kvb, spot_one, keys):
    half = kva.shape[0]
    lane = lane_of(half)
    for start, part in ((0, kva), (half, kvb)):
        tile = part[:, h * LANES : (h + 1) * LANES].astype(FULL)
        spots = spot_one[start : start + half, :].astype(FULL)
        keys[start : start + half, :LANES] = jnp.where(lane < 64, tile, spots).astype(LOW)


def attend_kernel(
    ids, query, kva, kvb, spot_one, spot_two, table, out, a0, a1, a2, a3, left, keys, turned, along
):
    rows = query.shape[0]
    heads = left.shape[0]
    half = kva.shape[0]
    lane32 = lane_of(32)
    block = 512
    lane = lane_of(block)
    size = a0.shape[0]
    turned[LANES:, :] = spot_two[...].astype(FULL).T.astype(LOW)
    for h in range(heads):
        key_tiles(h, kva, kvb, spot_one, keys)
        turned[:LANES, :] = keys[...].astype(FULL).T.astype(LOW)
        tile = query[:, (h // 2) * LANES : (h // 2 + 1) * LANES].astype(FULL)
        if h % 2:
            tile = pltpu.roll(tile, 64, 1)
        along[...] = dot_nn(tile.astype(LOW), table[...])
        for g in range(rows // 32):
            here = slice(g * 32, (g + 1) * 32)
            term_h = pltpu.roll(along[here, :LANES], 33 + grid_row(ids, g), 1)
            term_w = pltpu.roll(along[here, LANES:], 65, 1, stride=1, stride_axis=0)
            one = jnp.where(
                lane32 < 64, tile[here, :] * 0.125, jnp.where(lane32 < 96, term_h, term_w)
            )
            high = one.astype(LOW)
            rest = pltpu.roll(one - high.astype(FULL), 64, 1)
            left[h, here, :LANES] = high
            left[h, here, LANES:] = rest.astype(LOW)
        cols = slice(h * LANES, (h + 1) * LANES)
        spot = slice((h // 2) * LANES, (h // 2 + 1) * LANES)
        for q in range(rows // block):
            here = slice(q * block, (q + 1) * block)
            scores = dot_nn(left[h, here, :], turned[...])
            top = jnp.max(scores, axis=1, keepdims=True)
            expo = jnp.exp(scores - top)
            total = jnp.sum(expo, axis=1, keepdims=True)
            low = expo.astype(LOW)
            result = dot_nn(low[:, :half], kva[:, cols]) + dot_nn(low[:, half:], kvb[:, cols])
            result = result / total
            if h % 2 == 0:
                result = pltpu.roll(result, 64, 1)
            if h % 2:
                result = jnp.where(lane < 64, out[here, spot], result)
            else:
                result = jnp.where(lane < 64, result, 0.0)
            out[here, spot] = result
            for k in range(block // size):
                low_out = (a0, a1, a2, a3)[q * block // size + k]
                part = result[k * size : (k + 1) * size, :].astype(LOW)
                if h % 2:
                    low_out[:, spot] = part
                elif h == heads - 1:
                    low_out[:, h * 64 :] = part[:, :64]
            rest = left[h, here, LANES:].astype(FULL)
            left[h, here, LANES:] = pieces_at(lane, 64, -(top + jnp.log(total)), rest).astype(LOW)


def back_kernel(h):
    def kernel(
        ids, left, kva, kvb, spot_one, spot_two, table, g0, g1, g2, g3, value,
        dquery, dkv_mine, dkv_other, dtable,
        keys, vals, gright, qright, along, grad, left_t, right_t,
    ):
        rows = left.shape[1]
        half = kva.shape[0]
        lane = lane_of(rows)
        lane32 = lane_of(32)
        row = lax.broadcasted_iota(jnp.int32, (rows, LANES), 0)
        key_tiles(h, kva, kvb, spot_one, keys)
        keys[:, LANES:] = spot_two[...]
        cols = slice(h * LANES, (h + 1) * LANES)
        spot = slice((h // 2) * LANES, (h // 2 + 1) * LANES)
        for k, part in enumerate((g0, g1, g2, g3)):
            size, width = part.shape
            last = min(width, spot.stop)
            grad[k * size : (k + 1) * size, : last - spot.start] = part[:, spot.start : last].astype(FULL)
        vals[:half, :LANES] = kva[:, cols]
        vals[half:, :LANES] = kvb[:, cols]
        vals[:, LANES:] = spot_two[...]
        gtile = grad[...]
        otile = value[:, spot]
        if h % 2 == 0:
            gtile = pltpu.roll(gtile, 64, 1)
            otile = pltpu.roll(otile, 64, 1)
        gtile = jnp.where(lane >= 64, gtile, 0.0)
        inner = jnp.sum(gtile * otile, axis=1, keepdims=True)
        gright[...] = gtile.astype(LOW)
        extra = pieces_at(lane, 64, -inner, jnp.zeros_like(gtile))
        right_t[:LANES, :] = gtile.T.astype(LOW)
        right_t[LANES:, :] = extra.T.astype(LOW)
        for part in (slice(0, LANES), slice(LANES, 2 * LANES)):
            left_t[part, :] = left[h, :, part].astype(FULL).T.astype(LOW)
        qright[...] = jnp.where(lane < 64, left[h, :, :LANES].astype(FULL), 0.0).astype(LOW)
        probs = jnp.exp(dot_nn(keys[...], left_t[...]))
        dscores = (probs * dot_nn(vals[...], right_t[...])).astype(LOW)
        dkv = dot_nn(probs.astype(LOW), gright[...]) + dot_nn(dscores, qright[...])
        dkv_mine[...] = dkv[:half, :]
        dkv_other[...] = dkv[half:, :].astype(LOW)
        dq = dot_tn(keys[:, :LANES], dscores).T
        for g in range(rows // 32):
            here = slice(g * 32, (g + 1) * 32)
            part_h = jnp.where((lane32 >= 64) & (lane32 < 96), dq[here, :], 0.0)
            along[here, :LANES] = pltpu.roll(part_h, 95 - grid_row(ids, g), 1).astype(LOW)
        part_w = pltpu.roll(jnp.where(lane >= 96, dq, 0.0), 63, 1)
        for bit in range(5):
            moved = pltpu.roll(part_w, LANES - 2**bit, 1)
            part_w = jnp.where((row >> bit) & 1 == 1, moved, part_w)
        along[:, LANES:] = part_w.astype(LOW)
        dq = jnp.where(lane < 64, dq * 0.125 + dot_nt(along[...], table[...]), 0.0)
        if h % 2:
            dq = pltpu.roll(dq, 64, 1)
        dquery[...] = dq.astype(LOW)
        dtable[...] = dot_tn(along[...], qright[...])

    return kernel


def at(index, size):
    return pl.ds(pl.multiple_of(index * size, 16), size)


def lanes(index, size):
    return pl.ds(pl.multiple_of(index * size, LANES), size)


def mix_kernel(ids, n0, n1, n2, n3, mine, other, kv, query, rows, mix):
    half, last = mine.shape
    kv_cols = kv.shape[1]
    mix[at(ids[0], half), :last] = mine[...]
    mix[at(1 - ids[0], half), :last] = other[...]
    mix[:, last:] = jnp.zeros((mix.shape[0], mix.shape[1] - last), LOW)
    size = n0.shape[0]
    for k, part in enumerate((n0, n1, n2, n3)):
        here = slice(k * size, (k + 1) * size)
        rows[here, :] = part[...]
    both = dot_nn(rows[...], mix[...]).astype(LOW)
    kv[...] = both[:, :kv_cols]
    query[...] = both[:, kv_cols:]


def mid_kernel(
    ids, j0, j1, j2, j3, w_mine, w_other, w_two, own, own_got, params, middle, low, weight, whole
):
    fill_rows(ids, whole, w_mine, w_other, w_two)
    tok = own.shape[0]
    middle[:tok, :] = own[...]
    middle[tok:, :] = own_got[...]
    total = middle[...]
    width = j0.shape[1]
    for k, part in enumerate((j0, j1, j2, j3)):
        block = whole[at(ids[1] ^ k, width), :]
        weight[k * width : (k + 1) * width, :] = block
        total = total + dot_nn(part[...], block)
    middle[...] = total
    hat, _ = normal(total)
    low[...] = (hat * params[2:3, :] + params[3:4, :]).astype(LOW)


def feed_kernel(
    ids, r0, r1, r2, r3, c0, c1, c2, c3, up_mine, up_other, down_mine, down_other,
    d0, d1, d2, d3, active, dhidden, rows, cots, down, up,
):
    half = up_mine.shape[0]
    up[at(ids[0], half), :] = up_mine[...]
    up[at(1 - ids[0], half), :] = up_other[...]
    down[:, lanes(ids[0], half)] = down_mine[...]
    down[:, lanes(1 - ids[0], half)] = down_other[...]
    size = r0.shape[0]
    blocks = ((r0, c0, d0), (r1, c1, d1), (r2, c2, d2), (r3, c3, d3))
    for k, (row, cot, _) in enumerate(blocks):
        here = slice(k * size, (k + 1) * size)
        rows[here, :] = row[...]
        cots[here, :] = cot[...]
    hidden = dot_nn(rows[...], up[...])
    phi = 0.5 + 0.5 * lax.erf(hidden * 0.7071067811865476)
    active[...] = (hidden * phi).astype(LOW)
    slope = phi + hidden * (jnp.exp(hidden * hidden * -0.5) * 0.3989422804014327)
    dhidden[...] = (dot_nt(cots[...], down[...]) * slope).astype(LOW)
    back = dot_nt(dhidden[...], up[...]).astype(LOW)
    for k, (_, _, out) in enumerate(blocks):
        out[...] = back[k * size : (k + 1) * size, :]


def fed_kernel(active, down, f0, f1, f2):
    size = f0.shape[0]
    total = dot_nn(active[...], down[...]).astype(LOW)
    f0[...] = total[:size, :]
    f1[...] = total[size : 2 * size, :]
    f2[...] = total[2 * size :, :]


def outer_kernel(which, axis):
    def kernel(ids, a, b, sent, kept):
        half = sent.shape[axis]
        for index, out in ((1 - ids[which], sent), (ids[which], kept)):
            if axis == 0:
                out[...] = dot_tn(a[:, lanes(index, half)], b[...]).astype(LOW)
            else:
                out[...] = dot_tn(a[...], b[:, lanes(index, half)]).astype(LOW)

    return kernel


def proj_grad_kernel(ids, j0, j1, j2, j3, grad, sent, kept, whole):
    width = j0.shape[1]
    for k, part in enumerate((j0, j1, j2, j3)):
        whole[at(ids[1] ^ k, width), :] = dot_tn(part[...], grad[...])
    size = sent.shape[0] // 2
    for k, owner in enumerate((ids[0], 1 - ids[0])):
        here = slice(k * size, (k + 1) * size)
        sent[here, :] = whole[at(owner * 2 + 1 - ids[2], size), :].astype(LOW)
        kept[here, :] = whole[at(owner * 2 + ids[2], size), :].astype(LOW)


def split_kernel(which):
    def kernel(ids, a, b, sent, kept):
        size = sent.shape[0] // 2
        for k in range(2):
            here = slice(k * size, (k + 1) * size)
            for bit, out in ((1 - ids[which], sent), (ids[which], kept)):
                rows = pl.ds(pl.multiple_of(k * 2 * size + bit * size, 16), size)
                out[here, :] = (a[rows, :].astype(FULL) + b[rows, :].astype(FULL)).astype(LOW)

    return kernel


def owner_kernel(a, b, sent, kept):
    size = sent.shape[0]
    kept[...] = (a[:size, :].astype(FULL) + b[:size, :].astype(FULL)).astype(kept.dtype)
    sent[...] = (a[size:, :].astype(FULL) + b[size:, :].astype(FULL)).astype(LOW)


def tail_add_kernel(a, b, out):
    size = a.shape[0]
    out[...] = (a[...].astype(FULL) + b[b.shape[0] - size :, :].astype(FULL)).astype(out.dtype)


def vector_block(out, n0, n1, n2, n3, t0, t1, t2):
    out[...] = jnp.zeros_like(out)
    tables = (t0[...] + t1[...] + t2[...]) * 8.0
    side = 16
    for k in range(8):
        start = k // 4 * LANES + k % 4 * side
        out[:side, k * 64 : (k + 1) * 64] = tables[start : start + side, :64]
    tile = 0
    for row in (n0, n1, n2, n3):
        for k in range(row.shape[1] // LANES):
            spot = slice(tile % 4 * LANES, (tile % 4 + 1) * LANES)
            out[side + tile // 4 : side + tile // 4 + 1, spot] = row[:, k * LANES : (k + 1) * LANES]
            tile += 1


def row_sums(product):
    total = product[:, :LANES]
    for k in range(1, product.shape[1] // LANES):
        total = total + product[:, k * LANES : (k + 1) * LANES]
    return jnp.sum(total.T, axis=0, keepdims=True)


def vector_out_kernel(reach, split):
    def kernel(ids, *refs):
        *parts, params, n0, n1, n2, n3, t0, t1, total, norms = refs
        first = parts[0].shape[0] - total.shape[0]
        total[...] = sum(part[first:, :].astype(FULL) for part in parts)
        side = 16
        for tile in range(norms.shape[0] * norms.shape[1] // LANES):
            each = norms.shape[1] // LANES
            spot = slice(tile % 4 * LANES, (tile % 4 + 1) * LANES)
            norms[tile // each : tile // each + 1, tile % each * LANES : (tile % each + 1) * LANES] = (
                total[side + tile // 4 : side + tile // 4 + 1, spot]
            )
        gain, shift = params[0:1, :], params[1:2, :]
        norms[0:1, :] = (norms[0:1, :] - shift * norms[1:2, :]) / gain
        for k, out in enumerate((n0, n1, n2, n3)):
            width = out.shape[0]
            start = ids[7] * width if split else 0
            for tile in range(width // LANES):
                spot = pl.ds(pl.multiple_of(start + tile * LANES, LANES), LANES)
                out[tile * LANES : (tile + 1) * LANES] = norms[k, spot]
        rows = lax.broadcasted_iota(jnp.int32, (side, reach), 0)
        cols = lax.broadcasted_iota(jnp.int32, (side, reach), 1)
        for k, out in enumerate((t0, t1)):
            both = jnp.zeros((64, reach), FULL)
            for part in range(4):
                turn = jnp.where(rows + part * side == reach - 1 - cols, 1.0, 0.0)
                start = (k * 4 + part) * 64
                both = both + lax.dot_general(
                    total[:side, start : start + 64],
                    turn,
                    (((0,), (0,)), ((), ())),
                    precision=lax.Precision.HIGHEST,
                    preferred_element_type=FULL,
                )
            if split:
                size = out.shape[0]
                out[...] = jnp.where(ids[7] == 0, both[:size, :], both[size:, :])
            else:
                out[...] = both

    return kernel


def dmix_kernel(dkv, dquery, mix, mine, near, sent):
    size = mine.shape[0]
    cols = dkv.shape[1]
    total = dot_nt(dkv[...], mix[:, :cols]) + dot_nt(dquery[...], mix[:, cols:])
    for k, (out, start) in enumerate(((mine, 0), (sent, 0), (near, 0), (sent, size))):
        out[start : start + size, :] = total[k * size : (k + 1) * size, :].astype(LOW)


def dkv_kernel(m0, m1, m2, o0, o1, o2, q0, q1, q2, dkv, dquery):
    for h, (mine, got) in enumerate(((m0, o0), (m1, o1), (m2, o2))):
        cols = slice(h * LANES, (h + 1) * LANES)
        dkv[:, cols] = (mine[...] + got[...].astype(FULL)).astype(LOW)
    dquery[:, :LANES] = (q0[...].astype(FULL) + q1[...].astype(FULL)).astype(LOW)
    dquery[:, LANES:] = q2[...]


def qkv_grad_kernel(
    ids, rows, m0, m1, m2, o0, o1, o2, q0, q1, q2, mix, v2, v3, t0, t1, t2,
    dkv, dquery, sent, kept, whole, vector,
):
    dkv_kernel(m0, m1, m2, o0, o1, o2, q0, q1, q2, dkv, dquery)
    cols = dkv.shape[1]
    whole[:, :cols] = dot_tn(rows[...], dkv[...])
    whole[:, cols:] = dot_tn(rows[...], dquery[...])
    width = kept.shape[1]
    size = (kept.shape[0] - vector.shape[0]) // 2
    sums_block(whole, dkv, dquery, mix, v2, v3, t0, t1, t2, vector)
    for out, core in ((sent, 1 - ids[2]), (kept, ids[2])):
        for k, owner in enumerate((ids[0], 1 - ids[0])):
            here = slice(k * size, (k + 1) * size)
            out[here, :] = whole[at(owner * 2 + core, size), :width].astype(LOW)
        out[2 * size :, :] = vector[...].astype(LOW)


def sums_block(whole, dkv, dquery, mix, v2, v3, t0, t1, t2, vector):
    weights = mix[...].astype(FULL)
    sums = jnp.concatenate(
        [jnp.sum(part[...].astype(FULL), axis=0, keepdims=True) for part in (dkv, dquery)], axis=1
    )
    both = row_sums(whole[...] * weights)
    shift = row_sums(weights * sums)
    vector_block(vector, both, shift, v2, v3, t0, t1, t2)


def sums_kernel(rows, dkv, dquery, mix, v2, v3, t0, t1, t2, vector, whole):
    cols = dkv.shape[1]
    whole[:, :cols] = dot_tn(rows[...], dkv[...])
    whole[:, cols:] = dot_tn(rows[...], dquery[...])
    sums_block(whole, dkv, dquery, mix, v2, v3, t0, t1, t2, vector)


def qkv_owner_kernel(a, b, sent, kept):
    size = a.shape[0] - sent.shape[0]
    kept[:size, :] = a[:size, :].astype(FULL) + b[:size, :].astype(FULL)
    total = a[size:, :].astype(FULL) + b[size:, :].astype(FULL)
    kept[size:, :] = total[size:, :]
    sent[...] = total.astype(LOW)


def add_kernel(*refs):
    total = refs[0][...].astype(FULL)
    for ref in refs[1:-1]:
        total = total + ref[...].astype(FULL)
    refs[-1][...] = total.astype(refs[-1].dtype)


def halve_kernel(which):
    def kernel(ids, a, b, sent, kept):
        size = sent.shape[0]
        bit = ids[which]
        for index, out in ((1 - bit, sent), (bit, kept)):
            here = at(index, size)
            out[...] = (a[here, :].astype(FULL) + b[here, :].astype(FULL)).astype(out.dtype)

    return kernel


def join_kernel(which):
    def kernel(ids, mine, other, out):
        size = mine.shape[0]
        out[at(ids[which], size), :] = mine[...].astype(out.dtype)
        out[at(1 - ids[which], size), :] = other[...].astype(out.dtype)

    return kernel


def qkv_out_kernel(heads):
    def kernel(ids, q0, q1, q2, q3, o0, o1, o2, o3, out, whole, sem):
        size = out.shape[0] // 2
        lane = lane_of(size)
        first = lane < 64
        groups = 4
        share = heads * 64
        width = groups * share
        places = [pl.ds(pl.multiple_of(p * size, 16), size) for p in (ids[2], 1 - ids[2])]

        def fill(part, refs):
            here = places[part]

            def tile(g, column):
                stop = min(column + LANES, q0.shape[1])
                one = refs[g][:size, column:stop].astype(FULL)
                if stop - column < LANES:
                    one = jnp.concatenate([one, jnp.zeros_like(one)], axis=1)
                return one

            for pair in range(groups * heads // 2):
                ends = []
                for n in (2 * pair, 2 * pair + 1):
                    g, h = n // heads, n % heads
                    q = tile(g, 2 * share + (h // 2) * LANES)
                    if h % 2:
                        q = pltpu.roll(q, 64, 1)
                    ends.append((q, tile(g, h * LANES)))
                (qa, kva), (qb, kvb) = ends
                at_col = pair * LANES
                for start, a, b in (
                    (0, qa, pltpu.roll(qb, 64, 1)),
                    (width, kva, pltpu.roll(kvb, 64, 1)),
                    (2 * width, pltpu.roll(kva, 64, 1), kvb),
                ):
                    here_cols = slice(start + at_col, start + at_col + LANES)
                    whole[here, here_cols] = jnp.where(first, a, b)

        for part, refs in enumerate(((q0, q1, q2, q3), (o0, o1, o2, o3))):
            for g in range(groups):

                @pl.when(ids[1] == g)
                def _():
                    fill(part, [refs[k ^ g] for k in range(groups)])

            here = places[part]
            pltpu.make_async_copy(whole.at[here], out.at[here], sem.at[part]).start()
        for part, here in enumerate(places):
            pltpu.make_async_copy(whole.at[here], out.at[here], sem.at[part]).wait()

    return kernel


def change_kernel(middle, own, own_got, f0, f1, f2, mine, sent):
    tok = own.shape[0]
    for part, base, out in ((0, own, mine), (tok, own_got, sent)):
        here = slice(part, part + tok)
        fed = f0[here, :].astype(FULL) + f1[here, :].astype(FULL) + f2[here, :].astype(FULL)
        total = middle[here, :] + fed
        if part:
            total = total - base[...]
        out[...] = total.astype(out.dtype)


def place_kernel(ids, mine, got, base, out, low, sem):
    first = pltpu.make_async_copy(mine, out.at[ids[3]], sem.at[0])
    first.start()
    low[...] = got[...].astype(FULL) + base[...]
    second = pltpu.make_async_copy(low, out.at[1 - ids[3]], sem.at[1])
    second.start()
    first.wait()
    second.wait()


def place_two_kernel(ids, mine, got, out, low, sem):
    first = pltpu.make_async_copy(mine, out.at[ids[3]], sem.at[0])
    first.start()
    low[...] = got[...].astype(FULL)
    second = pltpu.make_async_copy(low, out.at[1 - ids[3]], sem.at[1])
    second.start()
    first.wait()
    second.wait()


def join_out_kernel(which):
    def kernel(ids, mine, other, out, whole, sem):
        size = mine.shape[0]
        copies = []
        for k, (place, ref) in enumerate(((ids[which], mine), (1 - ids[which], other))):
            here = at(place, size)
            whole[here, :] = ref[...].astype(FULL)
            copies.append(pltpu.make_async_copy(whole.at[here], out.at[here], sem.at[k]))
            copies[-1].start()
        for copy in copies:
            copy.wait()

    return kernel


def halve_lanes_kernel(which):
    def kernel(ids, a, b, sent, kept):
        size = sent.shape[1]
        for bit, out in ((1 - ids[which], sent), (ids[which], kept)):
            here = lanes(bit, size)
            out[...] = (a[:, here].astype(FULL) + b[:, here].astype(FULL)).astype(out.dtype)

    return kernel


def norm_back(grad, values, gain):
    hat, scale = normal(values)
    scaled = grad * gain
    back = scale * (
        scaled
        - jnp.mean(scaled, axis=-1, keepdims=True)
        - hat * jnp.mean(scaled * hat, axis=-1, keepdims=True)
    )
    return back, jnp.sum(grad * hat, axis=0, keepdims=True), jnp.sum(grad, axis=0, keepdims=True)


def mid_back_kernel(
    a0, a1, a2, middle, params, cot, weight, gmiddle, gbranch, b0, b1, b2, b3, dgain, dshift
):
    size = a0.shape[0]
    grad = a0[...].astype(FULL) + a1[...].astype(FULL) + a2[...].astype(FULL)
    back, dgain[...], dshift[...] = norm_back(grad, middle[...], params[2:3, :])
    total = cot[:size, :].astype(FULL) + back
    gmiddle[...] = total
    low = total.astype(LOW)
    gbranch[...] = low
    width = b0.shape[1]
    for k, out in enumerate((b0, b1, b2, b3)):
        out[...] = dot_nt(low, weight[k * width : (k + 1) * width, :]).astype(LOW)


def first_back_kernel(a0, a1, a2, own, own_got, params, gmiddle, mine, sent, rows):
    tok = own.shape[0]
    rows[:tok, :] = own[...]
    rows[tok:, :] = own_got[...]
    grad = a0[...].astype(FULL) + a1[: 2 * tok, :].astype(FULL) + a2[...].astype(FULL)
    back, _, _ = norm_back(grad, rows[...], params[0:1, :])
    total = gmiddle[...] + back
    mine[...] = total[:tok, :]
    sent[...] = total[tok:, :].astype(LOW)


def on_device(
    tokens,
    ln1_gain,
    ln1_bias,
    qkv_weight,
    rel_h,
    rel_w,
    proj_weight,
    ln2_gain,
    ln2_bias,
    fc1_weight,
    fc2_weight,
    cotangent,
):
    images, tok, width = tokens.shape
    hid = fc1_weight.shape[1]
    dp_count = lax.axis_size("dp")
    head = rel_h.shape[1] * dp_count
    reach = rel_h.shape[0]
    s, t = lax.axis_index("seq"), lax.axis_index("tp")
    d = lax.axis_index("dp")
    y, c = t // 2, t % 2
    image = s // 2
    group = (s % 2) * 2 + y
    groups = 4
    share = width // groups
    heads = share // head
    rows_n = 2 * tok
    half = width // 2
    me = d if dp_count == 2 else jnp.int32(0)
    ids = jnp.stack([me, group, c, image, s % 2, y, s, d]).astype(jnp.int32)
    n = 4 * rows_n
    kv_cols = 2 * share
    pad_share = 2 * LANES
    key_n = 2 * n
    qkv_cols = 3 * share
    low_tok, full_tok = shape((tok, width), LOW), shape((tok, width), FULL)
    low_rows, full_rows = shape((rows_n, width), LOW), shape((rows_n, width), FULL)
    two_rows = shape((2 * rows_n, width), LOW)
    heads_rows = shape((rows_n, share), LOW)
    way = (0, ROW, NEAR, ROW | NEAR)

    def add(kind, *args, wait=()):
        return call(add_kernel, [shape(args[0].shape, kind)], wait=wait)(*args)[0]

    call = in_order()
    quarter, eighth = half // 2, half // 4
    norm_sums = [shape((1, width), FULL)] * 2

    def written(kernel, dims, extra=2):
        return call(
            kernel,
            [shape(dims, FULL)],
            [pltpu.VMEM(dims, FULL), pltpu.SemaphoreType.DMA((2,))],
            smem=1,
            extra=extra,
            written=True,
        )

    def total_of(kind, *args):
        return call(add_kernel, [shape(args[0].shape, kind)])(*args)[0]

    def halve(which, a, b, kind=FULL):
        dims = (a.shape[0] // 2, a.shape[1])
        return call(halve_kernel(which), [shape(dims, LOW), shape(dims, kind)], smem=1)(ids, a, b)

    def split(which, a, b):
        dims = (a.shape[0] // 2, a.shape[1])
        return call(split_kernel(which), [shape(dims, LOW)] * 2, smem=1)(ids, a, b)

    def join(which, mine, other, kind):
        dims = (2 * mine.shape[0], mine.shape[1])
        return call(join_kernel(which), [shape(dims, kind)], smem=1)(ids, mine, other)[0]

    own, away = call(pick_kernel, [full_tok] * 2, smem=1)(ids, tokens)
    own_got = hop(away, FAR)
    small = jnp.concatenate([ln1_gain, ln1_bias, ln2_gain, ln2_bias]).reshape(4, -1)
    small, small_other, _ = pair_dp(after(small, away), 1)
    tables = jnp.stack([rel_h.T, rel_w.T])
    tables, tables_other, _ = pair_dp(after(tables, away), 1)
    cot_mine, cot_away = call(pick_kernel, [low_tok] * 2, smem=1)(ids, cotangent)
    cot_got = hop(cot_away, FAR)
    depth = qkv_weight.shape[0]
    mix_mine = call(
        pack_kernel(share, heads),
        [shape((depth, qkv_cols), LOW)],
        smem=1,
        wait=(small_other, tables_other),
    )(ids, qkv_weight)[0]
    mix_mine, mix_other, _ = pair_dp(after(mix_mine, own_got), 0)

    normed, params = call(norm_kernel, [low_rows, shape((4, width), FULL)], smem=1)(
        ids, own, own_got, small, small_other
    )
    normed_parts = [normed] + [hop(normed, b) for b in way[1:]]
    cot = call(stack_kernel, [low_rows])(cot_mine, cot_got)[0]
    table, spot_one, spot_two = call(
        table_kernel,
        [shape((LANES, 2 * LANES), LOW)] + [shape((key_n, LANES), LOW)] * 2,
        smem=1,
    )(ids, tables, tables_other)
    if dp_count == 2:
        proj_part = call(rows_kernel, [shape((half // 2, width), LOW)], smem=1)(ids, proj_weight)[0]

    kv, query, normed_all, mix = call(
        mix_kernel,
        [
            shape((n, kv_cols), LOW),
            shape((n, pad_share), LOW),
            shape((n, width), LOW),
            shape((width, kv_cols + pad_share), LOW),
        ],
        smem=1,
        extra=3,
    )(ids, *normed_parts, mix_mine, mix_other)
    kv_other = hop(kv, CORE)
    cot_row = hop(after(cot, kv), ROW)
    if dp_count == 2:
        proj_mine, proj_other = proj_weight, swap_dp(after(proj_part, normed))
    else:
        proj_mine, proj_other, _ = pair_dp(proj_weight, 0)
    proj_two = hop(after(proj_other, kv), CORE)
    up_mine, up_other, _ = pair_dp(after(fc1_weight, kv), 0)

    down_mine, down_other, _ = pair_dp(after(fc2_weight, kv), 1)

    attended, *attended_low, left = call(
        attend_kernel,
        [shape((n, pad_share), FULL)]
        + [heads_rows] * 4
        + [shape((heads, n, 2 * LANES), LOW)],
        [
            pltpu.VMEM((key_n, LANES), LOW),
            pltpu.VMEM((2 * LANES, key_n), LOW),
            pltpu.VMEM((n, 2 * LANES), FULL),
        ],
        smem=1,
        extra=16,
    )(ids, query, kv, kv_other, spot_one, spot_two, table)
    attended_low = lax.optimization_barrier((*attended_low, cot_row, proj_two))[:4]
    joined = [attended_low[0]] + [hop(attended_low[k], way[k]) for k in (1, 2, 3)]
    middle, normed_two, proj = call(
        mid_kernel,
        [full_rows, low_rows, shape((width, width), LOW)],
        [pltpu.VMEM((width, width), LOW)],
        smem=1,
    )(ids, *joined, proj_mine, proj_other, proj_two, own, own_got, params)

    two_row = hop(normed_two, ROW)
    two_core = hop(normed_two, CORE)
    two_diag = hop(two_row, CORE)
    cot_core = hop(after(cot, two_row), CORE)
    cot_diag = hop(after(cot_row, two_row), CORE)
    d0, d1, d2, d3, active, dhidden, rows_all, cot_all, down = call(
        feed_kernel,
        [low_rows] * 4
        + [shape((n, hid), LOW)] * 2
        + [shape((n, width), LOW)] * 2
        + [shape((hid, width), LOW)],
        [pltpu.VMEM((width, hid), LOW)],
        smem=1,
        extra=12,
    )(
        ids, normed_two, two_row, two_core, two_diag, cot, cot_row, cot_core, cot_diag,
        up_mine, up_other, down_mine, down_other,
    )
    dnorm_next = hop(d3, CORE)
    dnorm_mine = hop(d2, CORE)

    mixed_shapes = [shape((n, kv_cols), LOW), shape((n, pad_share), LOW)]
    vector_rows = 32
    whole_shape = pltpu.VMEM((width, kv_cols + pad_share), FULL)
    qkv_rows = (quarter + vector_rows, qkv_cols)
    proj_low = shape((eighth, width), LOW)
    v, fc1, fc2 = (types.SimpleNamespace() for _ in range(3))

    def send(value, bits, *events):
        return hop(after(value, *events) if events else value, bits)

    def dnorm_add():
        v.dnorm_row = send(total_of(LOW, d1, dnorm_next), ROW)

    def fc1_outer():
        sent, fc1.kept = call(outer_kernel(0, 0), [shape((half, hid), LOW)] * 2, smem=1, extra=4)(
            ids, rows_all, dhidden
        )
        if dp_count == 2:
            fc1.got = swap_dp(sent)

    def far_sum(part):
        def step():
            sent, part.kept = halve(3, part.kept, part.got)
            part.got = send(sent, FAR)

        return step

    def far_all(part):
        def step():
            part.kept = total_of(LOW, part.kept, part.got)
            part.got = send(part.kept, FAR)

        return step

    def near_all(part):
        def step():
            part.kept = join(3, part.kept, part.got, LOW)
            part.got = send(part.kept, NEAR)

        return step

    def last(part, dims):
        def step():
            part.grad = written(join_out_kernel(4), dims)(ids, part.kept, part.got)

        return step

    def fc2_outer():
        sent, fc2.kept = call(
            outer_kernel(4, 0), [shape((hid // 2, width), LOW)] * 2, smem=1, extra=4
        )(ids, active, cot_all)
        fc2.got = send(sent, NEAR)

    def mid_back():
        v.gmiddle, v.gbranch, *parts, v.dgain_two, v.dshift_two = call(
            mid_back_kernel, [full_rows, low_rows] + [heads_rows] * 4 + norm_sums
        )(d0, dnorm_mine, v.dnorm_row, middle, params, cot, proj)
        v.grads = [parts[0]] + [
            send(b, bits) for b, bits in zip(parts[1:], way[1:])
        ]

    def proj_outer():
        sent, v.proj = call(
            proj_grad_kernel,
            [shape((half, width), LOW)] * 2,
            [pltpu.VMEM((width, width), FULL)],
            smem=1,
        )(ids, *joined, v.gbranch)
        v.proj_got = send(after(sent, *v.grads), CORE)

    def fed():
        v.f0, v.f1, f2 = call(fed_kernel, [low_rows, low_rows, two_rows], extra=4)(
            active, down
        )
        v.fed_got = send(after(f2, *v.grads), CORE)

    def back(h):
        dquery, mine, other, dtable = call(
            back_kernel(h),
            [
                shape((n, LANES), LOW),
                shape((n, LANES), FULL),
                shape((n, LANES), LOW),
                shape((2 * LANES, LANES), FULL),
            ],
            [
                pltpu.VMEM((key_n, 2 * LANES), LOW),
                pltpu.VMEM((key_n, 2 * LANES), LOW),
                pltpu.VMEM((n, LANES), LOW),
                pltpu.VMEM((n, LANES), LOW),
                pltpu.VMEM((n, 2 * LANES), LOW),
                pltpu.VMEM((n, LANES), FULL),
                pltpu.VMEM((2 * LANES, n), LOW),
                pltpu.VMEM((2 * LANES, n), LOW),
            ],
            smem=1,
            extra=20,
            wait=(v.back[-1][1],) if v.back else (),
        )(ids, left, kv, kv_other, spot_one, spot_two, table, *v.grads, attended)
        v.back.append((mine, send(other, CORE), dquery, dtable))

    v.back = []

    def back0():
        back(0)

    def back1():
        back(1)

    def back2():
        back(2)

    def fed_add():
        sent = call(tail_add_kernel, [low_rows])(v.f1, v.fed_got)[0]
        v.fed_row = send(sent, ROW)

    def change():
        v.change, sent = call(change_kernel, [full_tok, low_tok])(
            middle, own, own_got, v.f0, v.fed_got, v.fed_row
        )
        v.change_got = send(sent, FAR)

    def place_output():
        v.output = call(
            place_kernel,
            [shape(tokens.shape, FULL)],
            [pltpu.VMEM((tok, width), FULL), pltpu.SemaphoreType.DMA((2,))],
            smem=1,
            written=True,
        )(ids, v.change, v.change_got, away)

    def qkv_outer():
        mine, got, queries, tables = zip(*v.back)
        v.dkv, v.dquery, sent, v.qkv = call(
            qkv_grad_kernel,
            mixed_shapes + [shape((half + vector_rows, qkv_cols), LOW)] * 2,
            [whole_shape, pltpu.VMEM((vector_rows, qkv_cols), FULL)],
            smem=1,
            extra=6,
        )(
            ids, normed_all, *mine, *got, *queries, mix, v.dgain_two, v.dshift_two, *tables
        )
        v.qkv_got = send(sent, CORE)

    def qkv_owner():
        sent, v.qkv = call(qkv_owner_kernel, [shape(qkv_rows, LOW), shape(qkv_rows, FULL)])(
            v.qkv, v.qkv_got
        )
        v.qkv_got = swap_dp(sent)

    def qkv_images():
        v.qkv = total_of(LOW, v.qkv, v.qkv_got)
        v.qkv_got = send(v.qkv, FAR)

    def qkv_total():
        part = total_of(LOW, v.qkv, v.qkv_got)
        near = send(part, NEAR)
        v.qkv_parts = [part, send(part, ROW), near, send(near, ROW)]

    def vector_last():
        *norms, table_h, table_w = vector_out(v.qkv_parts, half, head // 2)
        v.norms = norms
        v.tables = (table_h.T, table_w.T)
        v.qkv_others = [send(part, CORE) for part in v.qkv_parts]

    def qkv_last():
        v.qkv_grad = written(qkv_out_kernel(heads), (half, 3 * width), 4)(
            ids, *v.qkv_parts, *v.qkv_others
        )

    def mixed_back():
        v.e_mine, v.e_near, e_row = call(
            dmix_kernel, [low_rows, low_rows, two_rows], extra=6
        )(
            v.dkv, v.dquery, mix
        )
        v.e_got = send(e_row, ROW)

    def normed_near():
        sent = call(tail_add_kernel, [low_rows])(v.e_near, v.e_got)[0]
        v.e_last = send(sent, NEAR)

    def first_back():
        v.token, sent = call(
            first_back_kernel, [full_tok, low_tok], [pltpu.VMEM((rows_n, width), FULL)]
        )(v.e_mine, v.e_got, v.e_last, own, own_got, params, v.gmiddle)
        v.token_got = send(sent, FAR)

    def place_tokens():
        v.tokens_grad = call(
            place_two_kernel,
            [shape(tokens.shape, FULL)],
            [pltpu.VMEM((tok, width), FULL), pltpu.SemaphoreType.DMA((2,))],
            smem=1,
            written=True,
        )(ids, v.token, v.token_got)

    def fc1_near_sum():
        sent, fc1.kept = halve(4, fc1.kept, fc1.got)
        fc1.got = send(sent, NEAR)

    def fc2_near_sum():
        dims = (hid // 2, half)
        sent, fc2.kept = call(
            halve_lanes_kernel(0), [shape(dims, LOW), shape(dims, FULL)], smem=1
        )(ids, fc2.kept, fc2.got)
        fc2.got = swap_dp(sent)

    def proj_split():
        sent, v.proj = split(5, v.proj, v.proj_got)
        v.proj_got = send(sent, ROW)

    def proj_owner():
        sent, v.proj = call(owner_kernel, [proj_low] * 2)(v.proj, v.proj_got)
        v.proj_got = swap_dp(sent)

    def proj_sum(bits):
        def step():
            v.proj = total_of(LOW, v.proj, v.proj_got)
            v.proj_got = send(v.proj, bits)

        return step

    def proj_join():
        v.proj = join(5, v.proj, v.proj_got, LOW)
        v.proj_got = send(v.proj, CORE)

    def proj_last():
        v.proj_grad = written(join_out_kernel(2), (half, width))(ids, v.proj, v.proj_got)

    def vector_out(parts, size, features):
        return call(
            vector_out_kernel(reach, dp_count == 2),
            [shape((size,), FULL)] * 4 + [shape((features, reach), FULL)] * 2,
            [pltpu.VMEM((vector_rows, qkv_cols), FULL), pltpu.VMEM((4, width), FULL)],
            smem=1,
        )(ids, *parts, params)

    if dp_count == 2:
        for step in (
            fc2_outer,
            dnorm_add,
            fc1_outer,
            mid_back,
            fc2_near_sum,
            proj_outer,
            back0,
            back1,
            fed,
            back2,
            fc1_near_sum,
            far_sum(fc2),
            qkv_outer,
            qkv_owner,
            fed_add,
            proj_split,
            far_sum(fc1),
            qkv_images,
            mixed_back,
            far_all(fc2),
            proj_owner,
            proj_sum(NEAR),
            qkv_total,
            change,
            near_all(fc2),
            proj_sum(FAR),
            far_all(fc1),
            normed_near,
            proj_sum(ROW),
            place_output,
            first_back,
            proj_join,
            vector_last,
            last(fc2, (hid, half)),
            near_all(fc1),
            place_tokens,
            qkv_last,
            proj_last,
            last(fc1, (half, hid)),
        ):
            step()
        output, tokens_grad, qkv_grad = v.output, v.tokens_grad, v.qkv_grad
        proj_grad, fc1_grad, fc2_grad = v.proj_grad, fc1.grad, fc2.grad
        norms, dtables = v.norms, v.tables
    else:
        every = ("seq", "tp")
        for step in (dnorm_add, mid_back, fed, back0, back1, back2, fed_add, change, place_output):
            step()
        mine, other, queries, tables = zip(*v.back)
        v.dkv, v.dquery = call(dkv_kernel, mixed_shapes)(*mine, *other, *queries)
        for step in (mixed_back, normed_near, first_back, place_tokens):
            step()
        output, tokens_grad = v.output, v.tokens_grad
        dkv, dquery, gbranch = v.dkv, v.dquery, v.gbranch

        def weight_sum(a, b, axes, axis=0):
            part = lax.psum_scatter(
                dot_tn(a, b).astype(LOW), "dp", scatter_dimension=axis, tiled=True
            )
            return lax.psum(part, axes).astype(FULL)

        fc1_grad = weight_sum(rows_all, dhidden, "seq")
        fc2_grad = weight_sum(active, cot_all, "seq", 1)
        proj_grad = weight_sum(canon(joined, group, 1), gbranch, every)
        dmixed = jnp.concatenate([dkv, dquery], axis=1)[:, :qkv_cols]
        part = dot_tn(normed_all, dmixed).astype(LOW)
        part = lax.psum_scatter(part, "dp", scatter_dimension=0, tiled=True)
        part = part.astype(FULL) + hop(part, FAR).astype(FULL)
        part = part.astype(LOW)
        part = (part.astype(FULL) + hop(part, CORE).astype(FULL)).astype(LOW)
        whole = canon([part[None]] + [hop(part, bits)[None] for bits in way[1:]], group, 0)
        depth = whole.shape[1]
        pairs = whole[:, :, :kv_cols].reshape(groups, depth, heads, 2, head)
        qkv_grad = jnp.concatenate(
            [
                whole[:, :, kv_cols:].transpose(1, 0, 2).reshape(depth, width),
                pairs[:, :, :, 0].transpose(1, 0, 2, 3).reshape(depth, width),
                pairs[:, :, :, 1].transpose(1, 0, 2, 3).reshape(depth, width),
            ],
            axis=1,
        ).astype(FULL)
        vector = call(sums_kernel, [shape((vector_rows, qkv_cols), FULL)], [whole_shape], extra=6)(
            normed_all, dkv, dquery, mix, v.dgain_two, v.dshift_two, *tables
        )[0]
        vector = lax.psum(vector, ("dp", *every))
        *norms, table_h, table_w = vector_out((vector,), width, head)
        norms = [piece(row, d, width // dp_count, 0) for row in norms]
        dtables = [piece(t.T, d, head // dp_count, 1) for t in (table_h, table_w)]
    return (
        output,
        tokens_grad,
        norms[0],
        norms[1],
        qkv_grad,
        dtables[0],
        dtables[1],
        proj_grad,
        norms[2],
        norms[3],
        fc1_grad,
        fc2_grad,
    )


def solution(mesh):
    split = P("dp", ("seq", "tp"), None)
    params = (
        P("dp"),
        P("dp"),
        P("dp", None),
        P(None, "dp"),
        P(None, "dp"),
        P("dp", None),
        P("dp"),
        P("dp"),
        P("dp", "tp"),
        P("tp", "dp"),
    )
    return jax.shard_map(
        on_device,
        mesh=mesh,
        in_specs=(split, *params, split),
        out_specs=(split, split, *params),
        check_vma=False,
    )
```

```python
import math
import types

import jax
import jax.numpy as jnp
from jax import lax
from jax.experimental import pallas as pl
from jax.experimental.pallas import tpu as pltpu
from jax.sharding import PartitionSpec as P

EPS = 1e-06
LOW = jnp.bfloat16
FULL = jnp.float32
LANES = 128
CORE, ROW, NEAR, FAR = 1, 2, 4, 8


def hop(value, bits):
    count = lax.axis_size("seq") * lax.axis_size("tp")
    return lax.ppermute(value, ("seq", "tp"), [(i, i ^ bits) for i in range(count)])


def swap_dp(value):
    return lax.ppermute(value, "dp", [(0, 1), (1, 0)])


def pair_dp(value, axis):
    if lax.axis_size("dp") == 2:
        return value, swap_dp(value), lax.axis_index("dp")
    whole = lax.all_gather(value, "dp", axis=axis, tiled=True)
    low, high = jnp.split(whole, 2, axis=axis)
    return low, high, jnp.int32(0)


def after(value, *events):
    return lax.optimization_barrier((value, *events))[0]


def piece(value, index, size, axis):
    return lax.dynamic_slice_in_dim(value, index * size, size, axis)


def canon(blocks, index, axis):
    odd = (index & 1) == 1
    upper = (index & 2) == 2
    b = [
        jnp.where(odd, blocks[k ^ 1], blocks[k])
        for k in range(4)
    ]
    return jnp.concatenate([jnp.where(upper, b[k ^ 2], b[k]) for k in range(4)], axis=axis)


def dot_nn(a, b):
    return lax.dot_general(a, b, (((1,), (0,)), ((), ())), preferred_element_type=FULL)


def dot_nt(a, b):
    return lax.dot_general(a, b, (((1,), (1,)), ((), ())), preferred_element_type=FULL)


def dot_tn(a, b):
    return lax.dot_general(a, b, (((0,), (0,)), ((), ())), preferred_element_type=FULL)


def in_order():
    before = []

    def call(kernel, outs, scratch=(), smem=0, extra=2, wait=(), written=0, mark=False):
        def run(*args):
            held = sum(a.size * jnp.dtype(a.dtype).itemsize for a in (*args, *outs))
            held += sum(
                math.prod(a.shape) * jnp.dtype(a.dtype).itemsize
                for a in scratch
                if a.memory_space == pltpu.VMEM
            )
            used = len(args)
            events = (*before, *wait)

            def body(*refs):
                rest = refs[used + len(events) :]
                if written or mark:
                    rest[0][...] = jnp.zeros_like(rest[0])
                    rest = rest[1:]
                kernel(*refs[:used], *rest)

            vmem = pl.BlockSpec(memory_space=pltpu.VMEM)
            out_specs = [vmem] * len(outs)
            out_shape = list(outs)
            if written or mark:
                hbm = pl.BlockSpec(memory_space=pltpu.HBM)
                out_specs = [vmem] + [hbm if written else vmem] * len(outs)
                out_shape = [shape((8, LANES), FULL), *outs]
            results = pl.pallas_call(
                body,
                name=kernel.__qualname__.split(".")[0],
                out_shape=out_shape,
                in_specs=[pl.BlockSpec(memory_space=pltpu.SMEM)] * smem
                + [vmem] * (used - smem)
                + [pl.BlockSpec(memory_space=pl.ANY)] * len(events),
                out_specs=out_specs,
                scratch_shapes=scratch,
                compiler_params=pltpu.CompilerParams(vmem_limit_bytes=held + extra * 2**20),
                cost_estimate=pl.CostEstimate(flops=0, bytes_accessed=0, transcendentals=0),
            )(*args, *events)
            before[:] = [min(results, key=lambda r: r.size)]
            return results[1:] if written or mark else results

        return run

    return call


def shape(dims, kind):
    return jax.ShapeDtypeStruct(dims, kind)


def normal(values):
    center = values - jnp.mean(values, axis=-1, keepdims=True)
    scale = lax.rsqrt(jnp.mean(center * center, axis=-1, keepdims=True) + EPS)
    return center * scale, scale


def pick_kernel(ids, array, mine, other):
    mine[...] = array[ids[3]]
    other[...] = array[1 - ids[3]]


def stack_kernel(*refs):
    out, start = refs[-1], 0
    for ref in refs[:-1]:
        out[start : start + ref.shape[0], :] = ref[...]
        start += ref.shape[0]


def pack_kernel(share, heads):
    def kernel(ids, weight, out):
        width = weight.shape[1] // 3
        head = share // heads
        for g in range(width // share):

            @pl.when(ids[1] == g)
            def _():
                def move(at_col, first):
                    out[:, at_col : at_col + head] = weight[:, first : first + head]

                for h in range(heads):
                    first = g * share + h * head
                    move(2 * h * head, width + first)
                    move((2 * h + 1) * head, 2 * width + first)
                    move(2 * share + h * head, first)

    return kernel


def rows_kernel(ids, array, out):
    out[...] = array[at(ids[2], out.shape[0]), :]


def fill_rows(ids, out, mine, other, other_two):
    half = mine.shape[0]
    out[at(ids[0], half), :] = mine[...]
    if other.shape[0] == half:
        out[at(1 - ids[0], half), :] = other[...]
        return
    size = half // 2
    out[at((1 - ids[0]) * 2 + ids[2], size), :] = other[...]
    out[at((1 - ids[0]) * 2 + 1 - ids[2], size), :] = other_two[...]


def norm_kernel(ids, mine, other, small, small_other, out, params):
    width = small.shape[1]
    params[:, lanes(ids[0], width)] = small[...].astype(FULL)
    params[:, lanes(1 - ids[0], width)] = small_other[...].astype(FULL)
    half = mine.shape[0]
    for start, part in ((0, mine), (half, other)):
        hat, _ = normal(part[...])
        out[start : start + half, :] = (hat * params[0:1, :] + params[1:2, :]).astype(LOW)


def grid_row(ids, n):
    k, u, i = n // 4, (n // 2) % 2, n % 2
    chunk = ((ids[6] ^ (k >> 1)) ^ (2 * u)) * 4 + ((ids[5] ^ (k & 1)) * 2) + ids[2]
    return chunk * 2 + i


def table_kernel(ids, mine, other, table, spot_one, spot_two):
    part, reach = mine.shape[1:]
    rows = lax.broadcasted_iota(jnp.int32, (reach, LANES), 0)
    cols = lax.broadcasted_iota(jnp.int32, (reach, LANES), 1)
    turn = jnp.where(rows == reach - 1 - cols, 1.0, 0.0).astype(LOW)
    table[...] = jnp.zeros_like(table)
    for k in range(2):
        spot = slice(k * LANES, (k + 1) * LANES)
        table[at(ids[0], part), spot] = dot_nn(mine[k], turn).astype(LOW)
        table[at(1 - ids[0], part), spot] = dot_nn(other[k], turn).astype(LOW)
    side = (reach + 1) // 2
    lane = lane_of(side)
    col = lax.broadcasted_iota(jnp.int32, (side, LANES), 0)
    total = spot_one.shape[0] // side
    for n in range(total):
        row = grid_row(ids, n % (total // 2))
        if n >= total // 2:
            row = row ^ 2
        here = slice(n * side, (n + 1) * side)
        target = jnp.where(lane < 96, row + 64, col + 96)
        one = jnp.where(lane == target, 1.0, 0.0)
        spot_one[here, :] = one.astype(LOW)
        ones = jnp.where((lane >= 64) & (lane < 67), 1.0, 0.0)
        spot_two[here, :] = (pltpu.roll(one, 64, 1) + ones).astype(LOW)


def lane_of(rows):
    return lax.broadcasted_iota(jnp.int32, (rows, LANES), 1)


def pieces_at(lane, first, value, rest):
    high = value.astype(LOW).astype(FULL)
    left = value - high
    mid = left.astype(LOW).astype(FULL)
    tail = left - mid
    out = jnp.where(lane == first, high, rest)
    out = jnp.where(lane == first + 1, mid, out)
    return jnp.where(lane == first + 2, tail, out)


def key_tiles(h, kva, kvb, spot_one, keys):
    half = kva.shape[0]
    lane = lane_of(half)
    for start, part in ((0, kva), (half, kvb)):
        tile = part[:, h * LANES : (h + 1) * LANES].astype(FULL)
        spots = spot_one[start : start + half, :].astype(FULL)
        keys[start : start + half, :LANES] = jnp.where(lane < 64, tile, spots).astype(LOW)


def attend_kernel(
    ids, query, kva, kvb, spot_one, spot_two, table, out, a0, a1, a2, a3, left, keys, turned, along
):
    rows = query.shape[0]
    heads = left.shape[0]
    half = kva.shape[0]
    lane32 = lane_of(32)
    block = 512
    lane = lane_of(block)
    size = a0.shape[0]
    turned[LANES:, :] = spot_two[...].astype(FULL).T.astype(LOW)
    for h in range(heads):
        key_tiles(h, kva, kvb, spot_one, keys)
        turned[:LANES, :] = keys[...].astype(FULL).T.astype(LOW)
        tile = query[:, (h // 2) * LANES : (h // 2 + 1) * LANES].astype(FULL)
        if h % 2:
            tile = pltpu.roll(tile, 64, 1)
        along[...] = dot_nn(tile.astype(LOW), table[...])
        for g in range(rows // 32):
            here = slice(g * 32, (g + 1) * 32)
            term_h = pltpu.roll(along[here, :LANES], 33 + grid_row(ids, g), 1)
            term_w = pltpu.roll(along[here, LANES:], 65, 1, stride=1, stride_axis=0)
            one = jnp.where(
                lane32 < 64, tile[here, :] * 0.125, jnp.where(lane32 < 96, term_h, term_w)
            )
            high = one.astype(LOW)
            rest = pltpu.roll(one - high.astype(FULL), 64, 1)
            left[h, here, :LANES] = high
            left[h, here, LANES:] = rest.astype(LOW)
        cols = slice(h * LANES, (h + 1) * LANES)
        spot = slice((h // 2) * LANES, (h // 2 + 1) * LANES)
        for q in range(rows // block):
            here = slice(q * block, (q + 1) * block)
            scores = dot_nn(left[h, here, :], turned[...])
            top = jnp.max(scores, axis=1, keepdims=True)
            expo = jnp.exp(scores - top)
            total = jnp.sum(expo, axis=1, keepdims=True)
            low = expo.astype(LOW)
            result = dot_nn(low[:, :half], kva[:, cols]) + dot_nn(low[:, half:], kvb[:, cols])
            result = result / total
            if h % 2 == 0:
                result = pltpu.roll(result, 64, 1)
            if h % 2:
                result = jnp.where(lane < 64, out[here, spot], result)
            else:
                result = jnp.where(lane < 64, result, 0.0)
            out[here, spot] = result
            for k in range(block // size):
                low_out = (a0, a1, a2, a3)[q * block // size + k]
                part = result[k * size : (k + 1) * size, :].astype(LOW)
                if h % 2:
                    low_out[:, spot] = part
                elif h == heads - 1:
                    low_out[:, h * 64 :] = part[:, :64]
            rest = left[h, here, LANES:].astype(FULL)
            left[h, here, LANES:] = pieces_at(lane, 64, -(top + jnp.log(total)), rest).astype(LOW)


def back_kernel(h):
    def kernel(
        ids, left, kva, kvb, spot_one, spot_two, table, g0, g1, g2, g3, value,
        dquery, dkv_mine, dkv_other, dtable,
        keys, vals, gright, qright, along, grad, left_t, right_t,
    ):
        rows = left.shape[1]
        half = kva.shape[0]
        lane = lane_of(rows)
        lane32 = lane_of(32)
        row = lax.broadcasted_iota(jnp.int32, (rows, LANES), 0)
        key_tiles(h, kva, kvb, spot_one, keys)
        keys[:, LANES:] = spot_two[...]
        cols = slice(h * LANES, (h + 1) * LANES)
        spot = slice((h // 2) * LANES, (h // 2 + 1) * LANES)
        for k, part in enumerate((g0, g1, g2, g3)):
            size, width = part.shape
            last = min(width, spot.stop)
            grad[k * size : (k + 1) * size, : last - spot.start] = part[:, spot.start : last].astype(FULL)
        vals[:half, :LANES] = kva[:, cols]
        vals[half:, :LANES] = kvb[:, cols]
        vals[:, LANES:] = spot_two[...]
        gtile = grad[...]
        otile = value[:, spot]
        if h % 2 == 0:
            gtile = pltpu.roll(gtile, 64, 1)
            otile = pltpu.roll(otile, 64, 1)
        gtile = jnp.where(lane >= 64, gtile, 0.0)
        inner = jnp.sum(gtile * otile, axis=1, keepdims=True)
        gright[...] = gtile.astype(LOW)
        extra = pieces_at(lane, 64, -inner, jnp.zeros_like(gtile))
        right_t[:LANES, :] = gtile.T.astype(LOW)
        right_t[LANES:, :] = extra.T.astype(LOW)
        for part in (slice(0, LANES), slice(LANES, 2 * LANES)):
            left_t[part, :] = left[h, :, part].astype(FULL).T.astype(LOW)
        qright[...] = jnp.where(lane < 64, left[h, :, :LANES].astype(FULL), 0.0).astype(LOW)
        probs = jnp.exp(dot_nn(keys[...], left_t[...]))
        dscores = (probs * dot_nn(vals[...], right_t[...])).astype(LOW)
        dkv = dot_nn(probs.astype(LOW), gright[...]) + dot_nn(dscores, qright[...])
        dkv_mine[...] = dkv[:half, :]
        dkv_other[...] = dkv[half:, :].astype(LOW)
        dq = dot_tn(keys[:, :LANES], dscores).T
        for g in range(rows // 32):
            here = slice(g * 32, (g + 1) * 32)
            part_h = jnp.where((lane32 >= 64) & (lane32 < 96), dq[here, :], 0.0)
            along[here, :LANES] = pltpu.roll(part_h, 95 - grid_row(ids, g), 1).astype(LOW)
        part_w = pltpu.roll(jnp.where(lane >= 96, dq, 0.0), 63, 1)
        for bit in range(5):
            moved = pltpu.roll(part_w, LANES - 2**bit, 1)
            part_w = jnp.where((row >> bit) & 1 == 1, moved, part_w)
        along[:, LANES:] = part_w.astype(LOW)
        dq = jnp.where(lane < 64, dq * 0.125 + dot_nt(along[...], table[...]), 0.0)
        if h % 2:
            dq = pltpu.roll(dq, 64, 1)
        dquery[...] = dq.astype(LOW)
        dtable[...] = dot_tn(along[...], qright[...])

    return kernel


def at(index, size):
    return pl.ds(pl.multiple_of(index * size, 16), size)


def lanes(index, size):
    return pl.ds(pl.multiple_of(index * size, LANES), size)


def mix_kernel(ids, n0, n1, n2, n3, mine, other, kv, query, rows, mix):
    half, last = mine.shape
    kv_cols = kv.shape[1]
    mix[at(ids[0], half), :last] = mine[...]
    mix[at(1 - ids[0], half), :last] = other[...]
    mix[:, last:] = jnp.zeros((mix.shape[0], mix.shape[1] - last), LOW)
    size = n0.shape[0]
    for k, part in enumerate((n0, n1, n2, n3)):
        here = slice(k * size, (k + 1) * size)
        rows[here, :] = part[...]
    both = dot_nn(rows[...], mix[...]).astype(LOW)
    kv[...] = both[:, :kv_cols]
    query[...] = both[:, kv_cols:]


def mid_kernel(
    ids, j0, j1, j2, j3, w_mine, w_other, w_two, own, own_got, params, middle, low, weight, whole
):
    fill_rows(ids, whole, w_mine, w_other, w_two)
    tok = own.shape[0]
    middle[:tok, :] = own[...]
    middle[tok:, :] = own_got[...]
    total = middle[...]
    width = j0.shape[1]
    for k, part in enumerate((j0, j1, j2, j3)):
        block = whole[at(ids[1] ^ k, width), :]
        weight[k * width : (k + 1) * width, :] = block
        total = total + dot_nn(part[...], block)
    middle[...] = total
    hat, _ = normal(total)
    low[...] = (hat * params[2:3, :] + params[3:4, :]).astype(LOW)


def feed_kernel(
    ids, r0, r1, r2, r3, c0, c1, c2, c3, up_mine, up_other, down_mine, down_other,
    d0, d1, d2, d3, active, dhidden, rows, cots, down, up,
):
    half = up_mine.shape[0]
    up[at(ids[0], half), :] = up_mine[...]
    up[at(1 - ids[0], half), :] = up_other[...]
    down[:, lanes(ids[0], half)] = down_mine[...]
    down[:, lanes(1 - ids[0], half)] = down_other[...]
    size = r0.shape[0]
    blocks = ((r0, c0, d0), (r1, c1, d1), (r2, c2, d2), (r3, c3, d3))
    for k, (row, cot, _) in enumerate(blocks):
        here = slice(k * size, (k + 1) * size)
        rows[here, :] = row[...]
        cots[here, :] = cot[...]
    hidden = dot_nn(rows[...], up[...])
    phi = 0.5 + 0.5 * lax.erf(hidden * 0.7071067811865476)
    active[...] = (hidden * phi).astype(LOW)
    slope = phi + hidden * (jnp.exp(hidden * hidden * -0.5) * 0.3989422804014327)
    dhidden[...] = (dot_nt(cots[...], down[...]) * slope).astype(LOW)
    back = dot_nt(dhidden[...], up[...]).astype(LOW)
    for k, (_, _, out) in enumerate(blocks):
        out[...] = back[k * size : (k + 1) * size, :]


def fed_kernel(active, down, f0, f1, f2):
    size = f0.shape[0]
    total = dot_nn(active[...], down[...]).astype(LOW)
    f0[...] = total[:size, :]
    f1[...] = total[size : 2 * size, :]
    f2[...] = total[2 * size :, :]


def outer_kernel(which, axis):
    def kernel(ids, a, b, sent, kept):
        half = sent.shape[axis]
        for index, out in ((1 - ids[which], sent), (ids[which], kept)):
            if axis == 0:
                out[...] = dot_tn(a[:, lanes(index, half)], b[...]).astype(LOW)
            else:
                out[...] = dot_tn(a[...], b[:, lanes(index, half)]).astype(LOW)

    return kernel


def proj_grad_kernel(ids, j0, j1, j2, j3, grad, sent, kept, whole):
    width = j0.shape[1]
    for k, part in enumerate((j0, j1, j2, j3)):
        whole[at(ids[1] ^ k, width), :] = dot_tn(part[...], grad[...])
    size = sent.shape[0] // 2
    for k, owner in enumerate((ids[0], 1 - ids[0])):
        here = slice(k * size, (k + 1) * size)
        sent[here, :] = whole[at(owner * 2 + 1 - ids[2], size), :].astype(LOW)
        kept[here, :] = whole[at(owner * 2 + ids[2], size), :].astype(LOW)


def split_kernel(which):
    def kernel(ids, a, b, sent, kept):
        size = sent.shape[0] // 2
        for k in range(2):
            here = slice(k * size, (k + 1) * size)
            for bit, out in ((1 - ids[which], sent), (ids[which], kept)):
                rows = pl.ds(pl.multiple_of(k * 2 * size + bit * size, 16), size)
                out[here, :] = (a[rows, :].astype(FULL) + b[rows, :].astype(FULL)).astype(LOW)

    return kernel


def owner_kernel(a, b, sent, kept):
    size = sent.shape[0]
    kept[...] = (a[:size, :].astype(FULL) + b[:size, :].astype(FULL)).astype(kept.dtype)
    sent[...] = (a[size:, :].astype(FULL) + b[size:, :].astype(FULL)).astype(LOW)


def tail_add_kernel(a, b, out):
    size = a.shape[0]
    out[...] = (a[...].astype(FULL) + b[b.shape[0] - size :, :].astype(FULL)).astype(out.dtype)


def vector_block(out, n0, n1, n2, n3, t0, t1, t2):
    out[...] = jnp.zeros_like(out)
    tables = (t0[...] + t1[...] + t2[...]) * 8.0
    side = 16
    for k in range(8):
        start = k // 4 * LANES + k % 4 * side
        out[:side, k * 64 : (k + 1) * 64] = tables[start : start + side, :64]
    tile = 0
    for row in (n0, n1, n2, n3):
        for k in range(row.shape[1] // LANES):
            spot = slice(tile % 4 * LANES, (tile % 4 + 1) * LANES)
            out[side + tile // 4 : side + tile // 4 + 1, spot] = row[:, k * LANES : (k + 1) * LANES]
            tile += 1


def row_sums(product):
    total = product[:, :LANES]
    for k in range(1, product.shape[1] // LANES):
        total = total + product[:, k * LANES : (k + 1) * LANES]
    return jnp.sum(total.T, axis=0, keepdims=True)


def vector_out_kernel(reach, split):
    def kernel(ids, *refs):
        *parts, params, n0, n1, n2, n3, t0, t1, total, norms = refs
        first = parts[0].shape[0] - total.shape[0]
        total[...] = sum(part[first:, :].astype(FULL) for part in parts)
        side = 16
        for tile in range(norms.shape[0] * norms.shape[1] // LANES):
            each = norms.shape[1] // LANES
            spot = slice(tile % 4 * LANES, (tile % 4 + 1) * LANES)
            norms[tile // each : tile // each + 1, tile % each * LANES : (tile % each + 1) * LANES] = (
                total[side + tile // 4 : side + tile // 4 + 1, spot]
            )
        gain, shift = params[0:1, :], params[1:2, :]
        norms[0:1, :] = (norms[0:1, :] - shift * norms[1:2, :]) / gain
        for k, out in enumerate((n0, n1, n2, n3)):
            width = out.shape[0]
            start = ids[7] * width if split else 0
            for tile in range(width // LANES):
                spot = pl.ds(pl.multiple_of(start + tile * LANES, LANES), LANES)
                out[tile * LANES : (tile + 1) * LANES] = norms[k, spot]
        rows = lax.broadcasted_iota(jnp.int32, (side, reach), 0)
        cols = lax.broadcasted_iota(jnp.int32, (side, reach), 1)
        for k, out in enumerate((t0, t1)):
            both = jnp.zeros((64, reach), FULL)
            for part in range(4):
                turn = jnp.where(rows + part * side == reach - 1 - cols, 1.0, 0.0)
                start = (k * 4 + part) * 64
                both = both + lax.dot_general(
                    total[:side, start : start + 64],
                    turn,
                    (((0,), (0,)), ((), ())),
                    precision=lax.Precision.HIGHEST,
                    preferred_element_type=FULL,
                )
            if split:
                size = out.shape[0]
                out[...] = jnp.where(ids[7] == 0, both[:size, :], both[size:, :])
            else:
                out[...] = both

    return kernel


def dmix_kernel(dkv, dquery, mix, mine, near, sent):
    size = mine.shape[0]
    cols = dkv.shape[1]
    total = dot_nt(dkv[...], mix[:, :cols]) + dot_nt(dquery[...], mix[:, cols:])
    for k, (out, start) in enumerate(((mine, 0), (sent, 0), (near, 0), (sent, size))):
        out[start : start + size, :] = total[k * size : (k + 1) * size, :].astype(LOW)


def dkv_kernel(m0, m1, m2, o0, o1, o2, q0, q1, q2, dkv, dquery):
    for h, (mine, got) in enumerate(((m0, o0), (m1, o1), (m2, o2))):
        cols = slice(h * LANES, (h + 1) * LANES)
        dkv[:, cols] = (mine[...] + got[...].astype(FULL)).astype(LOW)
    dquery[:, :LANES] = (q0[...].astype(FULL) + q1[...].astype(FULL)).astype(LOW)
    dquery[:, LANES:] = q2[...]


def qkv_grad_kernel(
    ids, rows, m0, m1, m2, o0, o1, o2, q0, q1, q2, mix, v2, v3, t0, t1, t2,
    dkv, dquery, sent, kept, whole, vector,
):
    dkv_kernel(m0, m1, m2, o0, o1, o2, q0, q1, q2, dkv, dquery)
    cols = dkv.shape[1]
    whole[:, :cols] = dot_tn(rows[...], dkv[...])
    whole[:, cols:] = dot_tn(rows[...], dquery[...])
    width = kept.shape[1]
    size = (kept.shape[0] - vector.shape[0]) // 2
    sums_block(whole, dkv, dquery, mix, v2, v3, t0, t1, t2, vector)
    for out, core in ((sent, 1 - ids[2]), (kept, ids[2])):
        for k, owner in enumerate((ids[0], 1 - ids[0])):
            here = slice(k * size, (k + 1) * size)
            out[here, :] = whole[at(owner * 2 + core, size), :width].astype(LOW)
        out[2 * size :, :] = vector[...].astype(LOW)


def sums_block(whole, dkv, dquery, mix, v2, v3, t0, t1, t2, vector):
    weights = mix[...].astype(FULL)
    sums = jnp.concatenate(
        [jnp.sum(part[...].astype(FULL), axis=0, keepdims=True) for part in (dkv, dquery)], axis=1
    )
    both = row_sums(whole[...] * weights)
    shift = row_sums(weights * sums)
    vector_block(vector, both, shift, v2, v3, t0, t1, t2)


def sums_kernel(rows, dkv, dquery, mix, v2, v3, t0, t1, t2, vector, whole):
    cols = dkv.shape[1]
    whole[:, :cols] = dot_tn(rows[...], dkv[...])
    whole[:, cols:] = dot_tn(rows[...], dquery[...])
    sums_block(whole, dkv, dquery, mix, v2, v3, t0, t1, t2, vector)


def qkv_owner_kernel(a, b, sent, kept):
    size = a.shape[0] - sent.shape[0]
    kept[:size, :] = a[:size, :].astype(FULL) + b[:size, :].astype(FULL)
    total = a[size:, :].astype(FULL) + b[size:, :].astype(FULL)
    kept[size:, :] = total[size:, :]
    sent[...] = total.astype(LOW)


def add_kernel(*refs):
    total = refs[0][...].astype(FULL)
    for ref in refs[1:-1]:
        total = total + ref[...].astype(FULL)
    refs[-1][...] = total.astype(refs[-1].dtype)


def halve_kernel(which):
    def kernel(ids, a, b, sent, kept):
        size = sent.shape[0]
        bit = ids[which]
        for index, out in ((1 - bit, sent), (bit, kept)):
            here = at(index, size)
            out[...] = (a[here, :].astype(FULL) + b[here, :].astype(FULL)).astype(out.dtype)

    return kernel


def join_kernel(which):
    def kernel(ids, mine, other, out):
        size = mine.shape[0]
        out[at(ids[which], size), :] = mine[...].astype(out.dtype)
        out[at(1 - ids[which], size), :] = other[...].astype(out.dtype)

    return kernel


def qkv_out(heads, ids, mine, others, out, whole, sem, copies):
    size = out.shape[0] // 2
    lane = lane_of(size)
    first = lane < 64
    groups = 4
    share = heads * 64
    width = groups * share

    def fill(here, refs):
        def tile(g, column):
            stop = min(column + LANES, refs[g].shape[1])
            one = refs[g][:size, column:stop].astype(FULL)
            if stop - column < LANES:
                one = jnp.concatenate([one, jnp.zeros_like(one)], axis=1)
            return one

        for pair in range(groups * heads // 2):
            ends = []
            for n in (2 * pair, 2 * pair + 1):
                g, h = n // heads, n % heads
                q = tile(g, 2 * share + (h // 2) * LANES)
                if h % 2:
                    q = pltpu.roll(q, 64, 1)
                ends.append((q, tile(g, h * LANES)))
            (qa, kva), (qb, kvb) = ends
            at_col = pair * LANES
            for begin, a, b in (
                (0, qa, pltpu.roll(qb, 64, 1)),
                (width, kva, pltpu.roll(kvb, 64, 1)),
                (2 * width, pltpu.roll(kva, 64, 1), kvb),
            ):
                cols = slice(begin + at_col, begin + at_col + LANES)
                whole[here, cols] = jnp.where(first, a, b)

    for place, refs in ((ids[2], mine), (1 - ids[2], others)):
        here = pl.ds(pl.multiple_of(place * size, 16), size)
        for g in range(groups):

            @pl.when(ids[1] == g)
            def _():
                fill(here, [refs[k ^ g] for k in range(groups)])

        start(whole.at[here], out.at[here], sem, copies)


def halve_lanes_kernel(which):
    def kernel(ids, a, b, sent, kept):
        size = sent.shape[1]
        for bit, out in ((1 - ids[which], sent), (ids[which], kept)):
            here = lanes(bit, size)
            out[...] = (a[:, here].astype(FULL) + b[:, here].astype(FULL)).astype(out.dtype)

    return kernel


def start(source, target, sem, copies):
    copies.append(pltpu.make_async_copy(source, target, sem.at[len(copies)]))
    copies[-1].start()


def place_out(ids, mine, other, out, sem, copies):
    start(mine, out.at[ids[3]], sem, copies)
    start(other, out.at[1 - ids[3]], sem, copies)


def join_out(ids, which, mine, other, out, whole, sem, copies):
    size = mine.shape[0]
    for place, ref in ((ids[which], mine), (1 - ids[which], other)):
        here = at(place, size)
        whole[here, :] = ref[...].astype(FULL)
        start(whole.at[here], out.at[here], sem, copies)


def place_kernel(ids, token, change, got, away, output, tokens_grad, low, sem):
    copies = []
    tok = token.shape[0]
    low[:tok, :] = got[:tok, :].astype(FULL)
    place_out(ids, token, low.at[:tok], tokens_grad, sem, copies)
    low[tok:, :] = got[tok:, :].astype(FULL) + away[...]
    place_out(ids, change, low.at[tok:], output, sem, copies)
    for copy in copies:
        copy.wait()


def last_kernel(heads):
    def kernel(
        ids, q0, q1, q2, q3, o0, o1, o2, o3, token, change, got, away,
        proj, proj_got, first, first_got, second, second_got,
        output, tokens_grad, qkv_grad, proj_grad, fc1_grad, fc2_grad,
        low, qkv, wide, one, two, sem,
    ):
        copies = []
        tok = token.shape[0]
        low[:tok, :] = got[:tok, :].astype(FULL)
        place_out(ids, token, low.at[:tok], tokens_grad, sem, copies)
        low[tok:, :] = got[tok:, :].astype(FULL) + away[...]
        place_out(ids, change, low.at[tok:], output, sem, copies)
        join_out(ids, 2, proj, proj_got, proj_grad, wide, sem, copies)
        join_out(ids, 4, first, first_got, fc1_grad, one, sem, copies)
        join_out(ids, 4, second, second_got, fc2_grad, two, sem, copies)
        qkv_out(heads, ids, (q0, q1, q2, q3), (o0, o1, o2, o3), qkv_grad, qkv, sem, copies)
        for copy in copies:
            copy.wait()

    return kernel


def norm_back(grad, values, gain):
    hat, scale = normal(values)
    scaled = grad * gain
    back = scale * (
        scaled
        - jnp.mean(scaled, axis=-1, keepdims=True)
        - hat * jnp.mean(scaled * hat, axis=-1, keepdims=True)
    )
    return back, jnp.sum(grad * hat, axis=0, keepdims=True), jnp.sum(grad, axis=0, keepdims=True)


def mid_back_kernel(
    a0, a1, a2, middle, params, cot, weight, gmiddle, gbranch, b0, b1, b2, b3, dgain, dshift
):
    size = a0.shape[0]
    grad = a0[...].astype(FULL) + a1[...].astype(FULL) + a2[...].astype(FULL)
    back, dgain[...], dshift[...] = norm_back(grad, middle[...], params[2:3, :])
    total = cot[:size, :].astype(FULL) + back
    gmiddle[...] = total
    low = total.astype(LOW)
    gbranch[...] = low
    width = b0.shape[1]
    for k, out in enumerate((b0, b1, b2, b3)):
        out[...] = dot_nt(low, weight[k * width : (k + 1) * width, :]).astype(LOW)


def first_back_kernel(
    a0, a1, a2, own, own_got, params, gmiddle, middle, f0, f1, f2, mine, change, sent, rows
):
    tok = own.shape[0]
    fed = f0[...].astype(FULL) + f1[: 2 * tok, :].astype(FULL) + f2[...].astype(FULL)
    total = middle[...] + fed
    change[...] = total[:tok, :]
    sent[tok:, :] = (total[tok:, :] - own_got[...]).astype(LOW)
    rows[:tok, :] = own[...]
    rows[tok:, :] = own_got[...]
    grad = a0[...].astype(FULL) + a1[: 2 * tok, :].astype(FULL) + a2[...].astype(FULL)
    back, _, _ = norm_back(grad, rows[...], params[0:1, :])
    total = gmiddle[...] + back
    mine[...] = total[:tok, :]
    sent[:tok, :] = total[tok:, :].astype(LOW)


def on_device(
    tokens,
    ln1_gain,
    ln1_bias,
    qkv_weight,
    rel_h,
    rel_w,
    proj_weight,
    ln2_gain,
    ln2_bias,
    fc1_weight,
    fc2_weight,
    cotangent,
):
    images, tok, width = tokens.shape
    hid = fc1_weight.shape[1]
    dp_count = lax.axis_size("dp")
    head = rel_h.shape[1] * dp_count
    reach = rel_h.shape[0]
    s, t = lax.axis_index("seq"), lax.axis_index("tp")
    d = lax.axis_index("dp")
    y, c = t // 2, t % 2
    image = s // 2
    group = (s % 2) * 2 + y
    groups = 4
    share = width // groups
    heads = share // head
    rows_n = 2 * tok
    half = width // 2
    me = d if dp_count == 2 else jnp.int32(0)
    ids = jnp.stack([me, group, c, image, s % 2, y, s, d]).astype(jnp.int32)
    n = 4 * rows_n
    kv_cols = 2 * share
    pad_share = 2 * LANES
    key_n = 2 * n
    qkv_cols = 3 * share
    low_tok, full_tok = shape((tok, width), LOW), shape((tok, width), FULL)
    low_rows, full_rows = shape((rows_n, width), LOW), shape((rows_n, width), FULL)
    two_rows = shape((2 * rows_n, width), LOW)
    heads_rows = shape((rows_n, share), LOW)
    way = (0, ROW, NEAR, ROW | NEAR)

    def add(kind, *args, wait=()):
        return call(add_kernel, [shape(args[0].shape, kind)], wait=wait)(*args)[0]

    call = in_order()
    quarter, eighth = half // 2, half // 4
    norm_sums = [shape((1, width), FULL)] * 2

    def total_of(kind, *args):
        return call(add_kernel, [shape(args[0].shape, kind)])(*args)[0]

    def halve(which, a, b, kind=FULL):
        dims = (a.shape[0] // 2, a.shape[1])
        return call(halve_kernel(which), [shape(dims, LOW), shape(dims, kind)], smem=1)(ids, a, b)

    def split(which, a, b):
        dims = (a.shape[0] // 2, a.shape[1])
        return call(split_kernel(which), [shape(dims, LOW)] * 2, smem=1)(ids, a, b)

    def join(which, mine, other, kind):
        dims = (2 * mine.shape[0], mine.shape[1])
        return call(join_kernel(which), [shape(dims, kind)], smem=1)(ids, mine, other)[0]

    own, away = call(pick_kernel, [full_tok] * 2, smem=1)(ids, tokens)
    own_got = hop(away, FAR)
    small = jnp.concatenate([ln1_gain, ln1_bias, ln2_gain, ln2_bias]).reshape(4, -1)
    small, small_other, _ = pair_dp(after(small, away), 1)
    tables = jnp.stack([rel_h.T, rel_w.T])
    tables, tables_other, _ = pair_dp(after(tables, away), 1)
    cot_mine, cot_away = call(pick_kernel, [low_tok] * 2, smem=1)(ids, cotangent)
    cot_got = hop(cot_away, FAR)
    depth = qkv_weight.shape[0]
    mix_mine = call(
        pack_kernel(share, heads),
        [shape((depth, qkv_cols), LOW)],
        smem=1,
        wait=(small_other, tables_other),
    )(ids, qkv_weight)[0]
    mix_mine, mix_other, _ = pair_dp(after(mix_mine, own_got), 0)

    normed, params = call(norm_kernel, [low_rows, shape((4, width), FULL)], smem=1)(
        ids, own, own_got, small, small_other
    )
    normed_parts = [normed] + [hop(normed, b) for b in way[1:]]
    cot = call(stack_kernel, [low_rows])(cot_mine, cot_got)[0]
    if dp_count == 2:
        proj_part = call(rows_kernel, [shape((half // 2, width), LOW)], smem=1)(ids, proj_weight)[0]
    table, spot_one, spot_two = call(
        table_kernel,
        [shape((LANES, 2 * LANES), LOW)] + [shape((key_n, LANES), LOW)] * 2,
        smem=1,
        wait=(mix_other,),
    )(ids, tables, tables_other)

    kv, query, normed_all, mix = call(
        mix_kernel,
        [
            shape((n, kv_cols), LOW),
            shape((n, pad_share), LOW),
            shape((n, width), LOW),
            shape((width, kv_cols + pad_share), LOW),
        ],
        smem=1,
        extra=3,
    )(ids, *normed_parts, mix_mine, mix_other)
    kv_other = hop(kv, CORE)
    cot_row = hop(after(cot, kv), ROW)
    if dp_count == 2:
        proj_mine, proj_other = proj_weight, swap_dp(after(proj_part, normed))
    else:
        proj_mine, proj_other, _ = pair_dp(proj_weight, 0)
    proj_two = hop(after(proj_other, kv), CORE)
    up_mine, up_other, _ = pair_dp(after(fc1_weight, normed), 0)

    down_mine, down_other, _ = pair_dp(after(fc2_weight, kv), 1)

    attended, *attended_low, left = call(
        attend_kernel,
        [shape((n, pad_share), FULL)]
        + [heads_rows] * 4
        + [shape((heads, n, 2 * LANES), LOW)],
        [
            pltpu.VMEM((key_n, LANES), LOW),
            pltpu.VMEM((2 * LANES, key_n), LOW),
            pltpu.VMEM((n, 2 * LANES), FULL),
        ],
        smem=1,
        extra=16,
    )(ids, query, kv, kv_other, spot_one, spot_two, table)
    attended_low = lax.optimization_barrier((*attended_low, cot_row, proj_two))[:4]
    joined = [attended_low[0]] + [hop(attended_low[k], way[k]) for k in (1, 2, 3)]
    middle, normed_two, proj = call(
        mid_kernel,
        [full_rows, low_rows, shape((width, width), LOW)],
        [pltpu.VMEM((width, width), LOW)],
        smem=1,
        wait=(up_other,),
    )(ids, *joined, proj_mine, proj_other, proj_two, own, own_got, params)

    two_row = hop(normed_two, ROW)
    two_core = hop(normed_two, CORE)
    two_diag = hop(two_row, CORE)
    cot_core = hop(after(cot, two_row), CORE)
    cot_diag = hop(after(cot_row, two_row), CORE)
    d0, d1, d2, d3, active, dhidden, rows_all, cot_all, down = call(
        feed_kernel,
        [low_rows] * 4
        + [shape((n, hid), LOW)] * 2
        + [shape((n, width), LOW)] * 2
        + [shape((hid, width), LOW)],
        [pltpu.VMEM((width, hid), LOW)],
        smem=1,
        extra=12,
    )(
        ids, normed_two, two_row, two_core, two_diag, cot, cot_row, cot_core, cot_diag,
        up_mine, up_other, down_mine, down_other,
    )
    dnorm_next = hop(d3, CORE)
    dnorm_mine = hop(d2, CORE)

    mixed_shapes = [shape((n, kv_cols), LOW), shape((n, pad_share), LOW)]
    vector_rows = 32
    whole_shape = pltpu.VMEM((width, kv_cols + pad_share), FULL)
    qkv_rows = (quarter + vector_rows, qkv_cols)
    proj_low = shape((eighth, width), LOW)
    v, fc1, fc2 = (types.SimpleNamespace() for _ in range(3))

    def send(value, bits, *events):
        return hop(after(value, *events) if events else value, bits)

    def dnorm_add():
        v.dnorm_row = send(total_of(LOW, d1, dnorm_next), ROW)

    def fc1_outer():
        sent, fc1.kept = call(outer_kernel(0, 0), [shape((half, hid), LOW)] * 2, smem=1, extra=4)(
            ids, rows_all, dhidden
        )
        if dp_count == 2:
            fc1.got = swap_dp(sent)

    def far_sum(part):
        def step():
            sent, part.kept = halve(3, part.kept, part.got)
            part.got = send(sent, FAR)

        return step

    def far_all(part):
        def step():
            part.kept = total_of(LOW, part.kept, part.got)
            part.got = send(part.kept, FAR)

        return step

    def near_all(part):
        def step():
            part.kept = join(3, part.kept, part.got, LOW)
            part.got = send(part.kept, NEAR)

        return step

    def fc2_outer():
        sent, fc2.kept = call(
            outer_kernel(4, 0), [shape((hid // 2, width), LOW)] * 2, smem=1, extra=4
        )(ids, active, cot_all)
        fc2.got = send(sent, NEAR)

    def mid_back():
        v.gmiddle, v.gbranch, *parts, v.dgain_two, v.dshift_two = call(
            mid_back_kernel, [full_rows, low_rows] + [heads_rows] * 4 + norm_sums
        )(d0, dnorm_mine, v.dnorm_row, middle, params, cot, proj)
        v.grads = [parts[0]] + [
            send(b, bits) for b, bits in zip(parts[1:], way[1:])
        ]

    def proj_outer():
        sent, v.proj = call(
            proj_grad_kernel,
            [shape((half, width), LOW)] * 2,
            [pltpu.VMEM((width, width), FULL)],
            smem=1,
        )(ids, *joined, v.gbranch)
        v.proj_got = send(after(sent, *v.grads), CORE)

    def fed():
        v.f0, v.f1, f2 = call(fed_kernel, [low_rows, low_rows, two_rows], extra=4)(
            active, down
        )
        v.fed_got = send(after(f2, *v.grads), CORE)

    def back(h):
        dquery, mine, other, dtable = call(
            back_kernel(h),
            [
                shape((n, LANES), LOW),
                shape((n, LANES), FULL),
                shape((n, LANES), LOW),
                shape((2 * LANES, LANES), FULL),
            ],
            [
                pltpu.VMEM((key_n, 2 * LANES), LOW),
                pltpu.VMEM((key_n, 2 * LANES), LOW),
                pltpu.VMEM((n, LANES), LOW),
                pltpu.VMEM((n, LANES), LOW),
                pltpu.VMEM((n, 2 * LANES), LOW),
                pltpu.VMEM((n, LANES), FULL),
                pltpu.VMEM((2 * LANES, n), LOW),
                pltpu.VMEM((2 * LANES, n), LOW),
            ],
            smem=1,
            extra=20,
            wait=(v.back[-1][1],) if v.back else (),
        )(ids, left, kv, kv_other, spot_one, spot_two, table, *v.grads, attended)
        v.back.append((mine, send(other, CORE), dquery, dtable))

    v.back = []

    def back0():
        back(0)

    def back1():
        back(1)

    def back2():
        back(2)

    def fed_add():
        sent = call(tail_add_kernel, [low_rows])(v.f1, v.fed_got)[0]
        v.fed_row = send(sent, ROW)

    def last():
        dims = [tokens.shape] * 2 + [(half, 3 * width), (half, width), (half, hid), (hid, half)]
        (
            v.output, v.tokens_grad, v.qkv_grad, v.proj_grad, fc1.grad, fc2.grad,
        ) = call(
            last_kernel(heads),
            [shape(d, FULL) for d in dims],
            [pltpu.VMEM((rows_n, width), FULL)]
            + [pltpu.VMEM(d, FULL) for d in dims[2:]]
            + [pltpu.SemaphoreType.DMA((12,))],
            smem=1,
            extra=8,
            written=6,
        )(
            ids, *v.qkv_parts, *v.qkv_others, v.token, v.change, v.token_got, away,
            v.proj, v.proj_got, fc1.kept, fc1.got, fc2.kept, fc2.got,
        )

    def qkv_outer():
        mine, got, queries, tables = zip(*v.back)
        v.dkv, v.dquery, sent, v.qkv = call(
            qkv_grad_kernel,
            mixed_shapes + [shape((half + vector_rows, qkv_cols), LOW)] * 2,
            [whole_shape, pltpu.VMEM((vector_rows, qkv_cols), FULL)],
            smem=1,
            extra=6,
        )(
            ids, normed_all, *mine, *got, *queries, mix, v.dgain_two, v.dshift_two, *tables
        )
        v.qkv_got = send(sent, CORE)

    def qkv_owner():
        sent, v.qkv = call(qkv_owner_kernel, [shape(qkv_rows, LOW), shape(qkv_rows, FULL)])(
            v.qkv, v.qkv_got
        )
        v.qkv_got = swap_dp(sent)

    def qkv_images():
        v.qkv = total_of(LOW, v.qkv, v.qkv_got)
        v.qkv_got = send(v.qkv, FAR)

    def qkv_total():
        part = total_of(LOW, v.qkv, v.qkv_got)
        near = send(part, NEAR)
        v.qkv_parts = [part, send(part, ROW), near, send(near, ROW)]

    def vector_last():
        *norms, table_h, table_w = vector_out(v.qkv_parts, half, head // 2)
        v.norms = norms
        v.tables = (table_h.T, table_w.T)
        v.qkv_others = [send(part, CORE) for part in v.qkv_parts]

    def mixed_back():
        v.e_mine, v.e_near, e_row = call(
            dmix_kernel, [low_rows, low_rows, two_rows], extra=6
        )(
            v.dkv, v.dquery, mix
        )
        v.e_got = send(e_row, ROW)

    def normed_near():
        sent = call(tail_add_kernel, [low_rows])(v.e_near, v.e_got)[0]
        v.e_last = send(sent, NEAR)

    def first_back():
        v.token, v.change, sent = call(
            first_back_kernel, [full_tok, full_tok, low_rows], [pltpu.VMEM((rows_n, width), FULL)]
        )(
            v.e_mine, v.e_got, v.e_last, own, own_got, params, v.gmiddle,
            middle, v.f0, v.fed_got, v.fed_row,
        )
        v.token_got = send(sent, FAR)

    def fc1_near_sum():
        sent, fc1.kept = halve(4, fc1.kept, fc1.got)
        fc1.got = send(sent, NEAR)

    def fc2_near_sum():
        dims = (hid // 2, half)
        sent, fc2.kept = call(
            halve_lanes_kernel(0), [shape(dims, LOW), shape(dims, FULL)], smem=1
        )(ids, fc2.kept, fc2.got)
        fc2.got = swap_dp(sent)

    def proj_split():
        sent, v.proj = split(5, v.proj, v.proj_got)
        v.proj_got = send(sent, ROW)

    def proj_owner():
        sent, v.proj = call(owner_kernel, [proj_low] * 2)(v.proj, v.proj_got)
        v.proj_got = swap_dp(sent)

    def proj_sum(bits):
        def step():
            v.proj = total_of(LOW, v.proj, v.proj_got)
            v.proj_got = send(v.proj, bits)

        return step

    def proj_join():
        v.proj = join(5, v.proj, v.proj_got, LOW)
        v.proj_got = send(v.proj, CORE)

    def vector_out(parts, size, features):
        return call(
            vector_out_kernel(reach, dp_count == 2),
            [shape((size,), FULL)] * 4 + [shape((features, reach), FULL)] * 2,
            [pltpu.VMEM((vector_rows, qkv_cols), FULL), pltpu.VMEM((4, width), FULL)],
            smem=1,
            mark=True,
        )(ids, *parts, params)

    if dp_count == 2:
        for step in (
            fc2_outer,
            dnorm_add,
            fc1_outer,
            mid_back,
            fc2_near_sum,
            proj_outer,
            back0,
            fc1_near_sum,
            back1,
            proj_split,
            back2,
            far_sum(fc1),
            qkv_outer,
            fed,
            qkv_owner,
            mixed_back,
            proj_owner,
            qkv_images,
            far_all(fc1),
            far_sum(fc2),
            fed_add,
            proj_sum(NEAR),
            qkv_total,
            far_all(fc2),
            normed_near,
            near_all(fc1),
            proj_sum(FAR),
            near_all(fc2),
            first_back,
            proj_sum(ROW),
            vector_last,
            proj_join,
            last,
        ):
            step()
        output, tokens_grad, qkv_grad = v.output, v.tokens_grad, v.qkv_grad
        proj_grad, fc1_grad, fc2_grad = v.proj_grad, fc1.grad, fc2.grad
        norms, dtables = v.norms, v.tables
    else:
        every = ("seq", "tp")
        for step in (dnorm_add, mid_back, fed, back0, back1, back2, fed_add):
            step()
        mine, other, queries, tables = zip(*v.back)
        v.dkv, v.dquery = call(dkv_kernel, mixed_shapes)(*mine, *other, *queries)
        for step in (mixed_back, normed_near, first_back):
            step()
        output, tokens_grad = call(
            place_kernel,
            [shape(tokens.shape, FULL)] * 2,
            [pltpu.VMEM((rows_n, width), FULL), pltpu.SemaphoreType.DMA((4,))],
            smem=1,
            written=2,
        )(ids, v.token, v.change, v.token_got, away)
        dkv, dquery, gbranch = v.dkv, v.dquery, v.gbranch

        def weight_sum(a, b, axes, axis=0):
            part = lax.psum_scatter(
                dot_tn(a, b).astype(LOW), "dp", scatter_dimension=axis, tiled=True
            )
            return lax.psum(part, axes).astype(FULL)

        fc1_grad = weight_sum(rows_all, dhidden, "seq")
        fc2_grad = weight_sum(active, cot_all, "seq", 1)
        proj_grad = weight_sum(canon(joined, group, 1), gbranch, every)
        dmixed = jnp.concatenate([dkv, dquery], axis=1)[:, :qkv_cols]
        part = dot_tn(normed_all, dmixed).astype(LOW)
        part = lax.psum_scatter(part, "dp", scatter_dimension=0, tiled=True)
        part = part.astype(FULL) + hop(part, FAR).astype(FULL)
        part = part.astype(LOW)
        part = (part.astype(FULL) + hop(part, CORE).astype(FULL)).astype(LOW)
        whole = canon([part[None]] + [hop(part, bits)[None] for bits in way[1:]], group, 0)
        depth = whole.shape[1]
        pairs = whole[:, :, :kv_cols].reshape(groups, depth, heads, 2, head)
        qkv_grad = jnp.concatenate(
            [
                whole[:, :, kv_cols:].transpose(1, 0, 2).reshape(depth, width),
                pairs[:, :, :, 0].transpose(1, 0, 2, 3).reshape(depth, width),
                pairs[:, :, :, 1].transpose(1, 0, 2, 3).reshape(depth, width),
            ],
            axis=1,
        ).astype(FULL)
        vector = call(sums_kernel, [shape((vector_rows, qkv_cols), FULL)], [whole_shape], extra=6)(
            normed_all, dkv, dquery, mix, v.dgain_two, v.dshift_two, *tables
        )[0]
        vector = lax.psum(vector, ("dp", *every))
        *norms, table_h, table_w = vector_out((vector,), width, head)
        norms = [piece(row, d, width // dp_count, 0) for row in norms]
        dtables = [piece(t.T, d, head // dp_count, 1) for t in (table_h, table_w)]
    return (
        output,
        tokens_grad,
        norms[0],
        norms[1],
        qkv_grad,
        dtables[0],
        dtables[1],
        proj_grad,
        norms[2],
        norms[3],
        fc1_grad,
        fc2_grad,
    )


def solution(mesh):
    split = P("dp", ("seq", "tp"), None)
    params = (
        P("dp"),
        P("dp"),
        P("dp", None),
        P(None, "dp"),
        P(None, "dp"),
        P("dp", None),
        P("dp"),
        P("dp"),
        P("dp", "tp"),
        P("tp", "dp"),
    )
    return jax.shard_map(
        on_device,
        mesh=mesh,
        in_specs=(split, *params, split),
        out_specs=(split, split, *params),
        check_vma=False,
    )
```

```python
import math
import types

import jax
import jax.numpy as jnp
from jax import lax
from jax.experimental import pallas as pl
from jax.experimental.pallas import tpu as pltpu
from jax.sharding import PartitionSpec as P

EPS = 1e-06
LOW = jnp.bfloat16
FULL = jnp.float32
LANES = 128
CORE, ROW, NEAR, FAR = 1, 2, 4, 8


def hop(value, bits):
    count = lax.axis_size("seq") * lax.axis_size("tp")
    return lax.ppermute(value, ("seq", "tp"), [(i, i ^ bits) for i in range(count)])


def swap_dp(value):
    return lax.ppermute(value, "dp", [(0, 1), (1, 0)])


def pair_dp(value, axis):
    if lax.axis_size("dp") == 2:
        return value, swap_dp(value), lax.axis_index("dp")
    whole = lax.all_gather(value, "dp", axis=axis, tiled=True)
    low, high = jnp.split(whole, 2, axis=axis)
    return low, high, jnp.int32(0)


def after(value, *events):
    return lax.optimization_barrier((value, *events))[0]


def piece(value, index, size, axis):
    return lax.dynamic_slice_in_dim(value, index * size, size, axis)


def canon(blocks, index, axis):
    odd = (index & 1) == 1
    upper = (index & 2) == 2
    b = [
        jnp.where(odd, blocks[k ^ 1], blocks[k])
        for k in range(4)
    ]
    return jnp.concatenate([jnp.where(upper, b[k ^ 2], b[k]) for k in range(4)], axis=axis)


def dot_nn(a, b):
    return lax.dot_general(a, b, (((1,), (0,)), ((), ())), preferred_element_type=FULL)


def dot_nt(a, b):
    return lax.dot_general(a, b, (((1,), (1,)), ((), ())), preferred_element_type=FULL)


def dot_tn(a, b):
    return lax.dot_general(a, b, (((0,), (0,)), ((), ())), preferred_element_type=FULL)


def in_order():
    before = []

    def call(kernel, outs, scratch=(), smem=0, extra=2, wait=(), written=0, mark=False):
        def run(*args):
            held = sum(a.size * jnp.dtype(a.dtype).itemsize for a in (*args, *outs))
            held += sum(
                math.prod(a.shape) * jnp.dtype(a.dtype).itemsize
                for a in scratch
                if a.memory_space == pltpu.VMEM
            )
            used = len(args)
            events = (*before, *wait)

            def body(*refs):
                rest = refs[used + len(events) :]
                if written or mark:
                    rest[0][...] = jnp.zeros_like(rest[0])
                    rest = rest[1:]
                kernel(*refs[:used], *rest)

            vmem = pl.BlockSpec(memory_space=pltpu.VMEM)
            out_specs = [vmem] * len(outs)
            out_shape = list(outs)
            if written or mark:
                hbm = pl.BlockSpec(memory_space=pltpu.HBM)
                out_specs = [vmem] + [hbm if written else vmem] * len(outs)
                out_shape = [shape((8, LANES), FULL), *outs]
            results = pl.pallas_call(
                body,
                name=kernel.__qualname__.split(".")[0],
                out_shape=out_shape,
                in_specs=[pl.BlockSpec(memory_space=pltpu.SMEM)] * smem
                + [vmem] * (used - smem)
                + [pl.BlockSpec(memory_space=pl.ANY)] * len(events),
                out_specs=out_specs,
                scratch_shapes=scratch,
                compiler_params=pltpu.CompilerParams(vmem_limit_bytes=held + extra * 2**20),
                cost_estimate=pl.CostEstimate(flops=0, bytes_accessed=0, transcendentals=0),
            )(*args, *events)
            before[:] = [min(results, key=lambda r: r.size)]
            return results[1:] if written or mark else results

        return run

    return call


def shape(dims, kind):
    return jax.ShapeDtypeStruct(dims, kind)


def normal(values):
    center = values - jnp.mean(values, axis=-1, keepdims=True)
    scale = lax.rsqrt(jnp.mean(center * center, axis=-1, keepdims=True) + EPS)
    return center * scale, scale


def pick_kernel(ids, array, mine, other):
    mine[...] = array[ids[3]]
    other[...] = array[1 - ids[3]]


def stack_kernel(*refs):
    out, start = refs[-1], 0
    for ref in refs[:-1]:
        out[start : start + ref.shape[0], :] = ref[...]
        start += ref.shape[0]


def pack_kernel(share, heads):
    def kernel(ids, weight, out):
        width = weight.shape[1] // 3
        head = share // heads
        for g in range(width // share):

            @pl.when(ids[1] == g)
            def _():
                def move(at_col, first):
                    out[:, at_col : at_col + head] = weight[:, first : first + head]

                for h in range(heads):
                    first = g * share + h * head
                    move(2 * h * head, width + first)
                    move((2 * h + 1) * head, 2 * width + first)
                    move(2 * share + h * head, first)

    return kernel


def rows_kernel(ids, array, out):
    out[...] = array[at(ids[2], out.shape[0]), :]


def fill_rows(ids, out, mine, other, other_two):
    half = mine.shape[0]
    out[at(ids[0], half), :] = mine[...]
    if other.shape[0] == half:
        out[at(1 - ids[0], half), :] = other[...]
        return
    size = half // 2
    out[at((1 - ids[0]) * 2 + ids[2], size), :] = other[...]
    out[at((1 - ids[0]) * 2 + 1 - ids[2], size), :] = other_two[...]


def norm_kernel(ids, mine, other, small, small_other, out, params):
    width = small.shape[1]
    params[:, lanes(ids[0], width)] = small[...].astype(FULL)
    params[:, lanes(1 - ids[0], width)] = small_other[...].astype(FULL)
    half = mine.shape[0]
    for start, part in ((0, mine), (half, other)):
        hat, _ = normal(part[...])
        out[start : start + half, :] = (hat * params[0:1, :] + params[1:2, :]).astype(LOW)


def grid_row(ids, n):
    k, u, i = n // 4, (n // 2) % 2, n % 2
    chunk = ((ids[6] ^ (k >> 1)) ^ (2 * u)) * 4 + ((ids[5] ^ (k & 1)) * 2) + ids[2]
    return chunk * 2 + i


def table_kernel(ids, mine, other, table, spot_one, spot_two):
    part, reach = mine.shape[1:]
    rows = lax.broadcasted_iota(jnp.int32, (reach, LANES), 0)
    cols = lax.broadcasted_iota(jnp.int32, (reach, LANES), 1)
    turn = jnp.where(rows == reach - 1 - cols, 1.0, 0.0).astype(LOW)
    table[...] = jnp.zeros_like(table)
    for k in range(2):
        spot = slice(k * LANES, (k + 1) * LANES)
        table[at(ids[0], part), spot] = dot_nn(mine[k], turn).astype(LOW)
        table[at(1 - ids[0], part), spot] = dot_nn(other[k], turn).astype(LOW)
    side = (reach + 1) // 2
    lane = lane_of(side)
    col = lax.broadcasted_iota(jnp.int32, (side, LANES), 0)
    total = spot_one.shape[0] // side
    for n in range(total):
        row = grid_row(ids, n % (total // 2))
        if n >= total // 2:
            row = row ^ 2
        here = slice(n * side, (n + 1) * side)
        target = jnp.where(lane < 96, row + 64, col + 96)
        one = jnp.where(lane == target, 1.0, 0.0)
        spot_one[here, :] = one.astype(LOW)
        ones = jnp.where((lane >= 64) & (lane < 67), 1.0, 0.0)
        spot_two[here, :] = (pltpu.roll(one, 64, 1) + ones).astype(LOW)


def lane_of(rows):
    return lax.broadcasted_iota(jnp.int32, (rows, LANES), 1)


def pieces_at(lane, first, value, rest):
    high = value.astype(LOW).astype(FULL)
    left = value - high
    mid = left.astype(LOW).astype(FULL)
    tail = left - mid
    out = jnp.where(lane == first, high, rest)
    out = jnp.where(lane == first + 1, mid, out)
    return jnp.where(lane == first + 2, tail, out)


def key_tiles(h, kva, kvb, spot_one, keys):
    half = kva.shape[0]
    lane = lane_of(half)
    for start, part in ((0, kva), (half, kvb)):
        tile = part[:, h * LANES : (h + 1) * LANES].astype(FULL)
        spots = spot_one[start : start + half, :].astype(FULL)
        keys[start : start + half, :LANES] = jnp.where(lane < 64, tile, spots).astype(LOW)


def attend_kernel(
    ids, query, kva, kvb, spot_one, spot_two, table, out, a0, a1, a2, a3, left, keys, turned, along
):
    rows = query.shape[0]
    heads = left.shape[0]
    half = kva.shape[0]
    lane32 = lane_of(32)
    block = 512
    lane = lane_of(block)
    size = a0.shape[0]
    turned[LANES:, :] = spot_two[...].astype(FULL).T.astype(LOW)
    for h in range(heads):
        key_tiles(h, kva, kvb, spot_one, keys)
        turned[:LANES, :] = keys[...].astype(FULL).T.astype(LOW)
        tile = query[:, (h // 2) * LANES : (h // 2 + 1) * LANES].astype(FULL)
        if h % 2:
            tile = pltpu.roll(tile, 64, 1)
        along[...] = dot_nn(tile.astype(LOW), table[...])
        for g in range(rows // 32):
            here = slice(g * 32, (g + 1) * 32)
            term_h = pltpu.roll(along[here, :LANES], 33 + grid_row(ids, g), 1)
            term_w = pltpu.roll(along[here, LANES:], 65, 1, stride=1, stride_axis=0)
            one = jnp.where(
                lane32 < 64, tile[here, :] * 0.125, jnp.where(lane32 < 96, term_h, term_w)
            )
            high = one.astype(LOW)
            rest = pltpu.roll(one - high.astype(FULL), 64, 1)
            left[h, here, :LANES] = high
            left[h, here, LANES:] = rest.astype(LOW)
        cols = slice(h * LANES, (h + 1) * LANES)
        spot = slice((h // 2) * LANES, (h // 2 + 1) * LANES)
        for q in range(rows // block):
            here = slice(q * block, (q + 1) * block)
            scores = dot_nn(left[h, here, :], turned[...])
            top = jnp.max(scores, axis=1, keepdims=True)
            expo = jnp.exp(scores - top)
            total = jnp.sum(expo, axis=1, keepdims=True)
            low = expo.astype(LOW)
            result = dot_nn(low[:, :half], kva[:, cols]) + dot_nn(low[:, half:], kvb[:, cols])
            result = result / total
            if h % 2 == 0:
                result = pltpu.roll(result, 64, 1)
            if h % 2:
                result = jnp.where(lane < 64, out[here, spot], result)
            else:
                result = jnp.where(lane < 64, result, 0.0)
            out[here, spot] = result
            for k in range(block // size):
                low_out = (a0, a1, a2, a3)[q * block // size + k]
                part = result[k * size : (k + 1) * size, :].astype(LOW)
                if h % 2:
                    low_out[:, spot] = part
                elif h == heads - 1:
                    low_out[:, h * 64 :] = part[:, :64]
            rest = left[h, here, LANES:].astype(FULL)
            left[h, here, LANES:] = pieces_at(lane, 64, -(top + jnp.log(total)), rest).astype(LOW)


def back_kernel(h):
    def kernel(
        ids, left, kva, kvb, spot_one, spot_two, table, g0, g1, g2, g3, value,
        dquery, dkv_mine, dkv_other, dtable,
        keys, vals, gright, qright, along, grad, left_t, right_t,
    ):
        rows = left.shape[1]
        half = kva.shape[0]
        lane = lane_of(rows)
        lane32 = lane_of(32)
        row = lax.broadcasted_iota(jnp.int32, (rows, LANES), 0)
        key_tiles(h, kva, kvb, spot_one, keys)
        keys[:, LANES:] = spot_two[...]
        cols = slice(h * LANES, (h + 1) * LANES)
        spot = slice((h // 2) * LANES, (h // 2 + 1) * LANES)
        for k, part in enumerate((g0, g1, g2, g3)):
            size, width = part.shape
            last = min(width, spot.stop)
            grad[k * size : (k + 1) * size, : last - spot.start] = part[:, spot.start : last].astype(FULL)
        vals[:half, :LANES] = kva[:, cols]
        vals[half:, :LANES] = kvb[:, cols]
        vals[:, LANES:] = spot_two[...]
        gtile = grad[...]
        otile = value[:, spot]
        if h % 2 == 0:
            gtile = pltpu.roll(gtile, 64, 1)
            otile = pltpu.roll(otile, 64, 1)
        gtile = jnp.where(lane >= 64, gtile, 0.0)
        inner = jnp.sum(gtile * otile, axis=1, keepdims=True)
        gright[...] = gtile.astype(LOW)
        extra = pieces_at(lane, 64, -inner, jnp.zeros_like(gtile))
        right_t[:LANES, :] = gtile.T.astype(LOW)
        right_t[LANES:, :] = extra.T.astype(LOW)
        for part in (slice(0, LANES), slice(LANES, 2 * LANES)):
            left_t[part, :] = left[h, :, part].astype(FULL).T.astype(LOW)
        qright[...] = jnp.where(lane < 64, left[h, :, :LANES].astype(FULL), 0.0).astype(LOW)
        probs = jnp.exp(dot_nn(keys[...], left_t[...]))
        dscores = (probs * dot_nn(vals[...], right_t[...])).astype(LOW)
        dkv = dot_nn(probs.astype(LOW), gright[...]) + dot_nn(dscores, qright[...])
        dkv_mine[...] = dkv[:half, :]
        dkv_other[...] = dkv[half:, :].astype(LOW)
        dq = dot_tn(keys[:, :LANES], dscores).T
        for g in range(rows // 32):
            here = slice(g * 32, (g + 1) * 32)
            part_h = jnp.where((lane32 >= 64) & (lane32 < 96), dq[here, :], 0.0)
            along[here, :LANES] = pltpu.roll(part_h, 95 - grid_row(ids, g), 1).astype(LOW)
        part_w = pltpu.roll(jnp.where(lane >= 96, dq, 0.0), 63, 1)
        for bit in range(5):
            moved = pltpu.roll(part_w, LANES - 2**bit, 1)
            part_w = jnp.where((row >> bit) & 1 == 1, moved, part_w)
        along[:, LANES:] = part_w.astype(LOW)
        dq = jnp.where(lane < 64, dq * 0.125 + dot_nt(along[...], table[...]), 0.0)
        if h % 2:
            dq = pltpu.roll(dq, 64, 1)
        dquery[...] = dq.astype(LOW)
        dtable[...] = dot_tn(along[...], qright[...])

    return kernel


def at(index, size):
    return pl.ds(pl.multiple_of(index * size, 16), size)


def lanes(index, size):
    return pl.ds(pl.multiple_of(index * size, LANES), size)


def mix_kernel(ids, n0, n1, n2, n3, mine, other, kv, query, rows, mix):
    half, last = mine.shape
    kv_cols = kv.shape[1]
    mix[at(ids[0], half), :last] = mine[...]
    mix[at(1 - ids[0], half), :last] = other[...]
    mix[:, last:] = jnp.zeros((mix.shape[0], mix.shape[1] - last), LOW)
    size = n0.shape[0]
    for k, part in enumerate((n0, n1, n2, n3)):
        here = slice(k * size, (k + 1) * size)
        rows[here, :] = part[...]
    both = dot_nn(rows[...], mix[...]).astype(LOW)
    kv[...] = both[:, :kv_cols]
    query[...] = both[:, kv_cols:]


def mid_kernel(
    ids, j0, j1, j2, j3, w_mine, w_other, w_two, own, own_got, params, middle, low, weight, whole
):
    fill_rows(ids, whole, w_mine, w_other, w_two)
    tok = own.shape[0]
    middle[:tok, :] = own[...]
    middle[tok:, :] = own_got[...]
    total = middle[...]
    width = j0.shape[1]
    for k, part in enumerate((j0, j1, j2, j3)):
        block = whole[at(ids[1] ^ k, width), :]
        weight[k * width : (k + 1) * width, :] = block
        total = total + dot_nn(part[...], block)
    middle[...] = total
    hat, _ = normal(total)
    low[...] = (hat * params[2:3, :] + params[3:4, :]).astype(LOW)


def feed_kernel(
    ids, r0, r1, r2, r3, c0, c1, c2, c3, up_mine, up_other, down_mine, down_other,
    d0, d1, d2, d3, active, dhidden, rows, cots, down, up,
):
    half = up_mine.shape[0]
    up[at(ids[0], half), :] = up_mine[...]
    up[at(1 - ids[0], half), :] = up_other[...]
    down[:, lanes(ids[0], half)] = down_mine[...]
    down[:, lanes(1 - ids[0], half)] = down_other[...]
    size = r0.shape[0]
    blocks = ((r0, c0, d0), (r1, c1, d1), (r2, c2, d2), (r3, c3, d3))
    for k, (row, cot, _) in enumerate(blocks):
        here = slice(k * size, (k + 1) * size)
        rows[here, :] = row[...]
        cots[here, :] = cot[...]
    hidden = dot_nn(rows[...], up[...])
    phi = 0.5 + 0.5 * lax.erf(hidden * 0.7071067811865476)
    active[...] = (hidden * phi).astype(LOW)
    slope = phi + hidden * (jnp.exp(hidden * hidden * -0.5) * 0.3989422804014327)
    dhidden[...] = (dot_nt(cots[...], down[...]) * slope).astype(LOW)
    back = dot_nt(dhidden[...], up[...]).astype(LOW)
    for k, (_, _, out) in enumerate(blocks):
        out[...] = back[k * size : (k + 1) * size, :]


def fed_kernel(active, down, f0, f1, f2):
    size = f0.shape[0]
    total = dot_nn(active[...], down[...]).astype(LOW)
    f0[...] = total[:size, :]
    f1[...] = total[size : 2 * size, :]
    f2[...] = total[2 * size :, :]


def outer_kernel(which, axis):
    def kernel(ids, a, b, sent, kept):
        half = sent.shape[axis]
        for index, out in ((1 - ids[which], sent), (ids[which], kept)):
            if axis == 0:
                out[...] = dot_tn(a[:, lanes(index, half)], b[...]).astype(LOW)
            else:
                out[...] = dot_tn(a[...], b[:, lanes(index, half)]).astype(LOW)

    return kernel


def proj_grad_kernel(ids, j0, j1, j2, j3, grad, sent, kept, whole):
    width = j0.shape[1]
    for k, part in enumerate((j0, j1, j2, j3)):
        whole[at(ids[1] ^ k, width), :] = dot_tn(part[...], grad[...])
    size = sent.shape[0] // 2
    for k, owner in enumerate((ids[0], 1 - ids[0])):
        here = slice(k * size, (k + 1) * size)
        sent[here, :] = whole[at(owner * 2 + 1 - ids[2], size), :].astype(LOW)
        kept[here, :] = whole[at(owner * 2 + ids[2], size), :].astype(LOW)


def split_kernel(which):
    def kernel(ids, a, b, sent, kept):
        size = sent.shape[0] // 2
        for k in range(2):
            here = slice(k * size, (k + 1) * size)
            for bit, out in ((1 - ids[which], sent), (ids[which], kept)):
                rows = pl.ds(pl.multiple_of(k * 2 * size + bit * size, 16), size)
                out[here, :] = (a[rows, :].astype(FULL) + b[rows, :].astype(FULL)).astype(LOW)

    return kernel


def owner_kernel(a, b, sent, kept):
    size = sent.shape[0]
    kept[...] = (a[:size, :].astype(FULL) + b[:size, :].astype(FULL)).astype(kept.dtype)
    sent[...] = (a[size:, :].astype(FULL) + b[size:, :].astype(FULL)).astype(LOW)


def tail_add_kernel(a, b, out):
    size = a.shape[0]
    out[...] = (a[...].astype(FULL) + b[b.shape[0] - size :, :].astype(FULL)).astype(out.dtype)


def vector_block(out, n0, n1, n2, n3, t0, t1, t2):
    out[...] = jnp.zeros_like(out)
    tables = (t0[...] + t1[...] + t2[...]) * 8.0
    side = 16
    for k in range(8):
        start = k // 4 * LANES + k % 4 * side
        out[:side, k * 64 : (k + 1) * 64] = tables[start : start + side, :64]
    tile = 0
    for row in (n0, n1, n2, n3):
        for k in range(row.shape[1] // LANES):
            spot = slice(tile % 4 * LANES, (tile % 4 + 1) * LANES)
            out[side + tile // 4 : side + tile // 4 + 1, spot] = row[:, k * LANES : (k + 1) * LANES]
            tile += 1


def row_sums(product):
    total = product[:, :LANES]
    for k in range(1, product.shape[1] // LANES):
        total = total + product[:, k * LANES : (k + 1) * LANES]
    return jnp.sum(total.T, axis=0, keepdims=True)


def vector_out_kernel(reach, split):
    def kernel(ids, *refs):
        *parts, params, n0, n1, n2, n3, t0, t1, total, norms = refs
        first = parts[0].shape[0] - total.shape[0]
        total[...] = sum(part[first:, :].astype(FULL) for part in parts)
        side = 16
        for tile in range(norms.shape[0] * norms.shape[1] // LANES):
            each = norms.shape[1] // LANES
            spot = slice(tile % 4 * LANES, (tile % 4 + 1) * LANES)
            norms[tile // each : tile // each + 1, tile % each * LANES : (tile % each + 1) * LANES] = (
                total[side + tile // 4 : side + tile // 4 + 1, spot]
            )
        gain, shift = params[0:1, :], params[1:2, :]
        norms[0:1, :] = (norms[0:1, :] - shift * norms[1:2, :]) / gain
        for k, out in enumerate((n0, n1, n2, n3)):
            width = out.shape[0]
            start = ids[7] * width if split else 0
            for tile in range(width // LANES):
                spot = pl.ds(pl.multiple_of(start + tile * LANES, LANES), LANES)
                out[tile * LANES : (tile + 1) * LANES] = norms[k, spot]
        rows = lax.broadcasted_iota(jnp.int32, (side, reach), 0)
        cols = lax.broadcasted_iota(jnp.int32, (side, reach), 1)
        for k, out in enumerate((t0, t1)):
            both = jnp.zeros((64, reach), FULL)
            for part in range(4):
                turn = jnp.where(rows + part * side == reach - 1 - cols, 1.0, 0.0)
                start = (k * 4 + part) * 64
                both = both + lax.dot_general(
                    total[:side, start : start + 64],
                    turn,
                    (((0,), (0,)), ((), ())),
                    precision=lax.Precision.HIGHEST,
                    preferred_element_type=FULL,
                )
            if split:
                size = out.shape[0]
                out[...] = jnp.where(ids[7] == 0, both[:size, :], both[size:, :])
            else:
                out[...] = both

    return kernel


def dmix_kernel(dkv, dquery, mix, mine, near, sent):
    size = mine.shape[0]
    cols = dkv.shape[1]
    total = dot_nt(dkv[...], mix[:, :cols]) + dot_nt(dquery[...], mix[:, cols:])
    for k, (out, start) in enumerate(((mine, 0), (sent, 0), (near, 0), (sent, size))):
        out[start : start + size, :] = total[k * size : (k + 1) * size, :].astype(LOW)


def dkv_kernel(m0, m1, m2, o0, o1, o2, q0, q1, q2, dkv, dquery):
    for h, (mine, got) in enumerate(((m0, o0), (m1, o1), (m2, o2))):
        cols = slice(h * LANES, (h + 1) * LANES)
        dkv[:, cols] = (mine[...] + got[...].astype(FULL)).astype(LOW)
    dquery[:, :LANES] = (q0[...].astype(FULL) + q1[...].astype(FULL)).astype(LOW)
    dquery[:, LANES:] = q2[...]


def qkv_grad_kernel(
    ids, rows, m0, m1, m2, o0, o1, o2, q0, q1, q2, mix, v2, v3, t0, t1, t2,
    dkv, dquery, sent, kept, whole, vector,
):
    dkv_kernel(m0, m1, m2, o0, o1, o2, q0, q1, q2, dkv, dquery)
    cols = dkv.shape[1]
    whole[:, :cols] = dot_tn(rows[...], dkv[...])
    whole[:, cols:] = dot_tn(rows[...], dquery[...])
    width = kept.shape[1]
    size = (kept.shape[0] - vector.shape[0]) // 2
    sums_block(whole, dkv, dquery, mix, v2, v3, t0, t1, t2, vector)
    for out, core in ((sent, 1 - ids[2]), (kept, ids[2])):
        for k, owner in enumerate((ids[0], 1 - ids[0])):
            here = slice(k * size, (k + 1) * size)
            out[here, :] = whole[at(owner * 2 + core, size), :width].astype(LOW)
        out[2 * size :, :] = vector[...].astype(LOW)


def sums_block(whole, dkv, dquery, mix, v2, v3, t0, t1, t2, vector):
    weights = mix[...].astype(FULL)
    sums = jnp.concatenate(
        [jnp.sum(part[...].astype(FULL), axis=0, keepdims=True) for part in (dkv, dquery)], axis=1
    )
    both = row_sums(whole[...] * weights)
    shift = row_sums(weights * sums)
    vector_block(vector, both, shift, v2, v3, t0, t1, t2)


def sums_kernel(rows, dkv, dquery, mix, v2, v3, t0, t1, t2, vector, whole):
    cols = dkv.shape[1]
    whole[:, :cols] = dot_tn(rows[...], dkv[...])
    whole[:, cols:] = dot_tn(rows[...], dquery[...])
    sums_block(whole, dkv, dquery, mix, v2, v3, t0, t1, t2, vector)


def qkv_owner_kernel(a, b, sent, kept):
    size = a.shape[0] - sent.shape[0]
    kept[:size, :] = a[:size, :].astype(FULL) + b[:size, :].astype(FULL)
    total = a[size:, :].astype(FULL) + b[size:, :].astype(FULL)
    kept[size:, :] = total[size:, :]
    sent[...] = total.astype(LOW)


def add_kernel(*refs):
    total = refs[0][...].astype(FULL)
    for ref in refs[1:-1]:
        total = total + ref[...].astype(FULL)
    refs[-1][...] = total.astype(refs[-1].dtype)


def halve_kernel(which):
    def kernel(ids, a, b, sent, kept):
        size = sent.shape[0]
        bit = ids[which]
        for index, out in ((1 - bit, sent), (bit, kept)):
            here = at(index, size)
            out[...] = (a[here, :].astype(FULL) + b[here, :].astype(FULL)).astype(out.dtype)

    return kernel


def join_kernel(which):
    def kernel(ids, mine, other, out):
        size = mine.shape[0]
        out[at(ids[which], size), :] = mine[...].astype(out.dtype)
        out[at(1 - ids[which], size), :] = other[...].astype(out.dtype)

    return kernel


def qkv_out(heads, ids, mine, others, out, whole, sem, copies):
    size = out.shape[0] // 2
    lane = lane_of(size)
    first = lane < 64
    groups = 4
    share = heads * 64
    width = groups * share

    def fill(here, refs):
        def tile(g, column):
            stop = min(column + LANES, refs[g].shape[1])
            one = refs[g][:size, column:stop].astype(FULL)
            if stop - column < LANES:
                one = jnp.concatenate([one, jnp.zeros_like(one)], axis=1)
            return one

        for pair in range(groups * heads // 2):
            ends = []
            for n in (2 * pair, 2 * pair + 1):
                g, h = n // heads, n % heads
                q = tile(g, 2 * share + (h // 2) * LANES)
                if h % 2:
                    q = pltpu.roll(q, 64, 1)
                ends.append((q, tile(g, h * LANES)))
            (qa, kva), (qb, kvb) = ends
            at_col = pair * LANES
            for begin, a, b in (
                (0, qa, pltpu.roll(qb, 64, 1)),
                (width, kva, pltpu.roll(kvb, 64, 1)),
                (2 * width, pltpu.roll(kva, 64, 1), kvb),
            ):
                cols = slice(begin + at_col, begin + at_col + LANES)
                whole[here, cols] = jnp.where(first, a, b)

    for place, refs in ((ids[2], mine), (1 - ids[2], others)):
        here = pl.ds(pl.multiple_of(place * size, 16), size)
        for g in range(groups):

            @pl.when(ids[1] == g)
            def _():
                fill(here, [refs[k ^ g] for k in range(groups)])

        start(whole.at[here], out.at[here], sem, copies)


def halve_lanes_kernel(which):
    def kernel(ids, a, b, sent, kept):
        size = sent.shape[1]
        for bit, out in ((1 - ids[which], sent), (ids[which], kept)):
            here = lanes(bit, size)
            out[...] = (a[:, here].astype(FULL) + b[:, here].astype(FULL)).astype(out.dtype)

    return kernel


def start(source, target, sem, copies):
    copies.append(pltpu.make_async_copy(source, target, sem.at[len(copies)]))
    copies[-1].start()


def place_out(ids, mine, other, out, sem, copies):
    start(mine, out.at[ids[3]], sem, copies)
    start(other, out.at[1 - ids[3]], sem, copies)


def join_out(ids, which, mine, other, out, whole, sem, copies):
    size = mine.shape[0]
    for place, ref in ((ids[which], mine), (1 - ids[which], other)):
        here = at(place, size)
        whole[here, :] = ref[...].astype(FULL)
        start(whole.at[here], out.at[here], sem, copies)


def place_kernel(ids, token, change, got, away, output, tokens_grad, low, sem):
    copies = []
    tok = token.shape[0]
    low[:tok, :] = got[:tok, :].astype(FULL)
    place_out(ids, token, low.at[:tok], tokens_grad, sem, copies)
    low[tok:, :] = got[tok:, :].astype(FULL) + away[...]
    place_out(ids, change, low.at[tok:], output, sem, copies)
    for copy in copies:
        copy.wait()


def early_kernel(ids, first, first_got, out, whole, sem):
    copies = []
    join_out(ids, 4, first, first_got, out, whole, sem, copies)
    for copy in copies:
        copy.wait()


def last_kernel(heads):
    def kernel(
        ids, q0, q1, q2, q3, o0, o1, o2, o3, token, change, got, away,
        proj, proj_got, second, second_got,
        output, tokens_grad, qkv_grad, proj_grad, fc2_grad,
        low, qkv, wide, two, sem,
    ):
        copies = []
        tok = token.shape[0]
        low[:tok, :] = got[:tok, :].astype(FULL)
        place_out(ids, token, low.at[:tok], tokens_grad, sem, copies)
        low[tok:, :] = got[tok:, :].astype(FULL) + away[...]
        place_out(ids, change, low.at[tok:], output, sem, copies)
        join_out(ids, 2, proj, proj_got, proj_grad, wide, sem, copies)
        join_out(ids, 4, second, second_got, fc2_grad, two, sem, copies)
        qkv_out(heads, ids, (q0, q1, q2, q3), (o0, o1, o2, o3), qkv_grad, qkv, sem, copies)
        for copy in copies:
            copy.wait()

    return kernel


def norm_back(grad, values, gain):
    hat, scale = normal(values)
    scaled = grad * gain
    back = scale * (
        scaled
        - jnp.mean(scaled, axis=-1, keepdims=True)
        - hat * jnp.mean(scaled * hat, axis=-1, keepdims=True)
    )
    return back, jnp.sum(grad * hat, axis=0, keepdims=True), jnp.sum(grad, axis=0, keepdims=True)


def mid_back_kernel(
    a0, a1, a2, middle, params, cot, weight, gmiddle, gbranch, b0, b1, b2, b3, dgain, dshift
):
    size = a0.shape[0]
    grad = a0[...].astype(FULL) + a1[...].astype(FULL) + a2[...].astype(FULL)
    back, dgain[...], dshift[...] = norm_back(grad, middle[...], params[2:3, :])
    total = cot[:size, :].astype(FULL) + back
    gmiddle[...] = total
    low = total.astype(LOW)
    gbranch[...] = low
    width = b0.shape[1]
    for k, out in enumerate((b0, b1, b2, b3)):
        out[...] = dot_nt(low, weight[k * width : (k + 1) * width, :]).astype(LOW)


def first_back_kernel(
    a0, a1, a2, own, own_got, params, gmiddle, middle, f0, f1, f2, mine, change, sent, rows
):
    tok = own.shape[0]
    fed = f0[...].astype(FULL) + f1[: 2 * tok, :].astype(FULL) + f2[...].astype(FULL)
    total = middle[...] + fed
    change[...] = total[:tok, :]
    sent[tok:, :] = (total[tok:, :] - own_got[...]).astype(LOW)
    rows[:tok, :] = own[...]
    rows[tok:, :] = own_got[...]
    grad = a0[...].astype(FULL) + a1[: 2 * tok, :].astype(FULL) + a2[...].astype(FULL)
    back, _, _ = norm_back(grad, rows[...], params[0:1, :])
    total = gmiddle[...] + back
    mine[...] = total[:tok, :]
    sent[:tok, :] = total[tok:, :].astype(LOW)


def on_device(
    tokens,
    ln1_gain,
    ln1_bias,
    qkv_weight,
    rel_h,
    rel_w,
    proj_weight,
    ln2_gain,
    ln2_bias,
    fc1_weight,
    fc2_weight,
    cotangent,
):
    images, tok, width = tokens.shape
    hid = fc1_weight.shape[1]
    dp_count = lax.axis_size("dp")
    head = rel_h.shape[1] * dp_count
    reach = rel_h.shape[0]
    s, t = lax.axis_index("seq"), lax.axis_index("tp")
    d = lax.axis_index("dp")
    y, c = t // 2, t % 2
    image = s // 2
    group = (s % 2) * 2 + y
    groups = 4
    share = width // groups
    heads = share // head
    rows_n = 2 * tok
    half = width // 2
    me = d if dp_count == 2 else jnp.int32(0)
    ids = jnp.stack([me, group, c, image, s % 2, y, s, d]).astype(jnp.int32)
    n = 4 * rows_n
    kv_cols = 2 * share
    pad_share = 2 * LANES
    key_n = 2 * n
    qkv_cols = 3 * share
    low_tok, full_tok = shape((tok, width), LOW), shape((tok, width), FULL)
    low_rows, full_rows = shape((rows_n, width), LOW), shape((rows_n, width), FULL)
    two_rows = shape((2 * rows_n, width), LOW)
    heads_rows = shape((rows_n, share), LOW)
    way = (0, ROW, NEAR, ROW | NEAR)

    def add(kind, *args, wait=()):
        return call(add_kernel, [shape(args[0].shape, kind)], wait=wait)(*args)[0]

    call = in_order()
    quarter, eighth = half // 2, half // 4
    norm_sums = [shape((1, width), FULL)] * 2

    def total_of(kind, *args):
        return call(add_kernel, [shape(args[0].shape, kind)])(*args)[0]

    def halve(which, a, b, kind=FULL):
        dims = (a.shape[0] // 2, a.shape[1])
        return call(halve_kernel(which), [shape(dims, LOW), shape(dims, kind)], smem=1)(ids, a, b)

    def split(which, a, b):
        dims = (a.shape[0] // 2, a.shape[1])
        return call(split_kernel(which), [shape(dims, LOW)] * 2, smem=1)(ids, a, b)

    def join(which, mine, other, kind):
        dims = (2 * mine.shape[0], mine.shape[1])
        return call(join_kernel(which), [shape(dims, kind)], smem=1)(ids, mine, other)[0]

    own, away = call(pick_kernel, [full_tok] * 2, smem=1)(ids, tokens)
    own_got = hop(away, FAR)
    small = jnp.concatenate([ln1_gain, ln1_bias, ln2_gain, ln2_bias]).reshape(4, -1)
    small, small_other, _ = pair_dp(after(small, away), 1)
    tables = jnp.stack([rel_h.T, rel_w.T])
    tables, tables_other, _ = pair_dp(after(tables, away), 1)
    cot_mine, cot_away = call(pick_kernel, [low_tok] * 2, smem=1)(ids, cotangent)
    cot_got = hop(cot_away, FAR)
    depth = qkv_weight.shape[0]
    mix_mine = call(
        pack_kernel(share, heads),
        [shape((depth, qkv_cols), LOW)],
        smem=1,
        wait=(small_other, tables_other),
    )(ids, qkv_weight)[0]
    mix_mine, mix_other, _ = pair_dp(after(mix_mine, own_got), 0)

    normed, params = call(norm_kernel, [low_rows, shape((4, width), FULL)], smem=1)(
        ids, own, own_got, small, small_other
    )
    normed_parts = [normed] + [hop(normed, b) for b in way[1:]]
    cot = call(stack_kernel, [low_rows])(cot_mine, cot_got)[0]
    if dp_count == 2:
        proj_part = call(rows_kernel, [shape((half // 2, width), LOW)], smem=1)(ids, proj_weight)[0]
    table, spot_one, spot_two = call(
        table_kernel,
        [shape((LANES, 2 * LANES), LOW)] + [shape((key_n, LANES), LOW)] * 2,
        smem=1,
        wait=(mix_other,),
    )(ids, tables, tables_other)

    kv, query, normed_all, mix = call(
        mix_kernel,
        [
            shape((n, kv_cols), LOW),
            shape((n, pad_share), LOW),
            shape((n, width), LOW),
            shape((width, kv_cols + pad_share), LOW),
        ],
        smem=1,
        extra=3,
    )(ids, *normed_parts, mix_mine, mix_other)
    kv_other = hop(kv, CORE)
    cot_row = hop(after(cot, kv), ROW)
    if dp_count == 2:
        proj_mine, proj_other = proj_weight, swap_dp(after(proj_part, normed))
    else:
        proj_mine, proj_other, _ = pair_dp(proj_weight, 0)
    proj_two = hop(after(proj_other, kv), CORE)
    up_mine, up_other, _ = pair_dp(after(fc1_weight, normed), 0)

    down_mine, down_other, _ = pair_dp(after(fc2_weight, kv), 1)

    attended, *attended_low, left = call(
        attend_kernel,
        [shape((n, pad_share), FULL)]
        + [heads_rows] * 4
        + [shape((heads, n, 2 * LANES), LOW)],
        [
            pltpu.VMEM((key_n, LANES), LOW),
            pltpu.VMEM((2 * LANES, key_n), LOW),
            pltpu.VMEM((n, 2 * LANES), FULL),
        ],
        smem=1,
        extra=16,
    )(ids, query, kv, kv_other, spot_one, spot_two, table)
    attended_low = lax.optimization_barrier((*attended_low, cot_row, proj_two))[:4]
    joined = [attended_low[0]] + [hop(attended_low[k], way[k]) for k in (1, 2, 3)]
    middle, normed_two, proj = call(
        mid_kernel,
        [full_rows, low_rows, shape((width, width), LOW)],
        [pltpu.VMEM((width, width), LOW)],
        smem=1,
        wait=(up_other,),
    )(ids, *joined, proj_mine, proj_other, proj_two, own, own_got, params)

    two_row = hop(normed_two, ROW)
    two_core = hop(normed_two, CORE)
    two_diag = hop(two_row, CORE)
    cot_core = hop(after(cot, two_row), CORE)
    cot_diag = hop(after(cot_row, two_row), CORE)
    d0, d1, d2, d3, active, dhidden, rows_all, cot_all, down = call(
        feed_kernel,
        [low_rows] * 4
        + [shape((n, hid), LOW)] * 2
        + [shape((n, width), LOW)] * 2
        + [shape((hid, width), LOW)],
        [pltpu.VMEM((width, hid), LOW)],
        smem=1,
        extra=12,
    )(
        ids, normed_two, two_row, two_core, two_diag, cot, cot_row, cot_core, cot_diag,
        up_mine, up_other, down_mine, down_other,
    )
    dnorm_next = hop(d3, CORE)
    dnorm_mine = hop(d2, CORE)

    mixed_shapes = [shape((n, kv_cols), LOW), shape((n, pad_share), LOW)]
    vector_rows = 32
    whole_shape = pltpu.VMEM((width, kv_cols + pad_share), FULL)
    qkv_rows = (quarter + vector_rows, qkv_cols)
    proj_low = shape((eighth, width), LOW)
    v, fc1, fc2 = (types.SimpleNamespace() for _ in range(3))

    def send(value, bits, *events):
        return hop(after(value, *events) if events else value, bits)

    def dnorm_add():
        v.dnorm_row = send(total_of(LOW, d1, dnorm_next), ROW)

    def fc1_outer():
        sent, fc1.kept = call(outer_kernel(0, 0), [shape((half, hid), LOW)] * 2, smem=1, extra=4)(
            ids, rows_all, dhidden
        )
        if dp_count == 2:
            fc1.got = swap_dp(sent)

    def far_sum(part):
        def step():
            sent, part.kept = halve(3, part.kept, part.got)
            part.got = send(sent, FAR)

        return step

    def far_all(part):
        def step():
            part.kept = total_of(LOW, part.kept, part.got)
            part.got = send(part.kept, FAR)

        return step

    def near_all(part):
        def step():
            part.kept = join(3, part.kept, part.got, LOW)
            part.got = send(part.kept, NEAR)

        return step

    def fc2_outer():
        sent, fc2.kept = call(
            outer_kernel(4, 0), [shape((hid // 2, width), LOW)] * 2, smem=1, extra=4
        )(ids, active, cot_all)
        fc2.got = send(sent, NEAR)

    def mid_back():
        v.gmiddle, v.gbranch, *parts, v.dgain_two, v.dshift_two = call(
            mid_back_kernel, [full_rows, low_rows] + [heads_rows] * 4 + norm_sums
        )(d0, dnorm_mine, v.dnorm_row, middle, params, cot, proj)
        v.grads = [parts[0]] + [
            send(b, bits) for b, bits in zip(parts[1:], way[1:])
        ]

    def proj_outer():
        sent, v.proj = call(
            proj_grad_kernel,
            [shape((half, width), LOW)] * 2,
            [pltpu.VMEM((width, width), FULL)],
            smem=1,
        )(ids, *joined, v.gbranch)
        v.proj_got = send(after(sent, *v.grads), CORE)

    def fed():
        v.f0, v.f1, f2 = call(fed_kernel, [low_rows, low_rows, two_rows], extra=4)(
            active, down
        )
        v.fed_got = send(after(f2, *v.grads), CORE)

    def back(h):
        dquery, mine, other, dtable = call(
            back_kernel(h),
            [
                shape((n, LANES), LOW),
                shape((n, LANES), FULL),
                shape((n, LANES), LOW),
                shape((2 * LANES, LANES), FULL),
            ],
            [
                pltpu.VMEM((key_n, 2 * LANES), LOW),
                pltpu.VMEM((key_n, 2 * LANES), LOW),
                pltpu.VMEM((n, LANES), LOW),
                pltpu.VMEM((n, LANES), LOW),
                pltpu.VMEM((n, 2 * LANES), LOW),
                pltpu.VMEM((n, LANES), FULL),
                pltpu.VMEM((2 * LANES, n), LOW),
                pltpu.VMEM((2 * LANES, n), LOW),
            ],
            smem=1,
            extra=20,
            wait=(v.back[-1][1],) if v.back else (),
        )(ids, left, kv, kv_other, spot_one, spot_two, table, *v.grads, attended)
        v.back.append((mine, send(other, CORE), dquery, dtable))

    v.back = []

    def back0():
        back(0)

    def back1():
        back(1)

    def back2():
        back(2)

    def fed_add():
        sent = call(tail_add_kernel, [low_rows])(v.f1, v.fed_got)[0]
        v.fed_row = send(sent, ROW)

    def early():
        dims = (half, hid)
        (fc1.grad,) = call(
            early_kernel,
            [shape(dims, FULL)],
            [pltpu.VMEM(dims, FULL), pltpu.SemaphoreType.DMA((2,))],
            smem=1,
            written=1,
        )(ids, fc1.kept, fc1.got)

    def last():
        dims = [tokens.shape] * 2 + [(half, 3 * width), (half, width), (hid, half)]
        (
            v.output, v.tokens_grad, v.qkv_grad, v.proj_grad, fc2.grad,
        ) = call(
            last_kernel(heads),
            [shape(d, FULL) for d in dims],
            [pltpu.VMEM((rows_n, width), FULL)]
            + [pltpu.VMEM(d, FULL) for d in dims[2:]]
            + [pltpu.SemaphoreType.DMA((10,))],
            smem=1,
            extra=8,
            written=5,
        )(
            ids, *v.qkv_parts, *v.qkv_others, v.token, v.change, v.token_got, away,
            v.proj, v.proj_got, fc2.kept, fc2.got,
        )

    def qkv_outer():
        mine, got, queries, tables = zip(*v.back)
        v.dkv, v.dquery, sent, v.qkv = call(
            qkv_grad_kernel,
            mixed_shapes + [shape((half + vector_rows, qkv_cols), LOW)] * 2,
            [whole_shape, pltpu.VMEM((vector_rows, qkv_cols), FULL)],
            smem=1,
            extra=6,
        )(
            ids, normed_all, *mine, *got, *queries, mix, v.dgain_two, v.dshift_two, *tables
        )
        v.qkv_got = send(sent, CORE)

    def qkv_owner():
        sent, v.qkv = call(qkv_owner_kernel, [shape(qkv_rows, LOW), shape(qkv_rows, FULL)])(
            v.qkv, v.qkv_got
        )
        v.qkv_got = swap_dp(sent)

    def qkv_images():
        v.qkv = total_of(LOW, v.qkv, v.qkv_got)
        v.qkv_got = send(v.qkv, FAR)

    def qkv_total():
        part = total_of(LOW, v.qkv, v.qkv_got)
        near = send(part, NEAR)
        v.qkv_parts = [part, send(part, ROW), near, send(near, ROW)]

    def vector_last():
        *norms, table_h, table_w = vector_out(v.qkv_parts, half, head // 2)
        v.norms = norms
        v.tables = (table_h.T, table_w.T)
        v.qkv_others = [send(part, CORE) for part in v.qkv_parts]

    def mixed_back():
        v.e_mine, v.e_near, e_row = call(
            dmix_kernel, [low_rows, low_rows, two_rows], extra=6
        )(
            v.dkv, v.dquery, mix
        )
        v.e_got = send(e_row, ROW)

    def normed_near():
        sent = call(tail_add_kernel, [low_rows])(v.e_near, v.e_got)[0]
        v.e_last = send(sent, NEAR)

    def first_back():
        v.token, v.change, sent = call(
            first_back_kernel, [full_tok, full_tok, low_rows], [pltpu.VMEM((rows_n, width), FULL)]
        )(
            v.e_mine, v.e_got, v.e_last, own, own_got, params, v.gmiddle,
            middle, v.f0, v.fed_got, v.fed_row,
        )
        v.token_got = send(sent, FAR)

    def fc1_near_sum():
        sent, fc1.kept = halve(4, fc1.kept, fc1.got)
        fc1.got = send(sent, NEAR)

    def fc2_near_sum():
        dims = (hid // 2, half)
        sent, fc2.kept = call(
            halve_lanes_kernel(0), [shape(dims, LOW), shape(dims, FULL)], smem=1
        )(ids, fc2.kept, fc2.got)
        fc2.got = swap_dp(sent)

    def proj_split():
        sent, v.proj = split(5, v.proj, v.proj_got)
        v.proj_got = send(sent, ROW)

    def proj_owner():
        sent, v.proj = call(owner_kernel, [proj_low] * 2)(v.proj, v.proj_got)
        v.proj_got = swap_dp(sent)

    def proj_sum(bits):
        def step():
            v.proj = total_of(LOW, v.proj, v.proj_got)
            v.proj_got = send(v.proj, bits)

        return step

    def proj_join():
        v.proj = join(5, v.proj, v.proj_got, LOW)
        v.proj_got = send(v.proj, CORE)

    def vector_out(parts, size, features):
        return call(
            vector_out_kernel(reach, dp_count == 2),
            [shape((size,), FULL)] * 4 + [shape((features, reach), FULL)] * 2,
            [pltpu.VMEM((vector_rows, qkv_cols), FULL), pltpu.VMEM((4, width), FULL)],
            smem=1,
            mark=True,
        )(ids, *parts, params)

    if dp_count == 2:
        for step in (
            fc2_outer,
            dnorm_add,
            fc1_outer,
            mid_back,
            fc2_near_sum,
            proj_outer,
            back0,
            fc1_near_sum,
            back1,
            proj_split,
            back2,
            far_sum(fc1),
            qkv_outer,
            fed,
            qkv_owner,
            mixed_back,
            proj_owner,
            qkv_images,
            far_all(fc1),
            far_sum(fc2),
            fed_add,
            proj_sum(NEAR),
            qkv_total,
            far_all(fc2),
            normed_near,
            proj_sum(FAR),
            near_all(fc2),
            near_all(fc1),
            first_back,
            proj_sum(ROW),
            vector_last,
            early,
            proj_join,
            last,
        ):
            step()
        output, tokens_grad, qkv_grad = v.output, v.tokens_grad, v.qkv_grad
        proj_grad, fc1_grad, fc2_grad = v.proj_grad, fc1.grad, fc2.grad
        norms, dtables = v.norms, v.tables
    else:
        every = ("seq", "tp")
        for step in (dnorm_add, mid_back, fed, back0, back1, back2, fed_add):
            step()
        mine, other, queries, tables = zip(*v.back)
        v.dkv, v.dquery = call(dkv_kernel, mixed_shapes)(*mine, *other, *queries)
        for step in (mixed_back, normed_near, first_back):
            step()
        output, tokens_grad = call(
            place_kernel,
            [shape(tokens.shape, FULL)] * 2,
            [pltpu.VMEM((rows_n, width), FULL), pltpu.SemaphoreType.DMA((4,))],
            smem=1,
            written=2,
        )(ids, v.token, v.change, v.token_got, away)
        dkv, dquery, gbranch = v.dkv, v.dquery, v.gbranch

        def weight_sum(a, b, axes, axis=0):
            part = lax.psum_scatter(
                dot_tn(a, b).astype(LOW), "dp", scatter_dimension=axis, tiled=True
            )
            return lax.psum(part, axes).astype(FULL)

        fc1_grad = weight_sum(rows_all, dhidden, "seq")
        fc2_grad = weight_sum(active, cot_all, "seq", 1)
        proj_grad = weight_sum(canon(joined, group, 1), gbranch, every)
        dmixed = jnp.concatenate([dkv, dquery], axis=1)[:, :qkv_cols]
        part = dot_tn(normed_all, dmixed).astype(LOW)
        part = lax.psum_scatter(part, "dp", scatter_dimension=0, tiled=True)
        part = part.astype(FULL) + hop(part, FAR).astype(FULL)
        part = part.astype(LOW)
        part = (part.astype(FULL) + hop(part, CORE).astype(FULL)).astype(LOW)
        whole = canon([part[None]] + [hop(part, bits)[None] for bits in way[1:]], group, 0)
        depth = whole.shape[1]
        pairs = whole[:, :, :kv_cols].reshape(groups, depth, heads, 2, head)
        qkv_grad = jnp.concatenate(
            [
                whole[:, :, kv_cols:].transpose(1, 0, 2).reshape(depth, width),
                pairs[:, :, :, 0].transpose(1, 0, 2, 3).reshape(depth, width),
                pairs[:, :, :, 1].transpose(1, 0, 2, 3).reshape(depth, width),
            ],
            axis=1,
        ).astype(FULL)
        vector = call(sums_kernel, [shape((vector_rows, qkv_cols), FULL)], [whole_shape], extra=6)(
            normed_all, dkv, dquery, mix, v.dgain_two, v.dshift_two, *tables
        )[0]
        vector = lax.psum(vector, ("dp", *every))
        *norms, table_h, table_w = vector_out((vector,), width, head)
        norms = [piece(row, d, width // dp_count, 0) for row in norms]
        dtables = [piece(t.T, d, head // dp_count, 1) for t in (table_h, table_w)]
    return (
        output,
        tokens_grad,
        norms[0],
        norms[1],
        qkv_grad,
        dtables[0],
        dtables[1],
        proj_grad,
        norms[2],
        norms[3],
        fc1_grad,
        fc2_grad,
    )


def solution(mesh):
    split = P("dp", ("seq", "tp"), None)
    params = (
        P("dp"),
        P("dp"),
        P("dp", None),
        P(None, "dp"),
        P(None, "dp"),
        P("dp", None),
        P("dp"),
        P("dp"),
        P("dp", "tp"),
        P("tp", "dp"),
    )
    return jax.shard_map(
        on_device,
        mesh=mesh,
        in_specs=(split, *params, split),
        out_specs=(split, split, *params),
        check_vma=False,
    )
```
